128 devices in a mesh: tm: 16 (over y, z), fsdp: 8 (over x, core).
Axes of the slice: x: 4, y: 4, z: 4, core: 2. Of those that a mesh axis runs over, the one named last changes fastest.
Arguments:
- clip: bfloat16 [8, 32, 16, 64, 256], P('fsdp', 'tm'), may hold values from -12 to 12
- cotangent: bfloat16 [8, 32, 16, 64, 256], P('fsdp', 'tm'), may hold values from -5 to 5
- weights: bfloat16 [6912, 256], P('fsdp'), may hold values from -0.1 to 0.1
Outputs:
- grad_input: bfloat16 [8, 32, 16, 64, 256], P('fsdp', 'tm')
- grad_weight: float32 [6912, 256], P('fsdp')
The draws below stay inside these ranges and needn't reach their ends.
All inputs are finite; a program needn't handle non-finite values.
Results may differ from the reference program's by a relative error of at most 0.015.
Values may be sent and summed in bfloat16 or wider, within the bound.
No kernel may reach another device: no remote copies, remote signals or barrier semaphores. Data moves between devices by JAX's collectives and lax.ppermute only.
A program may use at most 128 MiB of HBM per device.

```python
import math
import jax
import jax.numpy as jnp
from jax import lax

C = 256
GROUPS = 32
TILE_H = 16
TILE_W = 64
FRAMES = 32
BATCH = 8


def draw_clip(key, part):
    first_key, second_key, third_key = jax.random.split(jax.random.fold_in(key, 11), 3)
    shape = (BATCH, FRAMES, TILE_H, TILE_W, C)
    fraction = jnp.arange(FRAMES, dtype=jnp.float32) / max(FRAMES - 1, 1)
    offsets = jax.random.uniform(first_key, (BATCH, 1, 1, 1, C), jnp.float32, -0.5, 0.5)
    frame_scale = jax.random.uniform(third_key, (BATCH, FRAMES, 1, 1, 1), jnp.float32, 0.4, 2.0)
    noise = jnp.clip(jax.random.normal(second_key, shape, jnp.float32), -3.5, 3.5)
    ramp = 0.5 + fraction
    return (ramp[None, :, None, None, None] * frame_scale * (offsets + noise)).astype(jnp.bfloat16)


def draw_cotangent(key, part):
    first_key, second_key = jax.random.split(jax.random.fold_in(key, 23))
    shape = (BATCH, FRAMES, TILE_H, TILE_W, C)
    raw_offsets = jax.random.uniform(first_key, (BATCH, 1, 1, 1, C), jnp.float32, -0.4, 0.4)
    offsets = raw_offsets - jnp.mean(raw_offsets, axis=0, keepdims=True)
    noise = jnp.clip(jax.random.normal(second_key, shape, jnp.float32), -4.0, 4.0)
    return (noise + offsets).astype(jnp.bfloat16)


def draw_weights(key, part):
    first_key, second_key = jax.random.split(jax.random.fold_in(key, 37))
    fan_scale = (27.0 * C) ** (-0.5)
    shared = jax.random.uniform(first_key, (C, C), jnp.float32, -0.03, 0.03)
    noise = jnp.clip(jax.random.normal(second_key, (27 * C, C), jnp.float32), -4.0, 4.0)
    return (noise * fan_scale + jnp.tile(shared, (27, 1))).astype(jnp.bfloat16)


def setup_inputs(seed: int = 0) -> dict:
    key_list = jax.random.split(jax.random.key(seed), 4)
    clip = draw_clip(jax.random.fold_in(key_list[3], 71), 0)
    cotangent = draw_cotangent(jax.random.fold_in(key_list[3], 71), 0)
    weights = draw_weights(jax.random.fold_in(key_list[3], 71), 0)
    return {"clip": clip, "cotangent": cotangent, "weights": weights}


epsilon = 1e-06

def group_sums(values):
    shaped = values.reshape(values.shape[:4] + (GROUPS, values.shape[4] // GROUPS))
    return shaped.sum(axis=(1, 2, 3, 5))

def expand(stat, channels):
    return jnp.repeat(stat, channels // GROUPS, axis=1)[:, None, None, None, :]

def reference(clip, cotangent, weights):
    batch, frames, height, tile_width, channels = clip.shape
    group_count = frames * height * tile_width * (channels // GROUPS)
    values = clip.astype(jnp.float32)
    center = group_sums(values) / group_count
    spread = group_sums(values * values) / group_count - center * center
    inverse = lax.rsqrt(spread + epsilon)
    normed = (values - expand(center, channels)) * expand(inverse, channels)
    activation = jax.nn.silu(normed).astype(jnp.bfloat16)
    act_pad = jnp.pad(activation, ((0, 0), (2, 0), (1, 1), (1, 1), (0, 0)))
    cot_pad = jnp.pad(cotangent, ((0, 0), (0, 2), (1, 1), (1, 1), (0, 0)))
    row_count = batch * frames * height * tile_width
    flat_cot = cotangent.reshape(row_count, channels)
    blocks = []
    input_grad = jnp.zeros((row_count, channels), jnp.float32)
    for tap in range(27):
        depth_tap = tap // 9
        level_tap = tap // 3 % 3
        width_tap = tap % 3
        window = act_pad[:, depth_tap:depth_tap + frames, level_tap:level_tap + height, width_tap:width_tap + tile_width, :].reshape(row_count, channels)
        blocks.append(jnp.dot(window.T, flat_cot, preferred_element_type=jnp.float32))
        kernel = weights[tap * channels:(tap + 1) * channels]
        shifted = cot_pad[:, 2 - depth_tap:2 - depth_tap + frames, 2 - level_tap:2 - level_tap + height, 2 - width_tap:2 - width_tap + tile_width, :].reshape(row_count, channels)
        input_grad = input_grad + jnp.dot(shifted, kernel.T, preferred_element_type=jnp.float32)
    grad_weight = jnp.concatenate(blocks, axis=0) * (1.0 / math.sqrt(row_count))
    sigmoid_val = jax.nn.sigmoid(normed)
    derivative = sigmoid_val * (1.0 + normed * (1.0 - sigmoid_val))
    norm_grad = input_grad.reshape(clip.shape) * derivative
    grad_total = group_sums(norm_grad) / group_count
    grad_cross = group_sums(norm_grad * normed) / group_count
    grad_input = cotangent.astype(jnp.float32) + expand(inverse, channels) * (norm_grad - expand(grad_total, channels) - normed * expand(grad_cross, channels))
    return (grad_input.astype(jnp.bfloat16), grad_weight)
```

```python
import functools
import math

import jax
import jax.numpy as jnp
from jax import lax
from jax.experimental import pallas as pl
from jax.experimental.pallas import tpu as pltpu
from jax.sharding import PartitionSpec as P

GROUPS = 32
C = 256
H = 16
W = 64
ROWS = H * W
PADDED = ROWS + 2 * W
SHARD = 864
SHARD_PAD = 896
QUARTER = 112
UNIT = 32
VMEM = 56 * 1024 * 1024
epsilon = 1e-06
f32 = jnp.float32
bf16 = jnp.bfloat16


def group_total(rows):
    lane = lax.broadcasted_iota(jnp.int32, rows.shape, 1)
    for s in (1, 2, 4):
        up = pltpu.roll(rows, s, 1)
        down = pltpu.roll(rows, C - s, 1)
        rows = rows + jnp.where((lane & s) != 0, up, down)
    return rows


def center_inverse(stats, count):
    sums = group_total(stats) / count
    center = sums[0:1]
    spread = sums[1:2] - center * center
    return center, lax.rsqrt(spread + epsilon)


def sigmoid(v):
    return 1.0 / (1.0 + jnp.exp(-v))


def widths(target, cot, slot):
    zero = jnp.zeros((W, C), bf16)
    for kw in range(3):
        target[kw, slot, 0:W] = zero
        target[kw, slot, W + ROWS : PADDED] = zero
    column = lax.broadcasted_iota(jnp.int32, (W, C), 0)

    @pl.loop(0, H)
    def _(h):
        row = cot(pl.multiple_of(h * W, W))
        at = pl.ds(pl.multiple_of(h * W + W, W), W)
        wide = row.astype(f32)
        target[1, slot, at] = row
        target[0, slot, at] = jnp.where(column == W - 1, 0.0, pltpu.roll(wide, W - 1, 0)).astype(bf16)
        target[2, slot, at] = jnp.where(column == 0, 0.0, pltpu.roll(wide, 1, 0)).astype(bf16)


def stats_kernel(clip, out):
    def step(i, carry):
        a, b = carry
        v = clip[pl.ds(pl.multiple_of(i * 128, 128), 128)].astype(f32)
        v = v.reshape(16, 8, C)
        return a + v.sum(0), b + (v * v).sum(0)

    zero = jnp.zeros((8, C), f32)
    a, b = lax.fori_loop(0, clip.shape[0] // 128, step, (zero, zero))
    out[0:1] = a.sum(0, keepdims=True)
    out[1:2] = b.sum(0, keepdims=True)


def weight_grad_kernel(count, scale, where, stats, clip, before, cot, after, keep, send, act, wide):
    center, inverse = center_inverse(stats[...], count)
    first = where[0]
    core = where[1]

    def activate(frame, slot, gain):
        @pl.loop(0, ROWS // 256)
        def _(i):
            at = pl.ds(pl.multiple_of(i * 256, 256), 256)
            v = (frame(at).astype(f32) - center) * inverse
            v = v * sigmoid(v)
            if gain is not None:
                v = v * gain
            act[slot, :, at] = v.T.astype(bf16)

    activate(lambda at: before[at], 0, jnp.where(first == 1, 0.0, 1.0))
    activate(lambda at: clip[0, at], 1, None)
    activate(lambda at: clip[1, at], 2, None)
    for t in range(2):
        widths(wide, lambda r, t=t: cot[t, pl.ds(r, W)], t)
    widths(wide, lambda r: after[pl.ds(r, W)], 2)

    @pl.loop(0, 9)
    def _(tap):
        kt = tap // 3
        kh = tap % 3
        frame = jnp.where(kt == 0, 0, 1)
        slot = jnp.where(kt == 2, 0, 1)
        rows = pl.ds(pl.multiple_of((2 - kh) * W, W), ROWS)
        for kw in range(3):
            total = jnp.dot(act[frame], wide[kw, slot, rows], preferred_element_type=f32)
            total += jnp.dot(act[frame + 1], wide[kw, slot + 1, rows], preferred_element_type=f32)
            total = total * scale
            for u in range(C // UNIT):
                unit = (tap * 3 + kw) * (C // UNIT) + u
                shard = unit // (SHARD // UNIT)
                x = shard // 2
                place = jnp.where(x == 0, 0, jnp.where(x == 3, 1, x + 1))
                dest = place * SHARD_PAD + (unit - shard * (SHARD // UNIT)) * UNIT
                mine = (shard % 2) == core
                spare = 4 * SHARD_PAD
                piece = total[u * UNIT : (u + 1) * UNIT]
                keep[pl.ds(pl.multiple_of(jnp.where(mine, dest, spare), UNIT), UNIT)] = piece
                send[pl.ds(pl.multiple_of(jnp.where(mine, spare, dest), UNIT), UNIT)] = piece.astype(bf16)

    for place in range(4):
        tail = slice(place * SHARD_PAD + SHARD, (place + 1) * SHARD_PAD)
        keep[tail] = jnp.zeros((SHARD_PAD - SHARD, C), f32)
        send[tail] = jnp.zeros((SHARD_PAD - SHARD, C), bf16)


def input_grad_kernel(count, stats, clip, cot, after, later, weights, grad, sums, wide):
    center, inverse = center_inverse(stats[...], count)
    for t in range(2):
        widths(wide, lambda r, t=t: cot[t, pl.ds(r, W)], t)
    widths(wide, lambda r: after[pl.ds(r, W)], 2)
    widths(wide, lambda r: later[pl.ds(r, W)], 3)
    contract = (((1,), (1,)), ((), ()))
    grad[...] = jnp.zeros_like(grad)

    @pl.loop(0, 18)
    def _(step):
        tap = step // 2
        frame = step % 2
        kt = tap // 3
        kh = tap % 3
        slot = frame + 2 - kt
        rows = pl.ds(pl.multiple_of((2 - kh) * W, W), ROWS)
        total = None
        for kw in range(3):
            w = weights[pl.ds(pl.multiple_of((tap * 3 + kw) * C, C), C)]
            part = lax.dot_general(wide[kw, slot, rows], w, contract, preferred_element_type=f32)
            total = part if total is None else total + part
        grad[frame] += total

    zero = jnp.zeros((8, C), f32)

    def finish(i, carry):
        a, b = carry
        at = pl.ds(pl.multiple_of((i % 16) * 64, 64), 64)
        frame = i // 16
        v = (clip[frame, at].astype(f32) - center) * inverse
        s = sigmoid(v)
        g = grad[frame, at] * (s * (1.0 + v * (1.0 - s)))
        grad[frame, at] = g
        return a + g.reshape(8, 8, C).sum(0), b + (g * v).reshape(8, 8, C).sum(0)

    a, b = lax.fori_loop(0, 32, finish, (zero, zero))
    sums[0:1] = a.sum(0, keepdims=True)
    sums[1:2] = b.sum(0, keepdims=True)


def final_kernel(count, stats, sums, clip, cot, grad, out):
    center, inverse = center_inverse(stats[...], count)
    means = group_total(sums[...]) / count
    total, cross = means[0:1], means[1:2]

    @pl.loop(0, 32)
    def _(i):
        at = pl.ds(pl.multiple_of((i % 16) * 64, 64), 64)
        frame = i // 16
        v = (clip[frame, at].astype(f32) - center) * inverse
        g = cot[frame, at].astype(f32) + inverse * (grad[frame, at] - total - v * cross)
        out[frame, at] = g.astype(bf16)


def call(kernel, out_shape, args, scratch=(), flops=0, bytes_accessed=4_000_000, scalars=0):
    specs = [pl.BlockSpec(memory_space=pltpu.SMEM)] * scalars
    specs += [pl.BlockSpec(memory_space=pltpu.VMEM)] * (len(args) - scalars)
    return pl.pallas_call(
        kernel,
        out_shape=out_shape,
        in_specs=specs,
        out_specs=jax.tree.map(lambda _: pl.BlockSpec(memory_space=pltpu.VMEM), out_shape),
        scratch_shapes=list(scratch),
        compiler_params=pltpu.CompilerParams(vmem_limit_bytes=VMEM),
        cost_estimate=pl.CostEstimate(flops=flops, bytes_accessed=bytes_accessed, transcendentals=0),
    )(*args)


FLIP = {"a": (1, 0, 3, 2), "b": (3, 2, 1, 0)}
AXES = {"z": ("tm", 16, 1), "y": ("tm", 16, 4), "x": ("fsdp", 8, 2)}


def swap(block, axis, step):
    name, size, stride = AXES[axis]
    route = []
    for i in range(size):
        place = (i // stride) % 4
        route.append((i, i + (FLIP[step][place] - place) * stride))
    return lax.ppermute(block, name, route)


def bit(axis, step):
    name, _, stride = AXES[axis]
    place = (lax.axis_index(name) // stride) % 4
    high, low = place // 2, place % 2
    return high ^ low if step == "a" else high


def pick(block, index, dim):
    return lax.dynamic_index_in_dim(block, index, dim, keepdims=False)


def halve(block, axis, step, dim):
    mine = bit(axis, step)
    arrived = swap(pick(block, 1 - mine, dim).astype(bf16), axis, step)
    return pick(block, mine, dim) + arrived.astype(f32)


def both(block, axis, step):
    sent = block.astype(bf16)
    return sent.astype(f32) + swap(sent, axis, step).astype(f32)


def double(block, axis, step, dim):
    other = swap(block, axis, step)
    mine = bit(axis, step)
    pair = jnp.stack([block, other], dim)
    flipped = jnp.stack([other, block], dim)
    return jnp.where(mine == 0, pair, flipped)


def all_sum(values):
    for axis, step in (("z", "a"), ("z", "b"), ("y", "a"), ("y", "b")):
        values = values + swap(values, axis, step)
    return values


def reduce_weight_grad(keep, send):
    arrived = lax.ppermute(send, "fsdp", [(i, i ^ 1) for i in range(8)])
    local = keep[: 4 * SHARD_PAD] + arrived[: 4 * SHARD_PAD].astype(f32)
    local = local.reshape(2, 2, 2, 2, 2, QUARTER, C)
    halves = []
    for half, axis in ((0, "z"), (1, "y")):
        left = local[:, :, half, :, :, :, : C // 2]
        right = local[:, :, half, :, :, :, C // 2 :]
        left = halve(left, axis, "a", 2)
        right = halve(right, axis, "b", 3)
        left = halve(left, axis, "b", 2)
        right = halve(right, axis, "a", 2)
        halves.append(jnp.concatenate([left, right], axis=-1))
    zs, ys = halves
    zs = halve(zs, "x", "a", 0)
    ys = halve(ys, "x", "b", 1)
    zs = halve(zs, "x", "b", 0)
    ys = halve(ys, "x", "a", 0)
    zs = both(both(zs, "y", "a"), "y", "b").astype(bf16)
    ys = both(both(ys, "z", "a"), "z", "b").astype(bf16)
    zs = double(double(zs, "z", "b", 0), "z", "a", 0)
    ys = double(double(ys, "y", "b", 0), "y", "a", 0)
    full = jnp.stack([zs, ys], 0).reshape(SHARD_PAD, C)
    return full[:SHARD].astype(f32)


def passed(block, distance):
    route = [(i - distance, i) for i in range(16) if 0 <= i - distance < 16]
    return lax.ppermute(block, "tm", route)


def per_device(clip, cotangent, weights):
    shape = clip.shape
    clip = clip.reshape(2, ROWS, C)
    cot = cotangent.reshape(2, ROWS, C)
    count = 32 * ROWS * (C // GROUPS)
    scale = 1.0 / math.sqrt(8 * 32 * ROWS)
    after = passed(cot[0], -1)
    before = passed(clip[1], 1)
    later = passed(cot[1], -1)
    full_weights = lax.all_gather(weights, "fsdp", axis=0, tiled=True)
    S = jax.ShapeDtypeStruct
    stats = call(stats_kernel, S((2, C), f32), (clip.reshape(2 * ROWS, C),))
    stats = all_sum(stats)
    where = jnp.stack([(lax.axis_index("tm") == 0).astype(jnp.int32), (lax.axis_index("fsdp") % 2).astype(jnp.int32)])


    keep, send = call(
        functools.partial(weight_grad_kernel, count, scale),
        (S((4 * SHARD_PAD + UNIT, C), f32), S((4 * SHARD_PAD + UNIT, C), bf16)),
        (where, stats, clip, before, cot, after),
        [pltpu.VMEM((3, C, ROWS), bf16), pltpu.VMEM((3, 3, PADDED, C), bf16)],
        flops=2 * 27 * C * C * 2 * ROWS,
        scalars=1,
    )
    grad_weight = reduce_weight_grad(keep, send)
    grad, sums = call(
        functools.partial(input_grad_kernel, count),
        (S((2, ROWS, C), f32), S((2, C), f32)),
        (stats, clip, cot, after, later, full_weights),
        [pltpu.VMEM((3, 4, PADDED, C), bf16)],
        flops=2 * 27 * C * C * 2 * ROWS,
    )
    sums = all_sum(sums)
    grad_input = call(
        functools.partial(final_kernel, count),
        S((2, ROWS, C), bf16),
        (stats, sums, clip, cot, grad),
    )
    return grad_input.reshape(shape), grad_weight


def solution(mesh):
    in_specs = (
        P("fsdp", "tm", None, None, None),
        P("fsdp", "tm", None, None, None),
        P("fsdp", None),
    )
    out_specs = (P("fsdp", "tm", None, None, None), P("fsdp", None))
    return jax.shard_map(
        per_device, mesh=mesh, in_specs=in_specs, out_specs=out_specs, check_vma=False
    )
```

```python
import functools
import math

import jax
import jax.numpy as jnp
from jax import lax
from jax.experimental import pallas as pl
from jax.experimental.pallas import tpu as pltpu
from jax.sharding import PartitionSpec as P

GROUPS = 32
C = 256
H = 16
W = 64
ROWS = H * W
PADDED = ROWS + 2 * W
HALF = C // 2
SHARD = 864
SHARD_PAD = 896
QUARTER = 224
UNIT = 32
VMEM = 28 * 1024 * 1024
epsilon = 1e-06
f32 = jnp.float32
bf16 = jnp.bfloat16


def group_total(rows):
    lane = lax.broadcasted_iota(jnp.int32, rows.shape, 1)
    for s in (1, 2, 4):
        up = pltpu.roll(rows, s, 1)
        down = pltpu.roll(rows, C - s, 1)
        rows = rows + jnp.where((lane & s) != 0, up, down)
    return rows


def center_inverse(stats, count):
    sums = group_total(stats) / count
    center = sums[0:1]
    spread = sums[1:2] - center * center
    return center, lax.rsqrt(spread + epsilon)


def sigmoid(v):
    return 1.0 / (1.0 + jnp.exp(-v))


def widths(target, cot, slot):
    zero = jnp.zeros((W, C), bf16)
    for kw in range(3):
        target[kw, slot, 0:W] = zero
        target[kw, slot, W + ROWS : PADDED] = zero
    column = lax.broadcasted_iota(jnp.int32, (W, C), 0)

    @pl.loop(0, H)
    def _(h):
        row = cot(pl.multiple_of(h * W, W))
        at = pl.ds(pl.multiple_of(h * W + W, W), W)
        wide = row.astype(f32)
        target[1, slot, at] = row
        target[0, slot, at] = jnp.where(column == W - 1, 0.0, pltpu.roll(wide, W - 1, 0)).astype(bf16)
        target[2, slot, at] = jnp.where(column == 0, 0.0, pltpu.roll(wide, 1, 0)).astype(bf16)


def stats_kernel(clip, out):
    def step(i, carry):
        a, b = carry
        v = clip[pl.ds(pl.multiple_of(i * 128, 128), 128)].astype(f32)
        v = v.reshape(16, 8, C)
        return a + v.sum(0), b + (v * v).sum(0)

    zero = jnp.zeros((8, C), f32)
    a, b = lax.fori_loop(0, clip.shape[0] // 128, step, (zero, zero))
    out[0:1] = a.sum(0, keepdims=True)
    out[1:2] = b.sum(0, keepdims=True)


def widths_kernel(cot, wide):
    for t in range(cot.shape[0]):
        widths(wide, lambda r, t=t: cot[t, pl.ds(r, W)], t)


def tap_rows(kh):
    return pl.ds(pl.multiple_of((2 - kh) * W, W), ROWS)


CONTRACT_ROWS = (((0,), (0,)), ((), ()))
CONTRACT_COLUMNS = (((1,), (1,)), ((), ()))


def tap_product(frames, views, channels):
    total = None
    for frame, view in zip(frames, views):
        part = lax.dot_general(frame[:, channels], view, CONTRACT_ROWS, preferred_element_type=f32)
        total = part if total is None else total + part
    return total


def store_tap(tap, total, first_unit, core, keep, send):
    spare = 2 * SHARD_PAD
    for u in range(total.shape[0] // UNIT):
        unit = tap * (C // UNIT) + first_unit + u
        shard = unit // (SHARD // UNIT)
        dest = (shard // 2 % 2) * SHARD_PAD + (unit - shard * (SHARD // UNIT)) * UNIT
        mine = (shard % 2) == core
        piece = total[u * UNIT : (u + 1) * UNIT]
        keep[pl.ds(pl.multiple_of(jnp.where(mine, dest, spare), UNIT), UNIT)] = piece
        send[pl.ds(pl.multiple_of(jnp.where(mine, spare, dest), UNIT), UNIT)] = piece.astype(bf16)


def clear_tails(keep, send):
    for place in range(2):
        tail = slice(place * SHARD_PAD + SHARD, (place + 1) * SHARD_PAD)
        keep[tail] = jnp.zeros((SHARD_PAD - SHARD, C), f32)
        send[tail] = jnp.zeros((SHARD_PAD - SHARD, C), bf16)
    keep[2 * SHARD_PAD :] = jnp.zeros((UNIT, C), f32)
    send[2 * SHARD_PAD :] = jnp.zeros((UNIT, C), bf16)


def upper_kernel(count, scale, where, stats, clip, before, near, after, act, keep, send):
    center, inverse = center_inverse(stats[...], count)
    core = where[1]

    def activate(frame, slot, gain):
        @pl.loop(0, ROWS // 64)
        def _(i):
            at = pl.ds(pl.multiple_of(i * 64, 64), 64)
            v = (frame(at).astype(f32) - center) * inverse
            v = v * sigmoid(v)
            if gain is not None:
                v = v * gain
            act[slot, at] = v.astype(bf16)

    activate(lambda at: before[at], 0, jnp.where(where[0] == 1, 0.0, 1.0))
    activate(lambda at: clip[0, at], 1, None)
    activate(lambda at: clip[1, at], 2, None)

    @pl.loop(0, 9)
    def _(t):
        rows = tap_rows(t // 3)
        kw = t % 3
        total = tap_product((act[1], act[2]), (near[kw, 0, rows], near[kw, 1, rows]), slice(None))
        store_tap(18 + t, total * scale, 0, core, keep, send)

    @pl.loop(5, 9)
    def _(t):
        rows = tap_rows(t // 3)
        kw = t % 3
        total = tap_product((act[1], act[2]), (near[kw, 1, rows], after[kw, 0, rows]), slice(None))
        store_tap(9 + t, total * scale, 0, core, keep, send)

    rows = slice(W, W + ROWS)
    total = tap_product((act[1], act[2]), (near[1, 1, rows], after[1, 0, rows]), slice(HALF, C))
    store_tap(13, total * scale, HALF // UNIT, core, keep, send)
    clear_tails(keep, send)


def lower_kernel(scale, where, act, near, after, keep, send):
    core = where[1]

    @pl.loop(0, 9)
    def _(t):
        rows = tap_rows(t // 3)
        kw = t % 3
        total = tap_product((act[0], act[1]), (near[kw, 1, rows], after[kw, 0, rows]), slice(None))
        store_tap(t, total * scale, 0, core, keep, send)

    @pl.loop(0, 4)
    def _(t):
        rows = tap_rows(t // 3)
        kw = t % 3
        total = tap_product((act[1], act[2]), (near[kw, 1, rows], after[kw, 0, rows]), slice(None))
        store_tap(9 + t, total * scale, 0, core, keep, send)

    rows = slice(W, W + ROWS)
    total = tap_product((act[1], act[2]), (near[1, 1, rows], after[1, 0, rows]), slice(0, HALF))
    store_tap(13, total * scale, 0, core, keep, send)
    clear_tails(keep, send)


def pack_kernel(where, own, left, right, far, packed):
    x = where[2]
    for block, distance in ((own, 0), (left, 3), (right, 1), (far, 2)):
        packed[(x + distance) % 4] = block[...]


def frame_grad(count, frame, stats, clip, views, weights, grad, sums):
    center, inverse = center_inverse(stats[...], count)
    rows_per = 256

    @pl.loop(0, ROWS // rows_per)
    def _(i):
        start = i * rows_per
        total = jnp.zeros((rows_per, C), f32)
        for tap in range(27):
            kt, kh, kw = tap // 9, tap // 3 % 3, tap % 3
            rows = pl.ds(pl.multiple_of((2 - kh) * W + start, W), rows_per)
            w = weights[tap * C : (tap + 1) * C]
            total += lax.dot_general(
                views[2 - kt](kw, rows), w, CONTRACT_COLUMNS, preferred_element_type=f32
            )
        grad[pl.ds(pl.multiple_of(start, rows_per), rows_per)] = total

    zero = jnp.zeros((8, C), f32)

    def finish(i, carry):
        a, b = carry
        at = pl.ds(pl.multiple_of(i * 64, 64), 64)
        v = (clip[frame, at].astype(f32) - center) * inverse
        s = sigmoid(v)
        g = grad[at] * (s * (1.0 + v * (1.0 - s)))
        grad[at] = g
        return a + g.reshape(8, 8, C).sum(0), b + (g * v).reshape(8, 8, C).sum(0)

    a, b = lax.fori_loop(0, ROWS // 64, finish, (zero, zero))
    sums[0:1] = a.sum(0, keepdims=True)
    sums[1:2] = b.sum(0, keepdims=True)


def first_grad_kernel(count, where, stats, clip, near, after, mine, other, order, grad, sums, full):
    core = where[1]
    for x in range(4):
        full[pl.ds(pl.multiple_of((2 * x + core) * SHARD, UNIT), SHARD)] = mine[x]
        full[pl.ds(pl.multiple_of((2 * x + 1 - core) * SHARD, UNIT), SHARD)] = other[x]
    views = (
        lambda kw, rows: near[kw, 0, rows],
        lambda kw, rows: near[kw, 1, rows],
        lambda kw, rows: after[kw, 0, rows],
    )
    frame_grad(count, 0, stats, clip, views, full, grad, sums)


def second_grad_kernel(count, stats, clip, near, after, later, full, order, grad, sums, wide):
    widths(wide, lambda r: later[pl.ds(r, W)], 0)
    views = (
        lambda kw, rows: near[kw, 1, rows],
        lambda kw, rows: after[kw, 0, rows],
        lambda kw, rows: wide[kw, 0, rows],
    )
    frame_grad(count, 1, stats, clip, views, full, grad, sums)


def final_kernel(count, stats, sums, clip, cot, grad0, grad1, out):
    center, inverse = center_inverse(stats[...], count)
    means = group_total(sums[...]) / count
    total, cross = means[0:1], means[1:2]
    for frame, grad in enumerate((grad0, grad1)):

        @pl.loop(0, ROWS // 64)
        def _(i, frame=frame, grad=grad):
            at = pl.ds(pl.multiple_of(i * 64, 64), 64)
            v = (clip[frame, at].astype(f32) - center) * inverse
            g = cot[frame, at].astype(f32) + inverse * (grad[at] - total - v * cross)
            out[frame, at] = g.astype(bf16)


def split_core_kernel(where, keep_up, keep_low, got_up, got_low, order, left, right, left_out, right_out):
    a, b = where[3], where[4]
    places = ((keep_low, got_low, 0), (keep_up, got_up, 1), (keep_low, got_low, 1), (keep_up, got_up, 0))
    for place, (keep, got, x) in enumerate(places):

        def block(quarter, columns):
            at = pl.ds(pl.multiple_of(x * SHARD_PAD + quarter * QUARTER, UNIT), QUARTER)
            return keep[at, columns] + got[at, columns].astype(f32)

        for i in range(2):
            left[place, i] = block(2 * a + i, slice(0, HALF))
            left_out[place, i] = block(2 * (1 - a) + i, slice(0, HALF)).astype(bf16)
            right[place, i] = block(2 * i + b, slice(HALF, C))
            right_out[place, i] = block(2 * i + 1 - b, slice(HALF, C)).astype(bf16)


def split_z_kernel(where, left, right, left_in, right_in, order, left_next, right_next, left_out, right_out):
    for place in range(4):
        for held, got, keep, out, mine in (
            (left, left_in, left_next, left_out, where[4]),
            (right, right_in, right_next, right_out, where[3]),
        ):
            keep[place] = held[place, mine] + got[place, mine].astype(f32)
            out[place] = (held[place, 1 - mine] + got[place, 1 - mine].astype(f32)).astype(bf16)


def split_x_kernel(where, left, right, left_in, right_in, left_next, right_next, left_out, right_out):
    a, b = where[5], where[6]
    for i in range(2):
        for held, got, keep, out, mine, its in (
            (left, left_in, left_next, left_out, 2 * a + i, 2 * (1 - a) + i),
            (right, right_in, right_next, right_out, 2 * i + b, 2 * i + 1 - b),
        ):
            keep[i] = held[mine] + got[mine].astype(f32)
            out[i] = (held[its] + got[its].astype(f32)).astype(bf16)


def split_last_kernel(where, left, right, left_in, right_in, left_next, right_next, left_out, right_out):
    for held, got, keep, out, mine in (
        (left, left_in, left_next, left_out, where[6]),
        (right, right_in, right_next, right_out, where[5]),
    ):
        keep[...] = held[mine] + got[mine].astype(f32)
        out[...] = (held[1 - mine] + got[1 - mine].astype(f32)).astype(bf16)


def write_sums(sums, rows, out):
    rows[12:16] = jnp.zeros((4, HALF), f32)
    rest = sums
    for k in range(3):
        term = rest.astype(bf16).astype(f32)
        rest = rest - term
        rows[4 * k : 4 * k + 2] = term[:, :HALF]
        rows[4 * k + 2 : 4 * k + 4] = term[:, HALF:]
    out[...] = rows[...].astype(bf16)


def read_sums(block):
    wide = block.astype(f32)
    total = wide[0:4] + wide[4:8] + wide[8:12]
    return jnp.concatenate([total[0:2], total[2:4]], axis=1)


def start_sum_kernel(left, right, left_in, right_in, sums0, sums1, left_out, right_out, rows):
    left_out[:QUARTER] = (left[...] + left_in[...].astype(f32)).astype(bf16)
    right_out[...] = (right[...] + right_in[...].astype(f32)).astype(bf16)
    write_sums(sums0[...] + sums1[...], rows, left_out.at[QUARTER:])


def next_sum_kernel(left, right, left_in, right_in, left_out, right_out, rows):
    at = slice(0, QUARTER)
    left_out[at] = (left[at].astype(f32) + left_in[at].astype(f32)).astype(bf16)
    right_out[...] = (right[...].astype(f32) + right_in[...].astype(f32)).astype(bf16)
    total = read_sums(left[QUARTER:]) + read_sums(left_in[QUARTER:])
    write_sums(total, rows, left_out.at[QUARTER:])


def join_kernel(where, left, right, left_in, right_in, left_out, right_out, rows):
    a, b = where[3], where[4]
    left_out[pl.ds(pl.multiple_of(b * QUARTER, UNIT), QUARTER)] = left[:QUARTER]
    left_out[pl.ds(pl.multiple_of((1 - b) * QUARTER, UNIT), QUARTER)] = left_in[:QUARTER]
    right_out[pl.ds(pl.multiple_of(a * QUARTER, UNIT), QUARTER)] = right[...]
    right_out[pl.ds(pl.multiple_of((1 - a) * QUARTER, UNIT), QUARTER)] = right_in[...]
    total = read_sums(left[QUARTER:]) + read_sums(left_in[QUARTER:])
    write_sums(total, rows, left_out.at[2 * QUARTER :])


def finish_kernel(where, left, right, left_in, right_in, grad_weight, sums, full):
    a, b = where[3], where[4]
    for i in range(2):
        held = slice(i * QUARTER, (i + 1) * QUARTER)
        for block, quarter in ((left, 2 * a + i), (left_in, 2 * (1 - a) + i)):
            at = pl.ds(pl.multiple_of(quarter * QUARTER, UNIT), QUARTER)
            full[at, :HALF] = block[held].astype(f32)
        for block, quarter in ((right, 2 * i + b), (right_in, 2 * i + 1 - b)):
            at = pl.ds(pl.multiple_of(quarter * QUARTER, UNIT), QUARTER)
            full[at, HALF:] = block[held].astype(f32)
    grad_weight[...] = full[:SHARD]
    sums[...] = read_sums(left[2 * QUARTER :]) + read_sums(left_in[2 * QUARTER :])


def call(kernel, out_shape, args, scratch=(), flops=0, bytes_accessed=1_000_000, scalars=0, order=()):
    specs = [pl.BlockSpec(memory_space=pltpu.SMEM)] * scalars
    specs += [pl.BlockSpec(memory_space=pltpu.VMEM)] * (len(args) - scalars)
    specs += [pl.BlockSpec(memory_space=pl.ANY)] * len(order)
    return pl.pallas_call(
        kernel,
        out_shape=out_shape,
        in_specs=specs,
        out_specs=jax.tree.map(lambda _: pl.BlockSpec(memory_space=pltpu.VMEM), out_shape),
        scratch_shapes=list(scratch),
        compiler_params=pltpu.CompilerParams(vmem_limit_bytes=VMEM),
        cost_estimate=pl.CostEstimate(flops=flops, bytes_accessed=bytes_accessed, transcendentals=0),
    )(*args, *order)


FLIP = {"a": (1, 0, 3, 2), "b": (3, 2, 1, 0), "left": (1, 2, 3, 0), "right": (3, 0, 1, 2), "far": (2, 3, 0, 1)}
AXES = {"z": ("tm", 16, 1), "y": ("tm", 16, 4), "x": ("fsdp", 8, 2)}


def swap(block, axis, step):
    name, size, stride = AXES[axis]
    route = []
    for i in range(size):
        place = (i // stride) % 4
        route.append((i, i + (FLIP[step][place] - place) * stride))
    return lax.ppermute(block, name, route)


def swap_core(block):
    return lax.ppermute(block, "fsdp", [(i, i ^ 1) for i in range(8)])


def all_sum(values):
    for axis, step in (("y", "a"), ("y", "b"), ("z", "a"), ("z", "b")):
        values = values + swap(values, axis, step)
    return values


def passed(block, distance):
    route = [(i - distance, i) for i in range(16) if 0 <= i - distance < 16]
    return lax.ppermute(block, "tm", route)


def per_device(clip, cotangent, weights):
    shape = clip.shape
    clip = clip.reshape(2, ROWS, C)
    cot = cotangent.reshape(2, ROWS, C)
    count = 32 * ROWS * (C // GROUPS)
    scale = 1.0 / math.sqrt(8 * 32 * ROWS)
    partial = functools.partial
    S = jax.ShapeDtypeStruct
    tm = lax.axis_index("tm")
    fsdp = lax.axis_index("fsdp")
    z, x = tm % 4, fsdp // 2
    where = [tm == 0, fsdp % 2, x, z // 2 ^ z % 2, z // 2, x // 2 ^ x % 2, x // 2]
    where = jnp.stack([jnp.asarray(v, jnp.int32) for v in where])

    after = passed(cot[0], -1)
    before = passed(clip[1], 1)
    later = passed(cot[1], -1)
    mine = call(
        pack_kernel,
        S((4, SHARD, C), bf16),
        (where, weights, swap(weights, "x", "left"), swap(weights, "x", "right"), swap(weights, "x", "far")),
        scalars=1,
    )
    other = swap_core(mine)
    stats = call(stats_kernel, S((2, C), f32), (clip.reshape(2 * ROWS, C),))
    stats = all_sum(stats)
    near = call(widths_kernel, S((3, 2, PADDED, C), bf16), (cot,))
    after = call(widths_kernel, S((3, 1, PADDED, C), bf16), (after[None],))

    rows = 2 * SHARD_PAD + UNIT
    half_flops = 27 * C * C * 2 * ROWS
    act, keep_up, send_up = call(
        partial(upper_kernel, count, scale),
        (S((3, ROWS, C), bf16), S((rows, C), f32), S((rows, C), bf16)),
        (where, stats, clip, before, near, after),
        flops=half_flops,
        scalars=1,
    )
    got_up = swap_core(send_up)
    keep_low, send_low = call(
        partial(lower_kernel, scale),
        (S((rows, C), f32), S((rows, C), bf16)),
        (where, act, near, after),
        flops=half_flops,
        scalars=1,
    )
    got_low = swap_core(send_low)
    grad0, sums0, full = call(
        partial(first_grad_kernel, count),
        (S((ROWS, C), f32), S((2, C), f32), S((8 * SHARD, C), bf16)),
        (where, stats, clip, near, after, mine, other),
        flops=half_flops,
        scalars=1,
        order=(keep_low,),
    )

    block = lambda *dims: (S(dims + (QUARTER, HALF), f32),) * 2 + (S(dims + (QUARTER, HALF), bf16),) * 2
    left, right, left_out, right_out = call(
        split_core_kernel, block(4, 2), (where, keep_up, keep_low, got_up, got_low), scalars=1, order=(sums0,)
    )
    grad1, sums1 = call(
        partial(second_grad_kernel, count),
        (S((ROWS, C), f32), S((2, C), f32)),
        (stats, clip, near, after, later, full),
        [pltpu.VMEM((3, 1, PADDED, C), bf16)],
        flops=half_flops,
        order=(left_out,),
    )
    got = swap(left_out, "z", "a"), swap(right_out, "z", "b")
    left, right, left_out, right_out = call(
        split_z_kernel, block(4), (where, left, right, *got), scalars=1, order=(sums1,)
    )
    got = swap(left_out, "z", "b"), swap(right_out, "z", "a")
    left, right, left_out, right_out = call(split_x_kernel, block(2), (where, left, right, *got), scalars=1)
    got = swap(left_out, "x", "a"), swap(right_out, "x", "b")
    left, right, left_out, right_out = call(split_last_kernel, block(), (where, left, right, *got), scalars=1)
    got = swap(left_out, "x", "b"), swap(right_out, "x", "a")

    pair = lambda n: (S((n * QUARTER + 16, HALF), bf16), S((n * QUARTER, HALF), bf16))
    rows16 = [pltpu.VMEM((16, HALF), f32)]
    left, right = call(start_sum_kernel, pair(1), (left, right, *got, sums0, sums1), rows16)
    got = swap(left, "y", "a"), swap(right, "y", "b")
    left, right = call(next_sum_kernel, pair(1), (left, right, *got), rows16)
    got = swap(left, "y", "b"), swap(right, "y", "a")
    left, right = call(next_sum_kernel, pair(1), (left, right, *got), rows16)
    got = swap(left, "z", "b"), swap(right, "z", "a")
    left, right = call(join_kernel, pair(2), (where, left, right, *got), rows16, scalars=1)
    got = swap(left, "z", "a"), swap(right, "z", "b")
    grad_weight, sums = call(
        finish_kernel,
        (S((SHARD, C), f32), S((2, C), f32)),
        (where, left, right, *got),
        [pltpu.VMEM((SHARD_PAD, C), f32)],
        scalars=1,
    )
    grad_input = call(
        partial(final_kernel, count), S((2, ROWS, C), bf16), (stats, sums, clip, cot, grad0, grad1)
    )
    return grad_input.reshape(shape), grad_weight


def solution(mesh):
    in_specs = (
        P("fsdp", "tm", None, None, None),
        P("fsdp", "tm", None, None, None),
        P("fsdp", None),
    )
    out_specs = (P("fsdp", "tm", None, None, None), P("fsdp", None))
    return jax.shard_map(
        per_device, mesh=mesh, in_specs=in_specs, out_specs=out_specs, check_vma=False
    )
```

```python
import functools
import math

import jax
import jax.numpy as jnp
from jax import lax
from jax.experimental import pallas as pl
from jax.experimental.pallas import tpu as pltpu
from jax.sharding import PartitionSpec as P

GROUPS = 32
C = 256
H = 16
W = 64
ROWS = H * W
PADDED = ROWS + 2 * W
HALF = C // 2
SHARD = 864
SHARD_PAD = 896
QUARTER = 224
UNIT = 32
VMEM = 20 * 1024 * 1024
epsilon = 1e-06
f32 = jnp.float32
bf16 = jnp.bfloat16


def group_total(rows):
    lane = lax.broadcasted_iota(jnp.int32, rows.shape, 1)
    for s in (1, 2, 4):
        up = pltpu.roll(rows, s, 1)
        down = pltpu.roll(rows, C - s, 1)
        rows = rows + jnp.where((lane & s) != 0, up, down)
    return rows


def center_inverse(stats, count):
    sums = group_total(stats) / count
    center = sums[0:1]
    spread = sums[1:2] - center * center
    return center, lax.rsqrt(spread + epsilon)


def sigmoid(v):
    return 1.0 / (1.0 + jnp.exp(-v))


def widths(target, cot, slot):
    zero = jnp.zeros((W, C), bf16)
    for kw in range(3):
        target[kw, slot, 0:W] = zero
        target[kw, slot, W + ROWS : PADDED] = zero
    column = lax.broadcasted_iota(jnp.int32, (W, C), 0)

    @pl.loop(0, H)
    def _(h):
        row = cot(pl.multiple_of(h * W, W))
        at = pl.ds(pl.multiple_of(h * W + W, W), W)
        wide = row.astype(f32)
        target[1, slot, at] = row
        target[0, slot, at] = jnp.where(column == W - 1, 0.0, pltpu.roll(wide, W - 1, 0)).astype(bf16)
        target[2, slot, at] = jnp.where(column == 0, 0.0, pltpu.roll(wide, 1, 0)).astype(bf16)


def stats_kernel(clip, out):
    def step(i, carry):
        a, b = carry
        v = clip[pl.ds(pl.multiple_of(i * 128, 128), 128)].astype(f32)
        v = v.reshape(16, 8, C)
        return a + v.sum(0), b + (v * v).sum(0)

    zero = jnp.zeros((8, C), f32)
    a, b = lax.fori_loop(0, clip.shape[0] // 128, step, (zero, zero))
    out[0:1] = a.sum(0, keepdims=True)
    out[1:2] = b.sum(0, keepdims=True)


def copy_kernel(clip, cot, order, first, second, last):
    first[...] = cot[0]
    second[...] = cot[1]
    last[...] = clip[1]


def widths_kernel(cot, *refs):
    wide = refs[-1]
    for t in range(cot.shape[0]):
        widths(wide, lambda r, t=t: cot[t, pl.ds(r, W)], t)


def ring_sum_kernel(own, before, after, far, out):
    out[...] = (own[...] + far[...]) + (before[...] + after[...])


def tap_rows(kh):
    return pl.ds(pl.multiple_of((2 - kh) * W, W), ROWS)


CONTRACT_ROWS = (((0,), (0,)), ((), ()))
CONTRACT_COLUMNS = (((1,), (1,)), ((), ()))


def tap_product(frames, views, channels):
    total = None
    for frame, view in zip(frames, views):
        part = lax.dot_general(frame[:, channels], view, CONTRACT_ROWS, preferred_element_type=f32)
        total = part if total is None else total + part
    return total


def store_tap(tap, total, first_unit, core, keep, send):
    spare = 2 * SHARD_PAD
    for u in range(total.shape[0] // UNIT):
        unit = tap * (C // UNIT) + first_unit + u
        shard = (unit * 1214) >> 15
        dest = ((shard >> 1) & 1) * SHARD_PAD + (unit - shard * (SHARD // UNIT)) * UNIT
        mine = (shard & 1) == core
        piece = total[u * UNIT : (u + 1) * UNIT]
        keep[pl.ds(pl.multiple_of(jnp.where(mine, dest, spare), UNIT), UNIT)] = piece
        send[pl.ds(pl.multiple_of(jnp.where(mine, spare, dest), UNIT), UNIT)] = piece.astype(bf16)


def clear_tails(keep, send):
    for place in range(2):
        tail = slice(place * SHARD_PAD + SHARD, (place + 1) * SHARD_PAD)
        keep[tail] = jnp.zeros((SHARD_PAD - SHARD, C), f32)
        send[tail] = jnp.zeros((SHARD_PAD - SHARD, C), bf16)
    keep[2 * SHARD_PAD :] = jnp.zeros((UNIT, C), f32)
    send[2 * SHARD_PAD :] = jnp.zeros((UNIT, C), bf16)


def middle_taps(low, high, channels, scale, core, act, near, after, keep, send):
    for tap in range(low, high):
        kh, kw = tap // 3 % 3, tap % 3
        rows = slice((2 - kh) * W, (2 - kh) * W + ROWS)
        total = tap_product((act[1], act[2]), (near[kw, 1, rows], after[kw, 0, rows]), channels)
        store_tap(tap, total * scale, channels.start // UNIT, core, keep, send)


def upper_kernel(count, scale, where, stats, clip, before, near, after, act, keep, send):
    center, inverse = center_inverse(stats[...], count)
    core = where[1]

    def activate(frame, slot, gain):
        @pl.loop(0, ROWS // 64)
        def _(i):
            at = pl.ds(pl.multiple_of(i * 64, 64), 64)
            v = (frame(at).astype(f32) - center) * inverse
            v = v * sigmoid(v)
            if gain is not None:
                v = v * gain
            act[slot, at] = v.astype(bf16)

    activate(lambda at: before[at], 0, jnp.where(where[0] == 1, 0.0, 1.0))
    activate(lambda at: clip[0, at], 1, None)
    activate(lambda at: clip[1, at], 2, None)

    @pl.loop(0, 3)
    def _(kh):
        rows = tap_rows(kh)
        for kw in range(3):
            total = tap_product((act[1], act[2]), (near[kw, 0, rows], near[kw, 1, rows]), slice(None))
            store_tap(18 + kh * 3 + kw, total * scale, 0, core, keep, send)

    middle_taps(14, 18, slice(0, C), scale, core, act, near, after, keep, send)
    middle_taps(13, 14, slice(HALF, C), scale, core, act, near, after, keep, send)
    clear_tails(keep, send)


def lower_kernel(scale, where, act, near, after, order, keep, send):
    core = where[1]

    @pl.loop(0, 3)
    def _(kh):
        rows = tap_rows(kh)
        for kw in range(3):
            total = tap_product((act[0], act[1]), (near[kw, 1, rows], after[kw, 0, rows]), slice(None))
            store_tap(kh * 3 + kw, total * scale, 0, core, keep, send)

    middle_taps(9, 13, slice(0, C), scale, core, act, near, after, keep, send)
    middle_taps(13, 14, slice(0, HALF), scale, core, act, near, after, keep, send)
    clear_tails(keep, send)


def pack_kernel(where, own, left, right, far, order, packed):
    x = where[2]
    for block, distance in ((own, 0), (left, 3), (right, 1), (far, 2)):
        packed[(x + distance) % 4] = block[...]


def frame_grad(count, frame, stats, clip, views, weights, grad, sums):
    center, inverse = center_inverse(stats[...], count)
    rows_per = 256

    @pl.loop(0, ROWS // rows_per)
    def _(i):
        start = i * rows_per
        total = jnp.zeros((rows_per, C), f32)
        for tap in range(27):
            kt, kh, kw = tap // 9, tap // 3 % 3, tap % 3
            rows = pl.ds(pl.multiple_of((2 - kh) * W + start, W), rows_per)
            w = weights[tap * C : (tap + 1) * C]
            total += lax.dot_general(
                views[2 - kt](kw, rows), w, CONTRACT_COLUMNS, preferred_element_type=f32
            )
        grad[pl.ds(pl.multiple_of(start, rows_per), rows_per)] = total

    zero = jnp.zeros((8, C), f32)

    def finish(i, carry):
        a, b = carry
        at = pl.ds(pl.multiple_of(i * 64, 64), 64)
        v = (clip[frame, at].astype(f32) - center) * inverse
        s = sigmoid(v)
        g = grad[at] * (s * (1.0 + v * (1.0 - s)))
        grad[at] = g
        return a + g.reshape(8, 8, C).sum(0), b + (g * v).reshape(8, 8, C).sum(0)

    a, b = lax.fori_loop(0, ROWS // 64, finish, (zero, zero))
    sums[0:1] = a.sum(0, keepdims=True)
    sums[1:2] = b.sum(0, keepdims=True)


def first_grad_kernel(count, where, stats, clip, near, after, mine, other, order0, order1, grad, sums, full):
    core = where[1]
    for x in range(4):
        full[pl.ds(pl.multiple_of((2 * x + core) * SHARD, UNIT), SHARD)] = mine[x]
        full[pl.ds(pl.multiple_of((2 * x + 1 - core) * SHARD, UNIT), SHARD)] = other[x]
    views = (
        lambda kw, rows: near[kw, 0, rows],
        lambda kw, rows: near[kw, 1, rows],
        lambda kw, rows: after[kw, 0, rows],
    )
    frame_grad(count, 0, stats, clip, views, full, grad, sums)


def second_grad_kernel(count, stats, clip, near, after, later, full, order, grad, sums):
    views = (
        lambda kw, rows: near[kw, 1, rows],
        lambda kw, rows: after[kw, 0, rows],
        lambda kw, rows: later[kw, 0, rows],
    )
    frame_grad(count, 1, stats, clip, views, full, grad, sums)


def final_kernel(count, stats, sums, clip, cot, grad0, grad1, out):
    center, inverse = center_inverse(stats[...], count)
    means = group_total(sums[...]) / count
    total, cross = means[0:1], means[1:2]
    for frame, grad in enumerate((grad0, grad1)):

        @pl.loop(0, ROWS // 64)
        def _(i, frame=frame, grad=grad):
            at = pl.ds(pl.multiple_of(i * 64, 64), 64)
            v = (clip[frame, at].astype(f32) - center) * inverse
            g = cot[frame, at].astype(f32) + inverse * (grad[at] - total - v * cross)
            out[frame, at] = g.astype(bf16)


STEPS = (1, 3, 2)


def split_core_kernel(where, keep, got, order, held, *out):
    z = where[3]

    def add(x, quarter):
        at = pl.ds(pl.multiple_of(x * SHARD_PAD + quarter * QUARTER, UNIT), QUARTER)
        return keep[at] + got[at].astype(f32)

    for x in range(2):
        held[x] = add(x, z)
        for step, to in zip(STEPS, out):
            to[x] = add(x, (z + step) & 3).astype(bf16)


def ring_add(own, arrived, at):
    return (own[at].astype(f32) + arrived[2][at].astype(f32)) + (arrived[0][at].astype(f32) + arrived[1][at].astype(f32))


def split_z_kernel(where, low, l0, l1, l2, up, u0, u1, u2, order, held, *out):
    x_own = where[2]

    def total(x, use):
        @pl.when(x < 2)
        def _():
            use(ring_add(low, (l0, l1, l2), x & 1))

        @pl.when(x >= 2)
        def _():
            use(ring_add(up, (u0, u1, u2), x & 1))

    def hold(value):
        held[...] = value

    total(x_own, hold)
    for step, to in zip(STEPS, out):

        def give(value, to=to):
            to[...] = value.astype(bf16)

        total((x_own + step) & 3, give)


def write_sums(sums, rows, out):
    rows[...] = jnp.zeros((16, C), f32)
    rest = sums
    for k in range(3):
        term = rest.astype(bf16).astype(f32)
        rest = rest - term
        rows[2 * k : 2 * k + 2] = term
    out[QUARTER:] = rows[...].astype(bf16)


def read_sums(block):
    wide = block[QUARTER:].astype(f32)
    return wide[0:2] + wide[2:4] + wide[4:6]


def ring_sums(own, arrived):
    return (read_sums(own) + read_sums(arrived[2])) + (read_sums(arrived[0]) + read_sums(arrived[1]))


def split_x_kernel(held, a0, a1, a2, sums0, sums1, out, rows):
    out[:QUARTER] = ring_add(held, (a0, a1, a2), slice(None)).astype(bf16)
    write_sums(sums0[...] + sums1[...], rows, out)


def reduced_kernel(own, a0, a1, a2, out, rows):
    out[:QUARTER] = ring_add(own, (a0, a1, a2), slice(0, QUARTER)).astype(bf16)
    write_sums(ring_sums(own, (a0, a1, a2)), rows, out)


def finish_kernel(where, own, a0, a1, a2, grad_weight, sums, full):
    z = where[3]
    for block, distance in ((own, 0), (a0, 3), (a1, 1), (a2, 2)):
        at = pl.ds(pl.multiple_of(((z + distance) & 3) * QUARTER, UNIT), QUARTER)
        full[at] = block[:QUARTER].astype(f32)
    grad_weight[...] = full[:SHARD]
    sums[...] = ring_sums(own, (a0, a1, a2))


def call(kernel, out_shape, args, scratch=(), flops=0, bytes_accessed=1_000_000, scalars=0, order=()):
    specs = [pl.BlockSpec(memory_space=pltpu.SMEM)] * scalars
    specs += [pl.BlockSpec(memory_space=pltpu.VMEM)] * (len(args) - scalars)
    specs += [pl.BlockSpec(memory_space=pl.ANY)] * len(order)
    return pl.pallas_call(
        kernel,
        out_shape=out_shape,
        in_specs=specs,
        out_specs=jax.tree.map(lambda _: pl.BlockSpec(memory_space=pltpu.VMEM), out_shape),
        scratch_shapes=list(scratch),
        compiler_params=pltpu.CompilerParams(vmem_limit_bytes=VMEM),
        cost_estimate=pl.CostEstimate(flops=flops, bytes_accessed=bytes_accessed, transcendentals=0),
    )(*args, *order)


AXES = {"z": ("tm", 16, 1), "y": ("tm", 16, 4), "x": ("fsdp", 8, 2)}


def ring(axis, blocks):
    name, size, stride = AXES[axis]
    got = []
    for block, distance in zip(blocks, STEPS):
        route = []
        for i in range(size):
            place = (i // stride) % 4
            route.append((i, i + ((place + distance) % 4 - place) * stride))
        got.append(lax.ppermute(block, name, route))
    return got


def swap_core(block):
    return lax.ppermute(block, "fsdp", [(i, i ^ 1) for i in range(8)])


def ring_sum(values, axis):
    return call(ring_sum_kernel, jax.ShapeDtypeStruct(values.shape, f32), (values, *ring(axis, [values] * 3)))


def passed(block, distance):
    route = [(i - distance, i) for i in range(16) if 0 <= i - distance < 16]
    return lax.ppermute(block, "tm", route)


def per_device(clip, cotangent, weights):
    shape = clip.shape
    clip = clip.reshape(2, ROWS, C)
    cot = cotangent.reshape(2, ROWS, C)
    count = 32 * ROWS * (C // GROUPS)
    scale = 1.0 / math.sqrt(8 * 32 * ROWS)
    partial = functools.partial
    S = jax.ShapeDtypeStruct
    tm = lax.axis_index("tm")
    fsdp = lax.axis_index("fsdp")
    where = [tm == 0, fsdp & 1, fsdp >> 1, tm & 3]
    where = jnp.stack([jnp.asarray(v, jnp.int32) for v in where])
    frame = S((ROWS, C), bf16)

    sums = call(stats_kernel, S((2, C), f32), (clip.reshape(2 * ROWS, C),))
    first, second, last = call(copy_kernel, (frame, frame, frame), (clip, cot), order=(sums,))
    sums = ring_sum(sums, "y")
    near = call(widths_kernel, S((3, 2, PADDED, C), bf16), (cot,), order=(sums,))
    stats = ring_sum(sums, "z")
    after = call(widths_kernel, S((3, 1, PADDED, C), bf16), (passed(first, -1)[None],))
    before = passed(last, 1)
    later = call(widths_kernel, S((3, 1, PADDED, C), bf16), (passed(second, -1)[None],))
    gathered = ring("x", [weights] * 3)

    rows = 2 * SHARD_PAD + UNIT
    half_flops = 27 * C * C * 2 * ROWS // 4
    act, keep_up, send_up = call(
        partial(upper_kernel, count, scale),
        (S((3, ROWS, C), bf16), S((rows, C), f32), S((rows, C), bf16)),
        (where, stats, clip, before, near, after),
        flops=half_flops,
        scalars=1,
    )
    got_up = swap_core(send_up)
    keep_low, send_low = call(
        partial(lower_kernel, scale),
        (S((rows, C), f32), S((rows, C), bf16)),
        (where, act, near, after),
        flops=half_flops,
        scalars=1,
        order=(send_up,),
    )
    got_low = swap_core(send_low)
    block = lambda *dims: (S(dims + (QUARTER, C), f32),) + (S(dims + (QUARTER, C), bf16),) * 3
    up, *out_up = call(split_core_kernel, block(2), (where, keep_up, got_up), scalars=1, order=(keep_low,))
    low, *out_low = call(split_core_kernel, block(2), (where, keep_low, got_low), scalars=1, order=(up,))
    arrived_up = ring("z", out_up)
    mine = call(pack_kernel, S((4, SHARD, C), bf16), (where, weights, *gathered), scalars=1, order=(arrived_up[0],))
    other = swap_core(mine)
    grad0, sums0, full = call(
        partial(first_grad_kernel, count),
        (S((ROWS, C), f32), S((2, C), f32), S((8 * SHARD, C), bf16)),
        (where, stats, clip, near, after, mine, other),
        flops=half_flops,
        scalars=1,
        order=(later, low),
    )
    grad1, sums1 = call(
        partial(second_grad_kernel, count),
        (S((ROWS, C), f32), S((2, C), f32)),
        (stats, clip, near, after, later, full),
        flops=half_flops,
        order=(sums0,),
    )
    got = (low, *ring("z", out_low), up, *arrived_up)
    held, *out = call(split_z_kernel, block(), (where, *got), scalars=1, order=(sums1,))
    rows16 = [pltpu.VMEM((16, C), f32)]
    message = S((QUARTER + 16, C), bf16)
    own = call(split_x_kernel, message, (held, *ring("x", out), sums0, sums1), rows16)
    own = call(reduced_kernel, message, (own, *ring("y", [own] * 3)), rows16)
    grad_weight, sums = call(
        finish_kernel,
        (S((SHARD, C), f32), S((2, C), f32)),
        (where, own, *ring("z", [own] * 3)),
        [pltpu.VMEM((SHARD_PAD, C), f32)],
        scalars=1,
    )
    grad_input = call(
        partial(final_kernel, count), S((2, ROWS, C), bf16), (stats, sums, clip, cot, grad0, grad1)
    )
    return grad_input.reshape(shape), grad_weight


def solution(mesh):
    in_specs = (
        P("fsdp", "tm", None, None, None),
        P("fsdp", "tm", None, None, None),
        P("fsdp", None),
    )
    out_specs = (P("fsdp", "tm", None, None, None), P("fsdp", None))
    return jax.shard_map(
        per_device, mesh=mesh, in_specs=in_specs, out_specs=out_specs, check_vma=False
    )
```

```python
import functools
import math

import jax
import jax.numpy as jnp
from jax import lax
from jax.experimental import pallas as pl
from jax.experimental.pallas import tpu as pltpu
from jax.sharding import PartitionSpec as P

GROUPS = 32
C = 256
H = 16
W = 64
ROWS = H * W
PADDED = ROWS + 2 * W
HALF = C // 2
SHARD = 864
SHARD_PAD = 896
QUARTER = 224
UNIT = 32
VMEM = 20 * 1024 * 1024
epsilon = 1e-06
f32 = jnp.float32
bf16 = jnp.bfloat16


def group_total(rows):
    lane = lax.broadcasted_iota(jnp.int32, rows.shape, 1)
    for s in (1, 2, 4):
        up = pltpu.roll(rows, s, 1)
        down = pltpu.roll(rows, C - s, 1)
        rows = rows + jnp.where((lane & s) != 0, up, down)
    return rows


def center_inverse(stats, count):
    sums = group_total(stats) / count
    center = sums[0:1]
    spread = sums[1:2] - center * center
    return center, lax.rsqrt(spread + epsilon)


def sigmoid(v):
    return 1.0 / (1.0 + jnp.exp(-v))


def widths(target, cot, slot):
    zero = jnp.zeros((W, C), bf16)
    for kw in range(3):
        target[kw, slot, 0:W] = zero
        target[kw, slot, W + ROWS : PADDED] = zero
    column = lax.broadcasted_iota(jnp.int32, (W, C), 0)

    @pl.loop(0, H)
    def _(h):
        row = cot(pl.multiple_of(h * W, W))
        at = pl.ds(pl.multiple_of(h * W + W, W), W)
        wide = row.astype(f32)
        target[1, slot, at] = row
        target[0, slot, at] = jnp.where(column == W - 1, 0.0, pltpu.roll(wide, W - 1, 0)).astype(bf16)
        target[2, slot, at] = jnp.where(column == 0, 0.0, pltpu.roll(wide, 1, 0)).astype(bf16)


def stats_kernel(clip, out):
    def step(i, carry):
        a, b = carry
        v = clip[pl.ds(pl.multiple_of(i * 128, 128), 128)].astype(f32)
        v = v.reshape(16, 8, C)
        return a + v.sum(0), b + (v * v).sum(0)

    zero = jnp.zeros((8, C), f32)
    a, b = lax.fori_loop(0, clip.shape[0] // 128, step, (zero, zero))
    out[0:1] = a.sum(0, keepdims=True)
    out[1:2] = b.sum(0, keepdims=True)


def copy_kernel(clip, cot, order, first, second, last):
    first[...] = cot[0]
    second[...] = cot[1]
    last[...] = clip[1]


def widths_kernel(cot, *refs):
    wide = refs[-1]
    for t in range(cot.shape[0]):
        widths(wide, lambda r, t=t: cot[t, pl.ds(r, W)], t)


def ring_sum_kernel(own, before, after, far, out):
    out[...] = (own[...] + far[...]) + (before[...] + after[...])


def tap_rows(kh):
    return pl.ds(pl.multiple_of((2 - kh) * W, W), ROWS)


CONTRACT_ROWS = (((0,), (0,)), ((), ()))
CONTRACT_COLUMNS = (((1,), (1,)), ((), ()))


def tap_product(frames, views, channels):
    total = None
    for frame, view in zip(frames, views):
        part = lax.dot_general(frame[:, channels], view, CONTRACT_ROWS, preferred_element_type=f32)
        total = part if total is None else total + part
    return total


def store_tap(tap, total, first_unit, core, keep, send):
    spare = 2 * SHARD_PAD
    for u in range(total.shape[0] // UNIT):
        unit = tap * (C // UNIT) + first_unit + u
        shard = (unit * 1214) >> 15
        dest = ((shard >> 1) & 1) * SHARD_PAD + (unit - shard * (SHARD // UNIT)) * UNIT
        mine = (shard & 1) == core
        piece = total[u * UNIT : (u + 1) * UNIT]
        keep[pl.ds(pl.multiple_of(jnp.where(mine, dest, spare), UNIT), UNIT)] = piece
        send[pl.ds(pl.multiple_of(jnp.where(mine, spare, dest), UNIT), UNIT)] = piece.astype(bf16)


def clear_tails(keep, send):
    for place in range(2):
        tail = slice(place * SHARD_PAD + SHARD, (place + 1) * SHARD_PAD)
        keep[tail] = jnp.zeros((SHARD_PAD - SHARD, C), f32)
        send[tail] = jnp.zeros((SHARD_PAD - SHARD, C), bf16)
    keep[2 * SHARD_PAD :] = jnp.zeros((UNIT, C), f32)
    send[2 * SHARD_PAD :] = jnp.zeros((UNIT, C), bf16)


def middle_taps(low, high, channels, scale, core, act, near, after, keep, send):
    for tap in range(low, high):
        kh, kw = tap // 3 % 3, tap % 3
        rows = slice((2 - kh) * W, (2 - kh) * W + ROWS)
        total = tap_product((act[0], act[1]), (near[kw, 1, rows], after[kw, 0, rows]), channels)
        store_tap(tap, total * scale, channels.start // UNIT, core, keep, send)


def activate(center, inverse, frame, act, gain=None):
    @pl.loop(0, ROWS // 64)
    def _(i):
        at = pl.ds(pl.multiple_of(i * 64, 64), 64)
        v = (frame(at).astype(f32) - center) * inverse
        v = v * sigmoid(v)
        if gain is not None:
            v = v * gain
        act[at] = v.astype(bf16)


def near_kernel(count, scale, where, stats, clip, near, act, keep, send):
    center, inverse = center_inverse(stats[...], count)
    for t in range(2):
        activate(center, inverse, lambda at, t=t: clip[t, at], act.at[t])

    @pl.loop(0, 3)
    def _(kh):
        rows = tap_rows(kh)
        for kw in range(3):
            total = tap_product((act[0], act[1]), (near[kw, 0, rows], near[kw, 1, rows]), slice(None))
            store_tap(18 + kh * 3 + kw, total * scale, 0, where[1], keep, send)

    clear_tails(keep, send)


def upper_kernel(scale, where, act, near, after, keep_in, send_in, order, keep, send):
    middle_taps(14, 18, slice(0, C), scale, where[1], act, near, after, keep, send)
    middle_taps(13, 14, slice(HALF, C), scale, where[1], act, near, after, keep, send)


def lower_kernel(count, scale, where, stats, act, before, near, after, order, keep, send, act_before):
    core = where[1]
    center, inverse = center_inverse(stats[...], count)
    gain = jnp.where(where[0] == 1, 0.0, 1.0)
    activate(center, inverse, lambda at: before[at], act_before, gain)

    @pl.loop(0, 3)
    def _(kh):
        rows = tap_rows(kh)
        for kw in range(3):
            total = tap_product((act_before, act[0]), (near[kw, 1, rows], after[kw, 0, rows]), slice(None))
            store_tap(kh * 3 + kw, total * scale, 0, core, keep, send)

    middle_taps(9, 13, slice(0, C), scale, core, act, near, after, keep, send)
    middle_taps(13, 14, slice(0, HALF), scale, core, act, near, after, keep, send)
    clear_tails(keep, send)


def pack_kernel(where, own, left, right, far, order, packed):
    x = where[2]
    for block, distance in ((own, 0), (left, 3), (right, 1), (far, 2)):
        packed[(x + distance) % 4] = block[...]


def frame_grad(count, frame, stats, clip, views, weights, grad, sums):
    center, inverse = center_inverse(stats[...], count)
    rows_per = 256

    @pl.loop(0, ROWS // rows_per)
    def _(i):
        start = i * rows_per
        total = jnp.zeros((rows_per, C), f32)
        for tap in range(27):
            kt, kh, kw = tap // 9, tap // 3 % 3, tap % 3
            rows = pl.ds(pl.multiple_of((2 - kh) * W + start, W), rows_per)
            w = weights[tap * C : (tap + 1) * C]
            total += lax.dot_general(
                views[2 - kt](kw, rows), w, CONTRACT_COLUMNS, preferred_element_type=f32
            )
        grad[pl.ds(pl.multiple_of(start, rows_per), rows_per)] = total

    zero = jnp.zeros((8, C), f32)

    def finish(i, carry):
        a, b = carry
        at = pl.ds(pl.multiple_of(i * 64, 64), 64)
        v = (clip[frame, at].astype(f32) - center) * inverse
        s = sigmoid(v)
        g = grad[at] * (s * (1.0 + v * (1.0 - s)))
        grad[at] = g
        return a + g.reshape(8, 8, C).sum(0), b + (g * v).reshape(8, 8, C).sum(0)

    a, b = lax.fori_loop(0, ROWS // 64, finish, (zero, zero))
    sums[0:1] = a.sum(0, keepdims=True)
    sums[1:2] = b.sum(0, keepdims=True)


def first_grad_kernel(count, where, stats, clip, near, after, mine, other, order, grad, sums, full):
    core = where[1]
    for x in range(4):
        full[pl.ds(pl.multiple_of((2 * x + core) * SHARD, UNIT), SHARD)] = mine[x]
        full[pl.ds(pl.multiple_of((2 * x + 1 - core) * SHARD, UNIT), SHARD)] = other[x]
    views = (
        lambda kw, rows: near[kw, 0, rows],
        lambda kw, rows: near[kw, 1, rows],
        lambda kw, rows: after[kw, 0, rows],
    )
    frame_grad(count, 0, stats, clip, views, full, grad, sums)


def second_grad_kernel(count, stats, clip, near, after, later, full, order, grad, sums):
    views = (
        lambda kw, rows: near[kw, 1, rows],
        lambda kw, rows: after[kw, 0, rows],
        lambda kw, rows: later[kw, 0, rows],
    )
    frame_grad(count, 1, stats, clip, views, full, grad, sums)


def final_kernel(count, stats, sums, clip, cot, grad0, grad1, out):
    center, inverse = center_inverse(stats[...], count)
    means = group_total(sums[...]) / count
    total, cross = means[0:1], means[1:2]
    for frame, grad in enumerate((grad0, grad1)):

        @pl.loop(0, ROWS // 64)
        def _(i, frame=frame, grad=grad):
            at = pl.ds(pl.multiple_of(i * 64, 64), 64)
            v = (clip[frame, at].astype(f32) - center) * inverse
            g = cot[frame, at].astype(f32) + inverse * (grad[at] - total - v * cross)
            out[frame, at] = g.astype(bf16)


STEPS = (1, 3, 2)


def split_core_kernel(where, keep, got, *refs):
    y = where[3]
    held, *out = refs[-4:]

    def add(x, quarter):
        at = pl.ds(pl.multiple_of(x * SHARD_PAD + quarter * QUARTER, UNIT), QUARTER)
        return keep[at] + got[at].astype(f32)

    for x in range(2):
        held[x] = add(x, y)
        for step, to in zip(STEPS, out):
            to[x] = add(x, (y + step) & 3).astype(bf16)


def ring_add(own, arrived, at):
    return (own[at].astype(f32) + arrived[2][at].astype(f32)) + (arrived[0][at].astype(f32) + arrived[1][at].astype(f32))


def split_y_kernel(where, low, l0, l1, l2, up, u0, u1, u2, order, held, *out):
    x_own = where[2]

    def total(x, use):
        @pl.when(x < 2)
        def _():
            use(ring_add(low, (l0, l1, l2), x & 1))

        @pl.when(x >= 2)
        def _():
            use(ring_add(up, (u0, u1, u2), x & 1))

    def hold(value):
        held[...] = value

    total(x_own, hold)
    for step, to in zip(STEPS, out):

        def give(value, to=to):
            to[...] = value.astype(bf16)

        total((x_own + step) & 3, give)


def write_sums(sums, rows, out):
    rows[...] = jnp.zeros((16, C), f32)
    rest = sums
    for k in range(3):
        term = rest.astype(bf16).astype(f32)
        rest = rest - term
        rows[2 * k : 2 * k + 2] = term
    out[QUARTER:] = rows[...].astype(bf16)


def read_sums(block):
    wide = block[QUARTER:].astype(f32)
    return wide[0:2] + wide[2:4] + wide[4:6]


def ring_sums(own, arrived):
    return (read_sums(own) + read_sums(arrived[2])) + (read_sums(arrived[0]) + read_sums(arrived[1]))


def split_x_kernel(held, a0, a1, a2, sums0, sums1, out, rows):
    out[:QUARTER] = ring_add(held, (a0, a1, a2), slice(None)).astype(bf16)
    write_sums(sums0[...] + sums1[...], rows, out)


def reduced_kernel(own, a0, a1, a2, out, rows):
    out[:QUARTER] = ring_add(own, (a0, a1, a2), slice(0, QUARTER)).astype(bf16)
    write_sums(ring_sums(own, (a0, a1, a2)), rows, out)


def finish_kernel(where, own, a0, a1, a2, grad_weight, sums, full):
    y = where[3]
    for block, distance in ((own, 0), (a0, 3), (a1, 1), (a2, 2)):
        at = pl.ds(pl.multiple_of(((y + distance) & 3) * QUARTER, UNIT), QUARTER)
        full[at] = block[:QUARTER].astype(f32)
    grad_weight[...] = full[:SHARD]
    sums[...] = ring_sums(own, (a0, a1, a2))


def call(kernel, out_shape, args, scratch=(), flops=0, bytes_accessed=0, scalars=0, order=(), aliases={}):
    specs = [pl.BlockSpec(memory_space=pltpu.SMEM)] * scalars
    specs += [pl.BlockSpec(memory_space=pltpu.VMEM)] * (len(args) - scalars)
    specs += [pl.BlockSpec(memory_space=pl.ANY)] * len(order)
    return pl.pallas_call(
        kernel,
        out_shape=out_shape,
        in_specs=specs,
        out_specs=jax.tree.map(lambda _: pl.BlockSpec(memory_space=pltpu.VMEM), out_shape),
        scratch_shapes=list(scratch),
        input_output_aliases=aliases,
        compiler_params=pltpu.CompilerParams(vmem_limit_bytes=VMEM),
        cost_estimate=pl.CostEstimate(flops=flops, bytes_accessed=bytes_accessed, transcendentals=0),
    )(*args, *order)


AXES = {"z": ("tm", 16, 1), "y": ("tm", 16, 4), "x": ("fsdp", 8, 2)}


def ring(axis, blocks):
    name, size, stride = AXES[axis]
    got = []
    for block, distance in zip(blocks, STEPS):
        route = []
        for i in range(size):
            place = (i // stride) % 4
            route.append((i, i + ((place + distance) % 4 - place) * stride))
        got.append(lax.ppermute(block, name, route))
    return got


def swap(block, axis, partners):
    name, size, stride = AXES[axis]
    route = []
    for i in range(size):
        place = (i // stride) % 4
        route.append((i, i + (partners[place] - place) * stride))
    return lax.ppermute(block, name, route)


def swap_core(block):
    return lax.ppermute(block, "fsdp", [(i, i ^ 1) for i in range(8)])


def ring_sum(values, got):
    return call(ring_sum_kernel, jax.ShapeDtypeStruct(values.shape, f32), (values, *got))


def passed(block, distance):
    route = [(i - distance, i) for i in range(16) if 0 <= i - distance < 16]
    return lax.ppermute(block, "tm", route)


def per_device(clip, cotangent, weights):
    shape = clip.shape
    clip = clip.reshape(2, ROWS, C)
    cot = cotangent.reshape(2, ROWS, C)
    count = 32 * ROWS * (C // GROUPS)
    scale = 1.0 / math.sqrt(8 * 32 * ROWS)
    partial = functools.partial
    S = jax.ShapeDtypeStruct
    tm = lax.axis_index("tm")
    fsdp = lax.axis_index("fsdp")
    where = [tm == 0, fsdp & 1, fsdp >> 1, tm >> 2]
    where = jnp.stack([jnp.asarray(v, jnp.int32) for v in where])
    frame = S((ROWS, C), bf16)

    sums = call(stats_kernel, S((2, C), f32), (clip.reshape(2 * ROWS, C),))
    sums = ring_sum(sums, ring("z", [sums] * 3))
    first, second, last = call(copy_kernel, (frame, frame, frame), (clip, cot), order=(sums,))
    near = call(widths_kernel, S((3, 2, PADDED, C), bf16), (cot,), order=(sums,))
    half = sums + swap(sums, "y", (1, 0, 3, 2))
    stats = half + swap(half, "y", (3, 2, 1, 0))
    after = call(widths_kernel, S((3, 1, PADDED, C), bf16), (passed(first, -1)[None],))
    before = passed(last, 1)
    later = call(widths_kernel, S((3, 1, PADDED, C), bf16), (passed(second, -1)[None],))

    rows = 2 * SHARD_PAD + UNIT
    tap_flops = C * C * 2 * ROWS * 2
    pieces = (S((rows, C), f32), S((rows, C), bf16))
    act, keep_up, send_up = call(
        partial(near_kernel, count, scale),
        (S((2, ROWS, C), bf16), *pieces),
        (where, stats, clip, near),
        flops=9 * tap_flops,
        scalars=1,
    )
    mine = call(pack_kernel, S((4, SHARD, C), bf16), (where, weights, *ring("x", [weights] * 3)), scalars=1, order=(act,))
    other = swap_core(mine)
    keep_up, send_up = call(
        partial(upper_kernel, scale),
        pieces,
        (where, act, near, after, keep_up, send_up),
        flops=9 * tap_flops // 2,
        scalars=1,
        order=(mine,),
        aliases={4: 0, 5: 1},
    )
    got_up = swap_core(send_up)
    keep_low, send_low = call(
        partial(lower_kernel, count, scale),
        pieces,
        (where, stats, act, before, near, after),
        [pltpu.VMEM((ROWS, C), bf16)],
        flops=27 * tap_flops // 2,
        scalars=1,
        order=(send_up,),
    )
    got_low = swap_core(send_low)

    block = lambda *dims: (S(dims + (QUARTER, C), f32),) + (S(dims + (QUARTER, C), bf16),) * 3
    up, *out_up = call(split_core_kernel, block(2), (where, keep_up, got_up), scalars=1, order=(keep_low,))
    low, *out_low = call(split_core_kernel, block(2), (where, keep_low, got_low), scalars=1, order=(up,))
    grad0, sums0, full = call(
        partial(first_grad_kernel, count),
        (S((ROWS, C), f32), S((2, C), f32), S((8 * SHARD, C), bf16)),
        (where, stats, clip, near, after, mine, other),
        flops=27 * tap_flops // 2,
        scalars=1,
        order=(low,),
    )
    grad1, sums1 = call(
        partial(second_grad_kernel, count),
        (S((ROWS, C), f32), S((2, C), f32)),
        (stats, clip, near, after, later, full),
        flops=27 * tap_flops // 2,
        order=(sums0,),
    )
    got = (low, *ring("y", out_low), up, *ring("y", out_up))
    held, *out = call(split_y_kernel, block(), (where, *got), scalars=1, order=(sums1,))
    rows16 = [pltpu.VMEM((16, C), f32)]
    message = S((QUARTER + 16, C), bf16)
    own = call(split_x_kernel, message, (held, *ring("x", out), sums0, sums1), rows16)
    own = call(reduced_kernel, message, (own, *ring("z", [own] * 3)), rows16)
    grad_weight, sums = call(
        finish_kernel,
        (S((SHARD, C), f32), S((2, C), f32)),
        (where, own, *ring("y", [own] * 3)),
        [pltpu.VMEM((SHARD_PAD, C), f32)],
        scalars=1,
    )
    grad_input = call(
        partial(final_kernel, count), S((2, ROWS, C), bf16), (stats, sums, clip, cot, grad0, grad1)
    )
    return grad_input.reshape(shape), grad_weight


def solution(mesh):
    in_specs = (
        P("fsdp", "tm", None, None, None),
        P("fsdp", "tm", None, None, None),
        P("fsdp", None),
    )
    out_specs = (P("fsdp", "tm", None, None, None), P("fsdp", None))
    return jax.shard_map(
        per_device, mesh=mesh, in_specs=in_specs, out_specs=out_specs, check_vma=False
    )
```

```python
import functools
import math

import jax
import jax.numpy as jnp
from jax import lax
from jax.experimental import pallas as pl
from jax.experimental.pallas import tpu as pltpu
from jax.sharding import PartitionSpec as P

GROUPS = 32
C = 256
H = 16
W = 64
ROWS = H * W
PADDED = ROWS + 2 * W
HALF = C // 2
SHARD = 864
SHARD_PAD = 896
QUARTER = 224
UNIT = 32
VMEM = 20 * 1024 * 1024
epsilon = 1e-06
f32 = jnp.float32
bf16 = jnp.bfloat16


def group_total(rows):
    lane = lax.broadcasted_iota(jnp.int32, rows.shape, 1)
    for s in (1, 2, 4):
        up = pltpu.roll(rows, s, 1)
        down = pltpu.roll(rows, C - s, 1)
        rows = rows + jnp.where((lane & s) != 0, up, down)
    return rows


def center_inverse(stats, count):
    sums = group_total(stats) / count
    center = sums[0:1]
    spread = sums[1:2] - center * center
    return center, lax.rsqrt(spread + epsilon)


def sigmoid(v):
    return 1.0 / (1.0 + jnp.exp(-v))


def widths(target, cot, slot):
    zero = jnp.zeros((W, C), bf16)
    for kw in range(3):
        target[kw, slot, 0:W] = zero
        target[kw, slot, W + ROWS : PADDED] = zero
    column = lax.broadcasted_iota(jnp.int32, (W, C), 0)

    @pl.loop(0, H)
    def _(h):
        row = cot(pl.multiple_of(h * W, W))
        at = pl.ds(pl.multiple_of(h * W + W, W), W)
        wide = row.astype(f32)
        target[1, slot, at] = row
        target[0, slot, at] = jnp.where(column == W - 1, 0.0, pltpu.roll(wide, W - 1, 0)).astype(bf16)
        target[2, slot, at] = jnp.where(column == 0, 0.0, pltpu.roll(wide, 1, 0)).astype(bf16)


def first_kernel(clip, cot, out, first, second, last):
    def step(i, carry):
        a, b = carry
        at = pl.ds(pl.multiple_of((i & 7) * 128, 128), 128)
        v = clip[i >> 3, at].astype(f32).reshape(16, 8, C)
        return a + v.sum(0), b + (v * v).sum(0)

    zero = jnp.zeros((8, C), f32)
    a, b = lax.fori_loop(0, 2 * ROWS // 128, step, (zero, zero))
    out[0:1] = a.sum(0, keepdims=True)
    out[1:2] = b.sum(0, keepdims=True)
    first[...] = cot[0]
    second[...] = cot[1]
    last[...] = clip[1]


def widths_kernel(cot, *refs):
    wide = refs[-1]
    for t in range(cot.shape[0]):
        widths(wide, lambda r, t=t: cot[t, pl.ds(r, W)], t)


def ring_sum_kernel(own, before, after, far, held0, held1, out, pass0, pass1):
    out[...] = (own[...] + far[...]) + (before[...] + after[...])


def tap_rows(kh):
    return pl.ds(pl.multiple_of((2 - kh) * W, W), ROWS)


CONTRACT_ROWS = (((0,), (0,)), ((), ()))
CONTRACT_COLUMNS = (((1,), (1,)), ((), ()))


def tap_product(frames, views, channels):
    total = None
    for frame, view in zip(frames, views):
        part = lax.dot_general(frame[:, channels], view, CONTRACT_ROWS, preferred_element_type=f32)
        total = part if total is None else total + part
    return total


def store_tap(tap, total, first_unit, core, keep, send):
    spare = 2 * SHARD_PAD
    for u in range(total.shape[0] // UNIT):
        unit = tap * (C // UNIT) + first_unit + u
        shard = (unit * 1214) >> 15
        dest = ((shard >> 1) & 1) * SHARD_PAD + (unit - shard * (SHARD // UNIT)) * UNIT
        mine = (shard & 1) == core
        piece = total[u * UNIT : (u + 1) * UNIT]
        keep[pl.ds(pl.multiple_of(jnp.where(mine, dest, spare), UNIT), UNIT)] = piece
        send[pl.ds(pl.multiple_of(jnp.where(mine, spare, dest), UNIT), UNIT)] = piece.astype(bf16)


def clear_tails(keep, send):
    for place in range(2):
        tail = slice(place * SHARD_PAD + SHARD, (place + 1) * SHARD_PAD)
        keep[tail] = jnp.zeros((SHARD_PAD - SHARD, C), f32)
        send[tail] = jnp.zeros((SHARD_PAD - SHARD, C), bf16)
    keep[2 * SHARD_PAD :] = jnp.zeros((UNIT, C), f32)
    send[2 * SHARD_PAD :] = jnp.zeros((UNIT, C), bf16)


def middle_taps(low, high, channels, scale, core, act, near, after, keep, send):
    for tap in range(low, high):
        kh, kw = tap // 3 % 3, tap % 3
        rows = slice((2 - kh) * W, (2 - kh) * W + ROWS)
        total = tap_product((act[0], act[1]), (near[kw, 1, rows], after[kw, 0, rows]), channels)
        store_tap(tap, total * scale, channels.start // UNIT, core, keep, send)


def activate(center, inverse, frame, act, gain=None):
    @pl.loop(0, ROWS // 64)
    def _(i):
        at = pl.ds(pl.multiple_of(i * 64, 64), 64)
        v = (frame(at).astype(f32) - center) * inverse
        v = v * sigmoid(v)
        if gain is not None:
            v = v * gain
        act[at] = v.astype(bf16)


def near_kernel(count, scale, where, stats, clip, near, act, keep, send):
    center, inverse = center_inverse(stats[...], count)
    for t in range(2):
        activate(center, inverse, lambda at, t=t: clip[t, at], act.at[t])

    @pl.loop(0, 3)
    def _(kh):
        rows = tap_rows(kh)
        for kw in range(3):
            total = tap_product((act[0], act[1]), (near[kw, 0, rows], near[kw, 1, rows]), slice(None))
            store_tap(18 + kh * 3 + kw, total * scale, 0, where[1], keep, send)

    clear_tails(keep, send)


def upper_kernel(scale, where, act, near, after, keep_in, send_in, order, keep, send):
    middle_taps(14, 18, slice(0, C), scale, where[1], act, near, after, keep, send)
    middle_taps(13, 14, slice(HALF, C), scale, where[1], act, near, after, keep, send)


def lower_kernel(count, scale, where, stats, act, before, near, after, order, keep, send, act_before):
    core = where[1]
    center, inverse = center_inverse(stats[...], count)
    gain = jnp.where(where[0] == 1, 0.0, 1.0)
    activate(center, inverse, lambda at: before[at], act_before, gain)

    @pl.loop(0, 3)
    def _(kh):
        rows = tap_rows(kh)
        for kw in range(3):
            total = tap_product((act_before, act[0]), (near[kw, 1, rows], after[kw, 0, rows]), slice(None))
            store_tap(kh * 3 + kw, total * scale, 0, core, keep, send)

    middle_taps(9, 13, slice(0, C), scale, core, act, near, after, keep, send)
    middle_taps(13, 14, slice(0, HALF), scale, core, act, near, after, keep, send)
    clear_tails(keep, send)


def pack_kernel(where, own, left, right, far, order, packed):
    x = where[2]
    for block, distance in ((own, 0), (left, 3), (right, 1), (far, 2)):
        packed[(x + distance) % 4] = block[...]


def frame_grad(count, frame, stats, clip, views, weights, grad, sums):
    center, inverse = center_inverse(stats[...], count)
    rows_per = 256

    @pl.loop(0, ROWS // rows_per)
    def _(i):
        start = i * rows_per
        total = jnp.zeros((rows_per, C), f32)
        for tap in range(27):
            kt, kh, kw = tap // 9, tap // 3 % 3, tap % 3
            rows = pl.ds(pl.multiple_of((2 - kh) * W + start, W), rows_per)
            w = weights[tap * C : (tap + 1) * C]
            total += lax.dot_general(
                views[2 - kt](kw, rows), w, CONTRACT_COLUMNS, preferred_element_type=f32
            )
        grad[pl.ds(pl.multiple_of(start, rows_per), rows_per)] = total

    zero = jnp.zeros((8, C), f32)

    def finish(i, carry):
        a, b = carry
        at = pl.ds(pl.multiple_of(i * 64, 64), 64)
        v = (clip[frame, at].astype(f32) - center) * inverse
        s = sigmoid(v)
        g = grad[at] * (s * (1.0 + v * (1.0 - s)))
        grad[at] = g
        return a + g.reshape(8, 8, C).sum(0), b + (g * v).reshape(8, 8, C).sum(0)

    a, b = lax.fori_loop(0, ROWS // 64, finish, (zero, zero))
    sums[0:1] = a.sum(0, keepdims=True)
    sums[1:2] = b.sum(0, keepdims=True)


def first_grad_kernel(count, where, stats, clip, near, after, mine, other, order, grad, sums, full):
    core = where[1]
    for x in range(4):
        full[pl.ds(pl.multiple_of((2 * x + core) * SHARD, UNIT), SHARD)] = mine[x]
        full[pl.ds(pl.multiple_of((2 * x + 1 - core) * SHARD, UNIT), SHARD)] = other[x]
    views = (
        lambda kw, rows: near[kw, 0, rows],
        lambda kw, rows: near[kw, 1, rows],
        lambda kw, rows: after[kw, 0, rows],
    )
    frame_grad(count, 0, stats, clip, views, full, grad, sums)


def second_grad_kernel(count, stats, clip, near, after, later, full, order, grad, sums):
    views = (
        lambda kw, rows: near[kw, 1, rows],
        lambda kw, rows: after[kw, 0, rows],
        lambda kw, rows: later[kw, 0, rows],
    )
    frame_grad(count, 1, stats, clip, views, full, grad, sums)


def final_kernel(count, stats, sums, clip, cot, grad0, grad1, out):
    center, inverse = center_inverse(stats[...], count)
    means = group_total(sums[...]) / count
    total, cross = means[0:1], means[1:2]
    for frame, grad in enumerate((grad0, grad1)):

        @pl.loop(0, ROWS // 64)
        def _(i, frame=frame, grad=grad):
            at = pl.ds(pl.multiple_of(i * 64, 64), 64)
            v = (clip[frame, at].astype(f32) - center) * inverse
            g = cot[frame, at].astype(f32) + inverse * (grad[at] - total - v * cross)
            out[frame, at] = g.astype(bf16)


STEPS = (1, 3, 2)


def split_core_kernel(where, keep, got, *refs):
    y = where[3]
    held, *out = refs[-4:]

    def add(x, quarter):
        at = pl.ds(pl.multiple_of(x * SHARD_PAD + quarter * QUARTER, UNIT), QUARTER)
        return keep[at] + got[at].astype(f32)

    for x in range(2):
        held[x] = add(x, y)
        for step, to in zip(STEPS, out):
            to[x] = add(x, (y + step) & 3).astype(bf16)


def ring_add(own, arrived, at):
    return (own[at].astype(f32) + arrived[2][at].astype(f32)) + (arrived[0][at].astype(f32) + arrived[1][at].astype(f32))


def split_y_kernel(where, low, l0, l1, l2, up, u0, u1, u2, order, held, *out):
    x_own = where[2]

    def total(x, use):
        @pl.when(x < 2)
        def _():
            use(ring_add(low, (l0, l1, l2), x & 1))

        @pl.when(x >= 2)
        def _():
            use(ring_add(up, (u0, u1, u2), x & 1))

    def hold(value):
        held[...] = value

    total(x_own, hold)
    for step, to in zip(STEPS, out):

        def give(value, to=to):
            to[...] = value.astype(bf16)

        total((x_own + step) & 3, give)


def write_sums(sums, rows, out):
    rows[...] = jnp.zeros((16, C), f32)
    rest = sums
    for k in range(3):
        term = rest.astype(bf16).astype(f32)
        rest = rest - term
        rows[2 * k : 2 * k + 2] = term
    out[QUARTER:] = rows[...].astype(bf16)


def read_sums(block):
    wide = block[QUARTER:].astype(f32)
    return wide[0:2] + wide[2:4] + wide[4:6]


def ring_sums(own, arrived):
    return (read_sums(own) + read_sums(arrived[2])) + (read_sums(arrived[0]) + read_sums(arrived[1]))


def split_x_kernel(held, a0, a1, a2, sums0, sums1, out, rows):
    out[:QUARTER] = ring_add(held, (a0, a1, a2), slice(None)).astype(bf16)
    write_sums(sums0[...] + sums1[...], rows, out)


def reduced_kernel(own, a0, a1, a2, out, rows):
    out[:QUARTER] = ring_add(own, (a0, a1, a2), slice(0, QUARTER)).astype(bf16)
    write_sums(ring_sums(own, (a0, a1, a2)), rows, out)


def finish_kernel(where, own, a0, a1, a2, grad_weight, sums, full):
    y = where[3]
    for block, distance in ((own, 0), (a0, 3), (a1, 1), (a2, 2)):
        at = pl.ds(pl.multiple_of(((y + distance) & 3) * QUARTER, UNIT), QUARTER)
        full[at] = block[:QUARTER].astype(f32)
    grad_weight[...] = full[:SHARD]
    sums[...] = ring_sums(own, (a0, a1, a2))


def call(kernel, out_shape, args, scratch=(), flops=0, bytes_accessed=0, scalars=0, order=(), aliases={}, passed_out=0):
    specs = [pl.BlockSpec(memory_space=pltpu.SMEM)] * scalars
    specs += [pl.BlockSpec(memory_space=pltpu.VMEM)] * (len(args) - scalars)
    specs += [pl.BlockSpec(memory_space=pl.ANY)] * len(order)
    out_specs = jax.tree.map(lambda _: pl.BlockSpec(memory_space=pltpu.VMEM), out_shape)
    if passed_out:
        out_specs = out_specs[:-passed_out] + (pl.BlockSpec(memory_space=pl.ANY),) * passed_out
    return pl.pallas_call(
        kernel,
        out_shape=out_shape,
        in_specs=specs,
        out_specs=out_specs,
        scratch_shapes=list(scratch),
        input_output_aliases=aliases,
        compiler_params=pltpu.CompilerParams(vmem_limit_bytes=VMEM),
        cost_estimate=pl.CostEstimate(flops=flops, bytes_accessed=bytes_accessed, transcendentals=0),
    )(*args, *order)


AXES = {"z": ("tm", 16, 1), "y": ("tm", 16, 4), "x": ("fsdp", 8, 2)}


def ring(axis, blocks):
    name, size, stride = AXES[axis]
    got = []
    for block, distance in zip(blocks, STEPS):
        route = []
        for i in range(size):
            place = (i // stride) % 4
            route.append((i, i + ((place + distance) % 4 - place) * stride))
        got.append(lax.ppermute(block, name, route))
    return got


def swap(block, axis, partners):
    name, size, stride = AXES[axis]
    route = []
    for i in range(size):
        place = (i // stride) % 4
        route.append((i, i + (partners[place] - place) * stride))
    return lax.ppermute(block, name, route)


def swap_core(block):
    return lax.ppermute(block, "fsdp", [(i, i ^ 1) for i in range(8)])


def passed(block, distance):
    route = [(i - distance, i) for i in range(16) if 0 <= i - distance < 16]
    return lax.ppermute(block, "tm", route)


def per_device(clip, cotangent, weights):
    shape = clip.shape
    clip = clip.reshape(2, ROWS, C)
    cot = cotangent.reshape(2, ROWS, C)
    count = 32 * ROWS * (C // GROUPS)
    scale = 1.0 / math.sqrt(8 * 32 * ROWS)
    partial = functools.partial
    S = jax.ShapeDtypeStruct
    tm = lax.axis_index("tm")
    fsdp = lax.axis_index("fsdp")
    where = [tm == 0, fsdp & 1, fsdp >> 1, tm >> 2]
    where = jnp.stack([jnp.asarray(v, jnp.int32) for v in where])
    frame = S((ROWS, C), bf16)

    sums, first, second, last = call(first_kernel, (S((2, C), f32), frame, frame, frame), (clip, cot))
    got = ring("z", [sums] * 3)
    sums, first, last = call(
        ring_sum_kernel,
        (S((2, C), f32), frame, frame),
        (sums, *got),
        order=(first, last),
        aliases={4: 1, 5: 2},
        passed_out=2,
    )
    near = call(widths_kernel, S((3, 2, PADDED, C), bf16), (cot,), order=(sums,))
    half = sums + swap(sums, "y", (1, 0, 3, 2))
    stats = half + swap(half, "y", (3, 2, 1, 0))
    after = call(widths_kernel, S((3, 1, PADDED, C), bf16), (passed(first, -1)[None],))
    before = passed(last, 1)
    later = passed(second, -1)[None]

    rows = 2 * SHARD_PAD + UNIT
    tap_flops = C * C * 2 * ROWS * 2
    pieces = (S((rows, C), f32), S((rows, C), bf16))
    act, keep_up, send_up = call(
        partial(near_kernel, count, scale),
        (S((2, ROWS, C), bf16), *pieces),
        (where, stats, clip, near),
        flops=9 * tap_flops,
        scalars=1,
    )
    mine = call(pack_kernel, S((4, SHARD, C), bf16), (where, weights, *ring("x", [weights] * 3)), scalars=1, order=(act,))
    other = swap_core(mine)
    keep_up, send_up = call(
        partial(upper_kernel, scale),
        pieces,
        (where, act, near, after, keep_up, send_up),
        flops=9 * tap_flops // 2,
        scalars=1,
        order=(mine,),
        aliases={4: 0, 5: 1},
    )
    got_up = swap_core(send_up)
    keep_low, send_low = call(
        partial(lower_kernel, count, scale),
        pieces,
        (where, stats, act, before, near, after),
        [pltpu.VMEM((ROWS, C), bf16)],
        flops=27 * tap_flops // 2,
        scalars=1,
        order=(send_up,),
    )
    got_low = swap_core(send_low)

    block = lambda *dims: (S(dims + (QUARTER, C), f32),) + (S(dims + (QUARTER, C), bf16),) * 3
    up, *out_up = call(split_core_kernel, block(2), (where, keep_up, got_up), scalars=1, order=(keep_low,))
    low, *out_low = call(split_core_kernel, block(2), (where, keep_low, got_low), scalars=1, order=(up,))
    grad0, sums0, full = call(
        partial(first_grad_kernel, count),
        (S((ROWS, C), f32), S((2, C), f32), S((8 * SHARD, C), bf16)),
        (where, stats, clip, near, after, mine, other),
        flops=27 * tap_flops // 2,
        scalars=1,
        order=(low,),
    )
    later = call(widths_kernel, S((3, 1, PADDED, C), bf16), (later,), order=(sums0,))
    grad1, sums1 = call(
        partial(second_grad_kernel, count),
        (S((ROWS, C), f32), S((2, C), f32)),
        (stats, clip, near, after, later, full),
        flops=27 * tap_flops // 2,
        order=(sums0,),
    )
    got = (low, *ring("y", out_low), up, *ring("y", out_up))
    held, *out = call(split_y_kernel, block(), (where, *got), scalars=1, order=(sums1,))
    rows16 = [pltpu.VMEM((16, C), f32)]
    message = S((QUARTER + 16, C), bf16)
    own = call(split_x_kernel, message, (held, *ring("x", out), sums0, sums1), rows16)
    own = call(reduced_kernel, message, (own, *ring("z", [own] * 3)), rows16)
    grad_weight, sums = call(
        finish_kernel,
        (S((SHARD, C), f32), S((2, C), f32)),
        (where, own, *ring("y", [own] * 3)),
        [pltpu.VMEM((SHARD_PAD, C), f32)],
        scalars=1,
    )
    grad_input = call(
        partial(final_kernel, count), S((2, ROWS, C), bf16), (stats, sums, clip, cot, grad0, grad1)
    )
    return grad_input.reshape(shape), grad_weight


def solution(mesh):
    in_specs = (
        P("fsdp", "tm", None, None, None),
        P("fsdp", "tm", None, None, None),
        P("fsdp", None),
    )
    out_specs = (P("fsdp", "tm", None, None, None), P("fsdp", None))
    return jax.shard_map(
        per_device, mesh=mesh, in_specs=in_specs, out_specs=out_specs, check_vma=False
    )
```

```python
import functools
import math

import jax
import jax.numpy as jnp
from jax import lax
from jax.experimental import pallas as pl
from jax.experimental.pallas import tpu as pltpu
from jax.sharding import PartitionSpec as P

GROUPS = 32
C = 256
H = 16
W = 64
ROWS = H * W
PADDED = ROWS + 2 * W
HALF = C // 2
SHARD = 864
SHARD_PAD = 896
QUARTER = 224
UNIT = 32
VMEM = 20 * 1024 * 1024
epsilon = 1e-06
f32 = jnp.float32
bf16 = jnp.bfloat16


def group_total(rows):
    lane = lax.broadcasted_iota(jnp.int32, rows.shape, 1)
    for s in (1, 2, 4):
        up = pltpu.roll(rows, s, 1)
        down = pltpu.roll(rows, C - s, 1)
        rows = rows + jnp.where((lane & s) != 0, up, down)
    return rows


def center_inverse(stats, count):
    sums = group_total(stats) / count
    center = sums[0:1]
    spread = sums[1:2] - center * center
    return center, lax.rsqrt(spread + epsilon)


def sigmoid(v):
    return 1.0 / (1.0 + jnp.exp(-v))


def widths(target, cot, slot):
    zero = jnp.zeros((W, C), bf16)
    for kw in range(3):
        target[kw, slot, 0:W] = zero
        target[kw, slot, W + ROWS : PADDED] = zero
    column = lax.broadcasted_iota(jnp.int32, (W, C), 0)

    @pl.loop(0, H)
    def _(h):
        row = cot(pl.multiple_of(h * W, W))
        at = pl.ds(pl.multiple_of(h * W + W, W), W)
        wide = row.astype(f32)
        target[1, slot, at] = row
        target[0, slot, at] = jnp.where(column == W - 1, 0.0, pltpu.roll(wide, W - 1, 0)).astype(bf16)
        target[2, slot, at] = jnp.where(column == 0, 0.0, pltpu.roll(wide, 1, 0)).astype(bf16)


def first_kernel(clip, cot, out, first, second, last):
    def step(i, carry):
        a, b = carry
        at = pl.ds(pl.multiple_of((i & 7) * 128, 128), 128)
        v = clip[i >> 3, at].astype(f32).reshape(16, 8, C)
        return a + v.sum(0), b + (v * v).sum(0)

    zero = jnp.zeros((8, C), f32)
    a, b = lax.fori_loop(0, 2 * ROWS // 128, step, (zero, zero))
    out[0:1] = a.sum(0, keepdims=True)
    out[1:2] = b.sum(0, keepdims=True)
    first[...] = cot[0]
    second[...] = cot[1]
    last[...] = clip[1]


def widths_kernel(cot, *refs):
    wide = refs[-1]
    for t in range(cot.shape[0]):
        widths(wide, lambda r, t=t: cot[t, pl.ds(r, W)], t)


def ring_sum_kernel(own, before, after, far, held0, held1, out, pass0, pass1):
    out[...] = (own[...] + far[...]) + (before[...] + after[...])


def tap_rows(kh):
    return pl.ds(pl.multiple_of((2 - kh) * W, W), ROWS)


CONTRACT_ROWS = (((0,), (0,)), ((), ()))
CONTRACT_COLUMNS = (((1,), (1,)), ((), ()))


def tap_product(frames, views, channels):
    total = None
    for frame, view in zip(frames, views):
        part = lax.dot_general(frame[:, channels], view, CONTRACT_ROWS, preferred_element_type=f32)
        total = part if total is None else total + part
    return total


def store_tap(tap, total, first_unit, core, keep, send):
    spare = 2 * SHARD_PAD
    for u in range(total.shape[0] // UNIT):
        unit = tap * (C // UNIT) + first_unit + u
        shard = (unit * 1214) >> 15
        dest = ((shard >> 1) & 1) * SHARD_PAD + (unit - shard * (SHARD // UNIT)) * UNIT
        mine = (shard & 1) == core
        piece = total[u * UNIT : (u + 1) * UNIT]
        keep[pl.ds(pl.multiple_of(jnp.where(mine, dest, spare), UNIT), UNIT)] = piece
        send[pl.ds(pl.multiple_of(jnp.where(mine, spare, dest), UNIT), UNIT)] = piece.astype(bf16)


def clear_tails(keep, send):
    for place in range(2):
        tail = slice(place * SHARD_PAD + SHARD, (place + 1) * SHARD_PAD)
        keep[tail] = jnp.zeros((SHARD_PAD - SHARD, C), f32)
        send[tail] = jnp.zeros((SHARD_PAD - SHARD, C), bf16)
    keep[2 * SHARD_PAD :] = jnp.zeros((UNIT, C), f32)
    send[2 * SHARD_PAD :] = jnp.zeros((UNIT, C), bf16)


def middle_taps(low, high, channels, scale, core, act, near, after, keep, send):
    for tap in range(low, high):
        kh, kw = tap // 3 % 3, tap % 3
        rows = slice((2 - kh) * W, (2 - kh) * W + ROWS)
        total = tap_product((act[0], act[1]), (near[kw, 1, rows], after[kw, 0, rows]), channels)
        store_tap(tap, total * scale, channels.start // UNIT, core, keep, send)


def activate(center, inverse, frame, act, gain=None):
    @pl.loop(0, ROWS // 64)
    def _(i):
        at = pl.ds(pl.multiple_of(i * 64, 64), 64)
        v = (frame(at).astype(f32) - center) * inverse
        v = v * sigmoid(v)
        if gain is not None:
            v = v * gain
        act[at] = v.astype(bf16)


def near_kernel(count, scale, where, stats, clip, near, act, keep, send):
    center, inverse = center_inverse(stats[...], count)
    for t in range(2):
        activate(center, inverse, lambda at, t=t: clip[t, at], act.at[t])

    @pl.loop(0, 3)
    def _(kh):
        rows = tap_rows(kh)
        for kw in range(3):
            total = tap_product((act[0], act[1]), (near[kw, 0, rows], near[kw, 1, rows]), slice(None))
            store_tap(18 + kh * 3 + kw, total * scale, 0, where[1], keep, send)

    clear_tails(keep, send)


def upper_kernel(scale, where, act, near, after, keep_in, send_in, order, keep, send):
    middle_taps(14, 18, slice(0, C), scale, where[1], act, near, after, keep, send)
    middle_taps(13, 14, slice(HALF, C), scale, where[1], act, near, after, keep, send)


def lower_kernel(count, scale, where, stats, act, before, near, after, order, keep, send, act_before):
    core = where[1]
    center, inverse = center_inverse(stats[...], count)
    gain = jnp.where(where[0] == 1, 0.0, 1.0)
    activate(center, inverse, lambda at: before[at], act_before, gain)

    @pl.loop(0, 3)
    def _(kh):
        rows = tap_rows(kh)
        for kw in range(3):
            total = tap_product((act_before, act[0]), (near[kw, 1, rows], after[kw, 0, rows]), slice(None))
            store_tap(kh * 3 + kw, total * scale, 0, core, keep, send)

    middle_taps(9, 13, slice(0, C), scale, core, act, near, after, keep, send)
    middle_taps(13, 14, slice(0, HALF), scale, core, act, near, after, keep, send)
    clear_tails(keep, send)


def pack_kernel(where, own, left, right, far, order, packed):
    x = where[2]
    for block, distance in ((own, 0), (left, 3), (right, 1), (far, 2)):
        packed[(x + distance) % 4] = block[...]


def frame_grad(count, frame, stats, clip, views, weights, grad, sums):
    center, inverse = center_inverse(stats[...], count)
    rows_per = 256

    @pl.loop(0, ROWS // rows_per)
    def _(i):
        start = i * rows_per
        total = jnp.zeros((rows_per, C), f32)
        for tap in range(27):
            kt, kh, kw = tap // 9, tap // 3 % 3, tap % 3
            rows = pl.ds(pl.multiple_of((2 - kh) * W + start, W), rows_per)
            w = weights[tap * C : (tap + 1) * C]
            total += lax.dot_general(
                views[2 - kt](kw, rows), w, CONTRACT_COLUMNS, preferred_element_type=f32
            )
        grad[pl.ds(pl.multiple_of(start, rows_per), rows_per)] = total

    zero = jnp.zeros((8, C), f32)

    def finish(i, carry):
        a, b = carry
        at = pl.ds(pl.multiple_of(i * 64, 64), 64)
        v = (clip[frame, at].astype(f32) - center) * inverse
        s = sigmoid(v)
        g = grad[at] * (s * (1.0 + v * (1.0 - s)))
        grad[at] = g
        return a + g.reshape(8, 8, C).sum(0), b + (g * v).reshape(8, 8, C).sum(0)

    a, b = lax.fori_loop(0, ROWS // 64, finish, (zero, zero))
    sums[0:1] = a.sum(0, keepdims=True)
    sums[1:2] = b.sum(0, keepdims=True)


def first_grad_kernel(count, where, stats, clip, near, after, mine, other, order, grad, sums, full):
    core = where[1]
    for x in range(4):
        full[pl.ds(pl.multiple_of((2 * x + core) * SHARD, UNIT), SHARD)] = mine[x]
        full[pl.ds(pl.multiple_of((2 * x + 1 - core) * SHARD, UNIT), SHARD)] = other[x]
    views = (
        lambda kw, rows: near[kw, 0, rows],
        lambda kw, rows: near[kw, 1, rows],
        lambda kw, rows: after[kw, 0, rows],
    )
    frame_grad(count, 0, stats, clip, views, full, grad, sums)


def second_grad_kernel(count, stats, clip, near, after, later, full, order, grad, sums):
    views = (
        lambda kw, rows: near[kw, 1, rows],
        lambda kw, rows: after[kw, 0, rows],
        lambda kw, rows: later[kw, 0, rows],
    )
    frame_grad(count, 1, stats, clip, views, full, grad, sums)


def final_kernel(count, stats, sums, clip, cot, grad0, grad1, out):
    center, inverse = center_inverse(stats[...], count)
    means = group_total(sums[...]) / count
    total, cross = means[0:1], means[1:2]
    for frame, grad in enumerate((grad0, grad1)):

        @pl.loop(0, ROWS // 64)
        def _(i, frame=frame, grad=grad):
            at = pl.ds(pl.multiple_of(i * 64, 64), 64)
            v = (clip[frame, at].astype(f32) - center) * inverse
            g = cot[frame, at].astype(f32) + inverse * (grad[at] - total - v * cross)
            out[frame, at] = g.astype(bf16)


STEPS = (1, 3, 2)


def split_core_kernel(where, keep_up, got_up, keep_low, got_low, held, *out):
    x_own = where[2]

    def total(x, to):
        at = pl.ds(pl.multiple_of((x & 1) * SHARD_PAD, UNIT), SHARD_PAD)

        @pl.when(x < 2)
        def _():
            to[...] = (keep_low[at] + got_low[at].astype(f32)).astype(to.dtype)

        @pl.when(x >= 2)
        def _():
            to[...] = (keep_up[at] + got_up[at].astype(f32)).astype(to.dtype)

    total(x_own, held)
    for step, to in zip(STEPS, out):
        total((x_own + step) & 3, to)


def ring_add(own, arrived, at):
    return (own[at].astype(f32) + arrived[2][at].astype(f32)) + (arrived[0][at].astype(f32) + arrived[1][at].astype(f32))


def split_x_kernel(where, own, a0, a1, a2, order, held, *out):
    y = where[3]

    def total(quarter):
        at = pl.ds(pl.multiple_of((quarter & 3) * QUARTER, UNIT), QUARTER)
        return ring_add(own, (a0, a1, a2), at)

    held[...] = total(y)
    for step, to in zip(STEPS, out):
        to[...] = total(y + step).astype(bf16)


def write_sums(sums, rows, out):
    rows[...] = jnp.zeros((16, C), f32)
    rest = sums
    for k in range(3):
        term = rest.astype(bf16).astype(f32)
        rest = rest - term
        rows[2 * k : 2 * k + 2] = term
    out[QUARTER:] = rows[...].astype(bf16)


def read_sums(block):
    wide = block[QUARTER:].astype(f32)
    return wide[0:2] + wide[2:4] + wide[4:6]


def ring_sums(own, arrived):
    return (read_sums(own) + read_sums(arrived[2])) + (read_sums(arrived[0]) + read_sums(arrived[1]))


def split_y_kernel(held, a0, a1, a2, sums0, sums1, out, rows):
    out[:QUARTER] = ring_add(held, (a0, a1, a2), slice(None)).astype(bf16)
    write_sums(sums0[...] + sums1[...], rows, out)


def reduced_kernel(own, a0, a1, a2, out, rows):
    out[:QUARTER] = ring_add(own, (a0, a1, a2), slice(0, QUARTER)).astype(bf16)
    write_sums(ring_sums(own, (a0, a1, a2)), rows, out)


def finish_kernel(where, own, a0, a1, a2, grad_weight, sums, full):
    y = where[3]
    for block, distance in ((own, 0), (a0, 3), (a1, 1), (a2, 2)):
        at = pl.ds(pl.multiple_of(((y + distance) & 3) * QUARTER, UNIT), QUARTER)
        full[at] = block[:QUARTER].astype(f32)
    grad_weight[...] = full[:SHARD]
    sums[...] = ring_sums(own, (a0, a1, a2))


def call(kernel, out_shape, args, scratch=(), flops=0, bytes_accessed=0, scalars=0, order=(), aliases={}, passed_out=0):
    specs = [pl.BlockSpec(memory_space=pltpu.SMEM)] * scalars
    specs += [pl.BlockSpec(memory_space=pltpu.VMEM)] * (len(args) - scalars)
    specs += [pl.BlockSpec(memory_space=pl.ANY)] * len(order)
    out_specs = jax.tree.map(lambda _: pl.BlockSpec(memory_space=pltpu.VMEM), out_shape)
    if passed_out:
        out_specs = out_specs[:-passed_out] + (pl.BlockSpec(memory_space=pl.ANY),) * passed_out
    return pl.pallas_call(
        kernel,
        out_shape=out_shape,
        in_specs=specs,
        out_specs=out_specs,
        scratch_shapes=list(scratch),
        input_output_aliases=aliases,
        compiler_params=pltpu.CompilerParams(vmem_limit_bytes=VMEM),
        cost_estimate=pl.CostEstimate(flops=flops, bytes_accessed=bytes_accessed, transcendentals=0),
    )(*args, *order)


AXES = {"z": ("tm", 16, 1), "y": ("tm", 16, 4), "x": ("fsdp", 8, 2)}


def ring(axis, blocks):
    name, size, stride = AXES[axis]
    got = []
    for block, distance in zip(blocks, STEPS):
        route = []
        for i in range(size):
            place = (i // stride) % 4
            route.append((i, i + ((place + distance) % 4 - place) * stride))
        got.append(lax.ppermute(block, name, route))
    return got


def swap(block, axis, partners):
    name, size, stride = AXES[axis]
    route = []
    for i in range(size):
        place = (i // stride) % 4
        route.append((i, i + (partners[place] - place) * stride))
    return lax.ppermute(block, name, route)


def swap_core(block):
    return lax.ppermute(block, "fsdp", [(i, i ^ 1) for i in range(8)])


def passed(block, distance):
    route = [(i - distance, i) for i in range(16) if 0 <= i - distance < 16]
    return lax.ppermute(block, "tm", route)


def per_device(clip, cotangent, weights):
    shape = clip.shape
    clip = clip.reshape(2, ROWS, C)
    cot = cotangent.reshape(2, ROWS, C)
    count = 32 * ROWS * (C // GROUPS)
    scale = 1.0 / math.sqrt(8 * 32 * ROWS)
    partial = functools.partial
    S = jax.ShapeDtypeStruct
    tm = lax.axis_index("tm")
    fsdp = lax.axis_index("fsdp")
    where = [tm == 0, fsdp & 1, fsdp >> 1, tm >> 2]
    where = jnp.stack([jnp.asarray(v, jnp.int32) for v in where])
    frame = S((ROWS, C), bf16)

    sums, first, second, last = call(first_kernel, (S((2, C), f32), frame, frame, frame), (clip, cot))
    got = ring("z", [sums] * 3)
    sums, first, last = call(
        ring_sum_kernel,
        (S((2, C), f32), frame, frame),
        (sums, *got),
        order=(first, last),
        aliases={4: 1, 5: 2},
        passed_out=2,
    )
    near = call(widths_kernel, S((3, 2, PADDED, C), bf16), (cot,), order=(sums,))
    half = sums + swap(sums, "y", (1, 0, 3, 2))
    stats = half + swap(half, "y", (3, 2, 1, 0))
    after = call(widths_kernel, S((3, 1, PADDED, C), bf16), (passed(first, -1)[None],))
    before = passed(last, 1)
    later = passed(second, -1)[None]

    rows = 2 * SHARD_PAD + UNIT
    tap_flops = C * C * 2 * ROWS * 2
    pieces = (S((rows, C), f32), S((rows, C), bf16))
    act, keep_up, send_up = call(
        partial(near_kernel, count, scale),
        (S((2, ROWS, C), bf16), *pieces),
        (where, stats, clip, near),
        flops=9 * tap_flops,
        scalars=1,
    )
    mine = call(pack_kernel, S((4, SHARD, C), bf16), (where, weights, *ring("x", [weights] * 3)), scalars=1, order=(act,))
    other = swap_core(mine)
    keep_up, send_up = call(
        partial(upper_kernel, scale),
        pieces,
        (where, act, near, after, keep_up, send_up),
        flops=9 * tap_flops // 2,
        scalars=1,
        order=(mine,),
        aliases={4: 0, 5: 1},
    )
    got_up = swap_core(send_up)
    keep_low, send_low = call(
        partial(lower_kernel, count, scale),
        pieces,
        (where, stats, act, before, near, after),
        [pltpu.VMEM((ROWS, C), bf16)],
        flops=27 * tap_flops // 2,
        scalars=1,
        order=(send_up,),
    )
    got_low = swap_core(send_low)

    block = lambda rows: (S((rows, C), f32),) + (S((rows, C), bf16),) * 3
    held, *out = call(
        split_core_kernel, block(SHARD_PAD), (where, keep_up, got_up, keep_low, got_low), scalars=1
    )
    grad0, sums0, full = call(
        partial(first_grad_kernel, count),
        (S((ROWS, C), f32), S((2, C), f32), S((8 * SHARD, C), bf16)),
        (where, stats, clip, near, after, mine, other),
        flops=27 * tap_flops // 2,
        scalars=1,
        order=(held,),
    )
    later = call(widths_kernel, S((3, 1, PADDED, C), bf16), (later,), order=(sums0,))
    grad1, sums1 = call(
        partial(second_grad_kernel, count),
        (S((ROWS, C), f32), S((2, C), f32)),
        (stats, clip, near, after, later, full),
        flops=27 * tap_flops // 2,
        order=(sums0,),
    )
    held, *out = call(
        split_x_kernel, block(QUARTER), (where, held, *ring("x", out)), scalars=1, order=(sums1,)
    )
    rows16 = [pltpu.VMEM((16, C), f32)]
    message = S((QUARTER + 16, C), bf16)
    own = call(split_y_kernel, message, (held, *ring("y", out), sums0, sums1), rows16)
    own = call(reduced_kernel, message, (own, *ring("z", [own] * 3)), rows16)
    grad_weight, sums = call(
        finish_kernel,
        (S((SHARD, C), f32), S((2, C), f32)),
        (where, own, *ring("y", [own] * 3)),
        [pltpu.VMEM((SHARD_PAD, C), f32)],
        scalars=1,
    )
    grad_input = call(
        partial(final_kernel, count), S((2, ROWS, C), bf16), (stats, sums, clip, cot, grad0, grad1)
    )
    return grad_input.reshape(shape), grad_weight


def solution(mesh):
    in_specs = (
        P("fsdp", "tm", None, None, None),
        P("fsdp", "tm", None, None, None),
        P("fsdp", None),
    )
    out_specs = (P("fsdp", "tm", None, None, None), P("fsdp", None))
    return jax.shard_map(
        per_device, mesh=mesh, in_specs=in_specs, out_specs=out_specs, check_vma=False
    )
```

```python
import functools
import math

import jax
import jax.numpy as jnp
from jax import lax
from jax.experimental import pallas as pl
from jax.experimental.pallas import tpu as pltpu
from jax.sharding import PartitionSpec as P

GROUPS = 32
C = 256
H = 16
W = 64
ROWS = H * W
PADDED = ROWS + 2 * W
HALF = C // 2
SHARD = 864
SHARD_PAD = 896
QUARTER = 224
UNIT = 32
VMEM = 20 * 1024 * 1024
epsilon = 1e-06
f32 = jnp.float32
bf16 = jnp.bfloat16


def group_total(rows):
    lane = lax.broadcasted_iota(jnp.int32, rows.shape, 1)
    for s in (1, 2, 4):
        up = pltpu.roll(rows, s, 1)
        down = pltpu.roll(rows, C - s, 1)
        rows = rows + jnp.where((lane & s) != 0, up, down)
    return rows


def center_inverse(stats, count):
    sums = group_total(stats) / count
    center = sums[0:1]
    spread = sums[1:2] - center * center
    return center, lax.rsqrt(spread + epsilon)


def sigmoid(v):
    return 1.0 / (1.0 + jnp.exp(-v))


def widths(target, cot, slot):
    zero = jnp.zeros((W, C), bf16)
    for kw in range(3):
        target[kw, slot, 0:W] = zero
        target[kw, slot, W + ROWS : PADDED] = zero
    column = lax.broadcasted_iota(jnp.int32, (W, C), 0)

    @pl.loop(0, H)
    def _(h):
        row = cot(pl.multiple_of(h * W, W))
        at = pl.ds(pl.multiple_of(h * W + W, W), W)
        wide = row.astype(f32)
        target[1, slot, at] = row
        target[0, slot, at] = jnp.where(column == W - 1, 0.0, pltpu.roll(wide, W - 1, 0)).astype(bf16)
        target[2, slot, at] = jnp.where(column == 0, 0.0, pltpu.roll(wide, 1, 0)).astype(bf16)


def first_kernel(clip, out, last):
    def step(i, carry):
        a, b = carry
        at = pl.ds(pl.multiple_of((i & 7) * 128, 128), 128)
        v = clip[i >> 3, at].astype(f32).reshape(16, 8, C)
        return a + v.sum(0), b + (v * v).sum(0)

    zero = jnp.zeros((8, C), f32)
    a, b = lax.fori_loop(0, 2 * ROWS // 128, step, (zero, zero))
    out[0:1] = a.sum(0, keepdims=True)
    out[1:2] = b.sum(0, keepdims=True)
    last[...] = clip[1]


def copy_kernel(cot, order, first, second):
    first[...] = cot[0]
    second[...] = cot[1]


def widths_kernel(cot, *refs):
    wide = refs[-1]
    for t in range(cot.shape[0]):
        widths(wide, lambda r, t=t: cot[t, pl.ds(r, W)], t)


def ring_sum_kernel(own, before, after, far, held0, held1, out, pass0, pass1):
    out[...] = (own[...] + far[...]) + (before[...] + after[...])


def tap_rows(kh):
    return pl.ds(pl.multiple_of((2 - kh) * W, W), ROWS)


CONTRACT_ROWS = (((0,), (0,)), ((), ()))
CONTRACT_COLUMNS = (((1,), (1,)), ((), ()))


def tap_product(frames, views, channels):
    total = None
    for frame, view in zip(frames, views):
        part = lax.dot_general(frame[:, channels], view, CONTRACT_ROWS, preferred_element_type=f32)
        total = part if total is None else total + part
    return total


def store_tap(tap, total, first_unit, core, keep, send):
    spare = 2 * SHARD_PAD
    for u in range(total.shape[0] // UNIT):
        unit = tap * (C // UNIT) + first_unit + u
        shard = (unit * 1214) >> 15
        dest = ((shard >> 1) & 1) * SHARD_PAD + (unit - shard * (SHARD // UNIT)) * UNIT
        mine = (shard & 1) == core
        piece = total[u * UNIT : (u + 1) * UNIT]
        keep[pl.ds(pl.multiple_of(jnp.where(mine, dest, spare), UNIT), UNIT)] = piece
        send[pl.ds(pl.multiple_of(jnp.where(mine, spare, dest), UNIT), UNIT)] = piece.astype(bf16)


def clear_tails(keep, send):
    for place in range(2):
        tail = slice(place * SHARD_PAD + SHARD, (place + 1) * SHARD_PAD)
        keep[tail] = jnp.zeros((SHARD_PAD - SHARD, C), f32)
        send[tail] = jnp.zeros((SHARD_PAD - SHARD, C), bf16)
    keep[2 * SHARD_PAD :] = jnp.zeros((UNIT, C), f32)
    send[2 * SHARD_PAD :] = jnp.zeros((UNIT, C), bf16)


def middle_taps(low, high, channels, scale, core, act, near, after, keep, send):
    for tap in range(low, high):
        kh, kw = tap // 3 % 3, tap % 3
        rows = slice((2 - kh) * W, (2 - kh) * W + ROWS)
        total = tap_product((act[0], act[1]), (near[kw, 1, rows], after[kw, 0, rows]), channels)
        store_tap(tap, total * scale, channels.start // UNIT, core, keep, send)


def activate(center, inverse, frame, act, gain=None):
    @pl.loop(0, ROWS // 64)
    def _(i):
        at = pl.ds(pl.multiple_of(i * 64, 64), 64)
        v = (frame(at).astype(f32) - center) * inverse
        v = v * sigmoid(v)
        if gain is not None:
            v = v * gain
        act[at] = v.astype(bf16)


def near_kernel(count, scale, where, stats, clip, near, act, keep, send):
    center, inverse = center_inverse(stats[...], count)
    for t in range(2):
        activate(center, inverse, lambda at, t=t: clip[t, at], act.at[t])

    @pl.loop(0, 3)
    def _(kh):
        rows = tap_rows(kh)
        for kw in range(3):
            total = tap_product((act[0], act[1]), (near[kw, 0, rows], near[kw, 1, rows]), slice(None))
            store_tap(18 + kh * 3 + kw, total * scale, 0, where[1], keep, send)

    clear_tails(keep, send)


def upper_kernel(scale, where, act, near, after, keep_in, send_in, order, keep, send):
    middle_taps(14, 18, slice(0, C), scale, where[1], act, near, after, keep, send)
    middle_taps(13, 14, slice(HALF, C), scale, where[1], act, near, after, keep, send)


def lower_kernel(count, scale, where, stats, act, before, near, after, order, keep, send, act_before):
    core = where[1]
    center, inverse = center_inverse(stats[...], count)
    gain = jnp.where(where[0] == 1, 0.0, 1.0)
    activate(center, inverse, lambda at: before[at], act_before, gain)

    @pl.loop(0, 3)
    def _(kh):
        rows = tap_rows(kh)
        for kw in range(3):
            total = tap_product((act_before, act[0]), (near[kw, 1, rows], after[kw, 0, rows]), slice(None))
            store_tap(kh * 3 + kw, total * scale, 0, core, keep, send)

    middle_taps(9, 13, slice(0, C), scale, core, act, near, after, keep, send)
    middle_taps(13, 14, slice(0, HALF), scale, core, act, near, after, keep, send)
    clear_tails(keep, send)


def pack_kernel(where, own, left, right, far, order, packed):
    x = where[2]
    for block, distance in ((own, 0), (left, 3), (right, 1), (far, 2)):
        packed[(x + distance) % 4] = block[...]


def frame_grad(count, frame, stats, clip, views, weights, grad, sums):
    center, inverse = center_inverse(stats[...], count)
    rows_per = 256

    @pl.loop(0, ROWS // rows_per)
    def _(i):
        start = i * rows_per
        total = jnp.zeros((rows_per, C), f32)
        for tap in range(27):
            kt, kh, kw = tap // 9, tap // 3 % 3, tap % 3
            rows = pl.ds(pl.multiple_of((2 - kh) * W + start, W), rows_per)
            w = weights[tap * C : (tap + 1) * C]
            total += lax.dot_general(
                views[2 - kt](kw, rows), w, CONTRACT_COLUMNS, preferred_element_type=f32
            )
        grad[pl.ds(pl.multiple_of(start, rows_per), rows_per)] = total

    zero = jnp.zeros((8, C), f32)

    def finish(i, carry):
        a, b = carry
        at = pl.ds(pl.multiple_of(i * 64, 64), 64)
        v = (clip[frame, at].astype(f32) - center) * inverse
        s = sigmoid(v)
        g = grad[at] * (s * (1.0 + v * (1.0 - s)))
        grad[at] = g
        return a + g.reshape(8, 8, C).sum(0), b + (g * v).reshape(8, 8, C).sum(0)

    a, b = lax.fori_loop(0, ROWS // 64, finish, (zero, zero))
    sums[0:1] = a.sum(0, keepdims=True)
    sums[1:2] = b.sum(0, keepdims=True)


def first_grad_kernel(count, where, stats, clip, near, after, mine, other, order, grad, sums, full):
    core = where[1]
    for x in range(4):
        full[pl.ds(pl.multiple_of((2 * x + core) * SHARD, UNIT), SHARD)] = mine[x]
        full[pl.ds(pl.multiple_of((2 * x + 1 - core) * SHARD, UNIT), SHARD)] = other[x]
    views = (
        lambda kw, rows: near[kw, 0, rows],
        lambda kw, rows: near[kw, 1, rows],
        lambda kw, rows: after[kw, 0, rows],
    )
    frame_grad(count, 0, stats, clip, views, full, grad, sums)


def second_grad_kernel(count, stats, clip, near, after, later, full, order, grad, sums):
    views = (
        lambda kw, rows: near[kw, 1, rows],
        lambda kw, rows: after[kw, 0, rows],
        lambda kw, rows: later[kw, 0, rows],
    )
    frame_grad(count, 1, stats, clip, views, full, grad, sums)


def final_kernel(count, stats, sums, clip, cot, grad0, grad1, out):
    center, inverse = center_inverse(stats[...], count)
    means = group_total(sums[...]) / count
    total, cross = means[0:1], means[1:2]
    for frame, grad in enumerate((grad0, grad1)):

        @pl.loop(0, ROWS // 64)
        def _(i, frame=frame, grad=grad):
            at = pl.ds(pl.multiple_of(i * 64, 64), 64)
            v = (clip[frame, at].astype(f32) - center) * inverse
            g = cot[frame, at].astype(f32) + inverse * (grad[at] - total - v * cross)
            out[frame, at] = g.astype(bf16)


STEPS = (1, 3, 2)


def split_core_kernel(where, keep_up, got_up, keep_low, got_low, held, *out):
    x_own = where[2]

    def total(x, to):
        at = pl.ds(pl.multiple_of((x & 1) * SHARD_PAD, UNIT), SHARD_PAD)

        @pl.when(x < 2)
        def _():
            to[...] = (keep_low[at] + got_low[at].astype(f32)).astype(to.dtype)

        @pl.when(x >= 2)
        def _():
            to[...] = (keep_up[at] + got_up[at].astype(f32)).astype(to.dtype)

    total(x_own, held)
    for step, to in zip(STEPS, out):
        total((x_own + step) & 3, to)


def ring_add(own, arrived, at):
    return (own[at].astype(f32) + arrived[2][at].astype(f32)) + (arrived[0][at].astype(f32) + arrived[1][at].astype(f32))


def split_x_kernel(where, own, a0, a1, a2, sums0, sums1, held, sums, m0, m1, m2, rows):
    out = (m0, m1, m2)
    y = where[3]

    def total(quarter):
        at = pl.ds(pl.multiple_of((quarter & 3) * QUARTER, UNIT), QUARTER)
        return ring_add(own, (a0, a1, a2), at)

    held[...] = total(y)
    sums[...] = sums0[...] + sums1[...]
    for step, to in zip(STEPS, out):
        to[:QUARTER] = total(y + step).astype(bf16)
        write_sums(sums[...], rows, to)


def write_sums(sums, rows, out):
    rows[...] = jnp.zeros((16, C), f32)
    rest = sums
    for k in range(3):
        term = rest.astype(bf16).astype(f32)
        rest = rest - term
        rows[2 * k : 2 * k + 2] = term
    out[QUARTER:] = rows[...].astype(bf16)


def read_sums(block):
    wide = block[QUARTER:].astype(f32)
    return wide[0:2] + wide[2:4] + wide[4:6]


def ring_sums(own, arrived):
    return (own + read_sums(arrived[2])) + (read_sums(arrived[0]) + read_sums(arrived[1]))


def split_y_kernel(held, sums, a0, a1, a2, out, next_sums, rows):
    out[:QUARTER] = ring_add(held, (a0, a1, a2), slice(0, QUARTER)).astype(bf16)
    next_sums[...] = ring_sums(sums[...], (a0, a1, a2))
    write_sums(next_sums[...], rows, out)


def reduced_kernel(own, sums, a0, a1, a2, out, next_sums):
    out[...] = ring_add(own, (a0, a1, a2), slice(0, QUARTER)).astype(bf16)
    next_sums[...] = ring_sums(sums[...], (a0, a1, a2))


def finish_kernel(where, own, a0, a1, a2, grad_weight, full):
    y = where[3]
    for block, distance in ((own, 0), (a0, 3), (a1, 1), (a2, 2)):
        at = pl.ds(pl.multiple_of(((y + distance) & 3) * QUARTER, UNIT), QUARTER)
        full[at] = block[...].astype(f32)
    grad_weight[...] = full[:SHARD]


def call(kernel, out_shape, args, scratch=(), flops=0, bytes_accessed=0, scalars=0, order=(), aliases={}, passed_out=0):
    specs = [pl.BlockSpec(memory_space=pltpu.SMEM)] * scalars
    specs += [pl.BlockSpec(memory_space=pltpu.VMEM)] * (len(args) - scalars)
    specs += [pl.BlockSpec(memory_space=pl.ANY)] * len(order)
    out_specs = jax.tree.map(lambda _: pl.BlockSpec(memory_space=pltpu.VMEM), out_shape)
    if passed_out:
        out_specs = out_specs[:-passed_out] + (pl.BlockSpec(memory_space=pl.ANY),) * passed_out
    return pl.pallas_call(
        kernel,
        out_shape=out_shape,
        in_specs=specs,
        out_specs=out_specs,
        scratch_shapes=list(scratch),
        input_output_aliases=aliases,
        compiler_params=pltpu.CompilerParams(vmem_limit_bytes=VMEM),
        cost_estimate=pl.CostEstimate(flops=flops, bytes_accessed=bytes_accessed, transcendentals=0),
    )(*args, *order)


AXES = {"z": ("tm", 16, 1), "y": ("tm", 16, 4), "x": ("fsdp", 8, 2)}


def ring(axis, blocks):
    name, size, stride = AXES[axis]
    got = []
    for block, distance in zip(blocks, STEPS):
        route = []
        for i in range(size):
            place = (i // stride) % 4
            route.append((i, i + ((place + distance) % 4 - place) * stride))
        got.append(lax.ppermute(block, name, route))
    return got


def swap(block, axis, partners):
    name, size, stride = AXES[axis]
    route = []
    for i in range(size):
        place = (i // stride) % 4
        route.append((i, i + (partners[place] - place) * stride))
    return lax.ppermute(block, name, route)


def swap_core(block):
    return lax.ppermute(block, "fsdp", [(i, i ^ 1) for i in range(8)])


def passed(block, distance):
    route = [(i - distance, i) for i in range(16) if 0 <= i - distance < 16]
    return lax.ppermute(block, "tm", route)


def per_device(clip, cotangent, weights):
    shape = clip.shape
    clip = clip.reshape(2, ROWS, C)
    cot = cotangent.reshape(2, ROWS, C)
    count = 32 * ROWS * (C // GROUPS)
    scale = 1.0 / math.sqrt(8 * 32 * ROWS)
    partial = functools.partial
    S = jax.ShapeDtypeStruct
    tm = lax.axis_index("tm")
    fsdp = lax.axis_index("fsdp")
    where = [tm == 0, fsdp & 1, fsdp >> 1, tm >> 2]
    where = jnp.stack([jnp.asarray(v, jnp.int32) for v in where])
    frame = S((ROWS, C), bf16)

    sums, last = call(first_kernel, (S((2, C), f32), frame), (clip,))
    got = ring("z", [sums] * 3)
    first, second = call(copy_kernel, (frame, frame), (cot,), order=(sums,))
    sums, first, last = call(
        ring_sum_kernel,
        (S((2, C), f32), frame, frame),
        (sums, *got),
        order=(first, last),
        aliases={4: 1, 5: 2},
        passed_out=2,
    )
    near = call(widths_kernel, S((3, 2, PADDED, C), bf16), (cot,), order=(sums,))
    half = sums + swap(sums, "y", (1, 0, 3, 2))
    stats = half + swap(half, "y", (3, 2, 1, 0))
    after = call(widths_kernel, S((3, 1, PADDED, C), bf16), (passed(first, -1)[None],))
    before = passed(last, 1)

    rows = 2 * SHARD_PAD + UNIT
    tap_flops = C * C * 2 * ROWS * 2
    pieces = (S((rows, C), f32), S((rows, C), bf16))
    act, keep_up, send_up = call(
        partial(near_kernel, count, scale),
        (S((2, ROWS, C), bf16), *pieces),
        (where, stats, clip, near),
        flops=9 * tap_flops,
        scalars=1,
    )
    mine = call(pack_kernel, S((4, SHARD, C), bf16), (where, weights, *ring("x", [weights] * 3)), scalars=1, order=(act,))
    other = swap_core(mine)
    keep_up, send_up = call(
        partial(upper_kernel, scale),
        pieces,
        (where, act, near, after, keep_up, send_up),
        flops=9 * tap_flops // 2,
        scalars=1,
        order=(mine,),
        aliases={4: 0, 5: 1},
    )
    got_up = swap_core(send_up)
    keep_low, send_low = call(
        partial(lower_kernel, count, scale),
        pieces,
        (where, stats, act, before, near, after),
        [pltpu.VMEM((ROWS, C), bf16)],
        flops=27 * tap_flops // 2,
        scalars=1,
        order=(send_up,),
    )
    got_low = swap_core(send_low)

    block = lambda rows: (S((rows, C), f32),) + (S((rows, C), bf16),) * 3
    held, *out = call(
        split_core_kernel, block(SHARD_PAD), (where, keep_up, got_up, keep_low, got_low), scalars=1
    )
    later = passed(second, -1)[None]
    grad0, sums0, full = call(
        partial(first_grad_kernel, count),
        (S((ROWS, C), f32), S((2, C), f32), S((8 * SHARD, C), bf16)),
        (where, stats, clip, near, after, mine, other),
        flops=27 * tap_flops // 2,
        scalars=1,
        order=(held,),
    )
    later = call(widths_kernel, S((3, 1, PADDED, C), bf16), (later,), order=(sums0,))
    grad1, sums1 = call(
        partial(second_grad_kernel, count),
        (S((ROWS, C), f32), S((2, C), f32)),
        (stats, clip, near, after, later, full),
        flops=27 * tap_flops // 2,
        order=(sums0,),
    )
    rows16 = [pltpu.VMEM((16, C), f32)]
    message = S((QUARTER + 16, C), bf16)
    held, sums, *out = call(
        split_x_kernel,
        (S((QUARTER, C), f32), S((2, C), f32), message, message, message),
        (where, held, *ring("x", out), sums0, sums1),
        rows16,
        scalars=1,
    )
    own, sums = call(split_y_kernel, (message, S((2, C), f32)), (held, sums, *ring("y", out)), rows16)
    own, sums = call(
        reduced_kernel, (S((QUARTER, C), bf16), S((2, C), f32)), (own, sums, *ring("z", [own] * 3))
    )
    grad_input = call(
        partial(final_kernel, count),
        S((2, ROWS, C), bf16),
        (stats, sums, clip, cot, grad0, grad1),
        bytes_accessed=8_000_000,
    )
    grad_weight = call(
        finish_kernel,
        S((SHARD, C), f32),
        (where, own, *ring("y", [own] * 3)),
        [pltpu.VMEM((SHARD_PAD, C), f32)],
        scalars=1,
    )
    return grad_input.reshape(shape), grad_weight


def solution(mesh):
    in_specs = (
        P("fsdp", "tm", None, None, None),
        P("fsdp", "tm", None, None, None),
        P("fsdp", None),
    )
    out_specs = (P("fsdp", "tm", None, None, None), P("fsdp", None))
    return jax.shard_map(
        per_device, mesh=mesh, in_specs=in_specs, out_specs=out_specs, check_vma=False
    )
```

```python
import functools
import math

import jax
import jax.numpy as jnp
from jax import lax
from jax.experimental import pallas as pl
from jax.experimental.pallas import tpu as pltpu
from jax.sharding import PartitionSpec as P

GROUPS = 32
C = 256
H = 16
W = 64
ROWS = H * W
PADDED = ROWS + 2 * W
HALF = C // 2
SHARD = 864
SHARD_PAD = 896
QUARTER = 224
UNIT = 32
VMEM = 20 * 1024 * 1024
epsilon = 1e-06
f32 = jnp.float32
bf16 = jnp.bfloat16


def group_total(rows):
    lane = lax.broadcasted_iota(jnp.int32, rows.shape, 1)
    for s in (1, 2, 4):
        up = pltpu.roll(rows, s, 1)
        down = pltpu.roll(rows, C - s, 1)
        rows = rows + jnp.where((lane & s) != 0, up, down)
    return rows


def center_inverse(stats, count):
    sums = group_total(stats) / count
    center = sums[0:1]
    spread = sums[1:2] - center * center
    return center, lax.rsqrt(spread + epsilon)


def sigmoid(v):
    return 1.0 / (1.0 + jnp.exp(-v))


def widths(target, cot, slot):
    zero = jnp.zeros((W, C), bf16)
    for kw in range(3):
        target[kw, slot, 0:W] = zero
        target[kw, slot, W + ROWS : PADDED] = zero
    column = lax.broadcasted_iota(jnp.int32, (W, C), 0)

    @pl.loop(0, H)
    def _(h):
        row = cot(pl.multiple_of(h * W, W))
        at = pl.ds(pl.multiple_of(h * W + W, W), W)
        wide = row.astype(f32)
        target[1, slot, at] = row
        target[0, slot, at] = jnp.where(column == W - 1, 0.0, pltpu.roll(wide, W - 1, 0)).astype(bf16)
        target[2, slot, at] = jnp.where(column == 0, 0.0, pltpu.roll(wide, 1, 0)).astype(bf16)


def first_kernel(clip, out, last):
    def step(i, carry):
        a, b = carry
        at = pl.ds(pl.multiple_of((i & 7) * 128, 128), 128)
        v = clip[i >> 3, at].astype(f32).reshape(16, 8, C)
        return a + v.sum(0), b + (v * v).sum(0)

    zero = jnp.zeros((8, C), f32)
    a, b = lax.fori_loop(0, 2 * ROWS // 128, step, (zero, zero))
    row = lax.broadcasted_iota(jnp.int32, (8, C), 0)
    both = jnp.where(row == 0, a.sum(0, keepdims=True), jnp.where(row == 1, b.sum(0, keepdims=True), 0.0))
    for i in range(16):
        out[i] = both
    last[...] = clip[1]


def copy_kernel(cot, order, first, second):
    first[...] = cot[0]
    second[...] = cot[1]


def widths_kernel(cot, *refs):
    wide = refs[-1]
    for t in range(cot.shape[0]):
        widths(wide, lambda r, t=t: cot[t, pl.ds(r, W)], t)


def total_kernel(parts, held0, held1, out, pass0, pass1):
    total = parts[0]
    for i in range(1, 16):
        total = total + parts[i]
    out[...] = total[0:2]


def tap_rows(kh):
    return pl.ds(pl.multiple_of((2 - kh) * W, W), ROWS)


CONTRACT_ROWS = (((0,), (0,)), ((), ()))
CONTRACT_COLUMNS = (((1,), (1,)), ((), ()))


def tap_product(frames, views, channels):
    total = None
    for frame, view in zip(frames, views):
        part = lax.dot_general(frame[:, channels], view, CONTRACT_ROWS, preferred_element_type=f32)
        total = part if total is None else total + part
    return total


def store_tap(tap, total, first_unit, core, keep, send):
    spare = 2 * SHARD_PAD
    for u in range(total.shape[0] // UNIT):
        unit = tap * (C // UNIT) + first_unit + u
        shard = (unit * 1214) >> 15
        dest = ((shard >> 1) & 1) * SHARD_PAD + (unit - shard * (SHARD // UNIT)) * UNIT
        mine = (shard & 1) == core
        piece = total[u * UNIT : (u + 1) * UNIT]
        keep[pl.ds(pl.multiple_of(jnp.where(mine, dest, spare), UNIT), UNIT)] = piece
        send[pl.ds(pl.multiple_of(jnp.where(mine, spare, dest), UNIT), UNIT)] = piece.astype(bf16)


def clear_tails(keep, send):
    for place in range(2):
        tail = slice(place * SHARD_PAD + SHARD, (place + 1) * SHARD_PAD)
        keep[tail] = jnp.zeros((SHARD_PAD - SHARD, C), f32)
        send[tail] = jnp.zeros((SHARD_PAD - SHARD, C), bf16)
    keep[2 * SHARD_PAD :] = jnp.zeros((UNIT, C), f32)
    send[2 * SHARD_PAD :] = jnp.zeros((UNIT, C), bf16)


def middle_taps(low, high, channels, scale, core, act, near, after, keep, send):
    for tap in range(low, high):
        kh, kw = tap // 3 % 3, tap % 3
        rows = slice((2 - kh) * W, (2 - kh) * W + ROWS)
        total = tap_product((act[0], act[1]), (near[kw, 1, rows], after[kw, 0, rows]), channels)
        store_tap(tap, total * scale, channels.start // UNIT, core, keep, send)


def activate(center, inverse, frame, act, gain=None):
    @pl.loop(0, ROWS // 64)
    def _(i):
        at = pl.ds(pl.multiple_of(i * 64, 64), 64)
        v = (frame(at).astype(f32) - center) * inverse
        v = v * sigmoid(v)
        if gain is not None:
            v = v * gain
        act[at] = v.astype(bf16)


def near_kernel(count, scale, where, stats, clip, near, act, keep, send):
    center, inverse = center_inverse(stats[...], count)
    for t in range(2):
        activate(center, inverse, lambda at, t=t: clip[t, at], act.at[t])

    @pl.loop(0, 3)
    def _(kh):
        rows = tap_rows(kh)
        for kw in range(3):
            total = tap_product((act[0], act[1]), (near[kw, 0, rows], near[kw, 1, rows]), slice(None))
            store_tap(18 + kh * 3 + kw, total * scale, 0, where[1], keep, send)

    clear_tails(keep, send)


def upper_kernel(scale, where, act, near, after, keep_in, send_in, order, keep, send):
    middle_taps(14, 18, slice(0, C), scale, where[1], act, near, after, keep, send)
    middle_taps(13, 14, slice(HALF, C), scale, where[1], act, near, after, keep, send)


def lower_kernel(count, scale, where, stats, act, before, near, after, order, keep, send, act_before):
    core = where[1]
    center, inverse = center_inverse(stats[...], count)
    gain = jnp.where(where[0] == 1, 0.0, 1.0)
    activate(center, inverse, lambda at: before[at], act_before, gain)

    @pl.loop(0, 3)
    def _(kh):
        rows = tap_rows(kh)
        for kw in range(3):
            total = tap_product((act_before, act[0]), (near[kw, 1, rows], after[kw, 0, rows]), slice(None))
            store_tap(kh * 3 + kw, total * scale, 0, core, keep, send)

    middle_taps(9, 13, slice(0, C), scale, core, act, near, after, keep, send)
    middle_taps(13, 14, slice(0, HALF), scale, core, act, near, after, keep, send)
    clear_tails(keep, send)


def pack_kernel(where, own, left, right, far, order, packed):
    x = where[2]
    for block, distance in ((own, 0), (left, 3), (right, 1), (far, 2)):
        packed[(x + distance) % 4] = block[...]


def frame_grad(count, frame, stats, clip, views, weights, grad, sums):
    center, inverse = center_inverse(stats[...], count)
    rows_per = 256

    @pl.loop(0, ROWS // rows_per)
    def _(i):
        start = i * rows_per
        total = jnp.zeros((rows_per, C), f32)
        for tap in range(27):
            kt, kh, kw = tap // 9, tap // 3 % 3, tap % 3
            rows = pl.ds(pl.multiple_of((2 - kh) * W + start, W), rows_per)
            w = weights[tap * C : (tap + 1) * C]
            total += lax.dot_general(
                views[2 - kt](kw, rows), w, CONTRACT_COLUMNS, preferred_element_type=f32
            )
        grad[pl.ds(pl.multiple_of(start, rows_per), rows_per)] = total

    zero = jnp.zeros((8, C), f32)

    def finish(i, carry):
        a, b = carry
        at = pl.ds(pl.multiple_of(i * 64, 64), 64)
        v = (clip[frame, at].astype(f32) - center) * inverse
        s = sigmoid(v)
        g = grad[at] * (s * (1.0 + v * (1.0 - s)))
        grad[at] = g
        return a + g.reshape(8, 8, C).sum(0), b + (g * v).reshape(8, 8, C).sum(0)

    a, b = lax.fori_loop(0, ROWS // 64, finish, (zero, zero))
    sums[0:1] = a.sum(0, keepdims=True)
    sums[1:2] = b.sum(0, keepdims=True)


def first_grad_kernel(count, where, stats, clip, near, after, mine, other, order, grad, sums, full):
    core = where[1]
    for x in range(4):
        full[pl.ds(pl.multiple_of((2 * x + core) * SHARD, UNIT), SHARD)] = mine[x]
        full[pl.ds(pl.multiple_of((2 * x + 1 - core) * SHARD, UNIT), SHARD)] = other[x]
    views = (
        lambda kw, rows: near[kw, 0, rows],
        lambda kw, rows: near[kw, 1, rows],
        lambda kw, rows: after[kw, 0, rows],
    )
    frame_grad(count, 0, stats, clip, views, full, grad, sums)


def second_grad_kernel(count, stats, clip, near, after, later, full, order, grad, sums):
    views = (
        lambda kw, rows: near[kw, 1, rows],
        lambda kw, rows: after[kw, 0, rows],
        lambda kw, rows: later[kw, 0, rows],
    )
    frame_grad(count, 1, stats, clip, views, full, grad, sums)


def final_kernel(count, stats, sums, clip, cot, grad0, grad1, out):
    center, inverse = center_inverse(stats[...], count)
    means = group_total(sums[...]) / count
    total, cross = means[0:1], means[1:2]
    for frame, grad in enumerate((grad0, grad1)):

        @pl.loop(0, ROWS // 64)
        def _(i, frame=frame, grad=grad):
            at = pl.ds(pl.multiple_of(i * 64, 64), 64)
            v = (clip[frame, at].astype(f32) - center) * inverse
            g = cot[frame, at].astype(f32) + inverse * (grad[at] - total - v * cross)
            out[frame, at] = g.astype(bf16)


STEPS = (1, 3, 2)


def split_core_kernel(where, keep_up, got_up, keep_low, got_low, held, *out):
    x_own = where[2]

    def total(x, to):
        at = pl.ds(pl.multiple_of((x & 1) * SHARD_PAD, UNIT), SHARD_PAD)

        @pl.when(x < 2)
        def _():
            to[...] = (keep_low[at] + got_low[at].astype(f32)).astype(to.dtype)

        @pl.when(x >= 2)
        def _():
            to[...] = (keep_up[at] + got_up[at].astype(f32)).astype(to.dtype)

    total(x_own, held)
    for step, to in zip(STEPS, out):
        total((x_own + step) & 3, to)


def ring_add(own, arrived, at):
    return (own[at].astype(f32) + arrived[2][at].astype(f32)) + (arrived[0][at].astype(f32) + arrived[1][at].astype(f32))


def split_x_kernel(where, own, a0, a1, a2, sums0, sums1, held, sums, m0, m1, m2, rows):
    out = (m0, m1, m2)
    y = where[3]

    def total(quarter):
        at = pl.ds(pl.multiple_of((quarter & 3) * QUARTER, UNIT), QUARTER)
        return ring_add(own, (a0, a1, a2), at)

    held[...] = total(y)
    sums[...] = sums0[...] + sums1[...]
    for step, to in zip(STEPS, out):
        to[:QUARTER] = total(y + step).astype(bf16)
        write_sums(sums[...], rows, to)


def write_sums(sums, rows, out):
    rows[...] = jnp.zeros((16, C), f32)
    rest = sums
    for k in range(3):
        term = rest.astype(bf16).astype(f32)
        rest = rest - term
        rows[2 * k : 2 * k + 2] = term
    out[QUARTER:] = rows[...].astype(bf16)


def read_sums(block):
    wide = block[QUARTER:].astype(f32)
    return wide[0:2] + wide[2:4] + wide[4:6]


def ring_sums(own, arrived):
    return (own + read_sums(arrived[2])) + (read_sums(arrived[0]) + read_sums(arrived[1]))


def split_y_kernel(held, sums, a0, a1, a2, out, next_sums, rows):
    out[:QUARTER] = ring_add(held, (a0, a1, a2), slice(0, QUARTER)).astype(bf16)
    next_sums[...] = ring_sums(sums[...], (a0, a1, a2))
    write_sums(next_sums[...], rows, out)


def reduced_kernel(own, sums, a0, a1, a2, out, next_sums):
    out[...] = ring_add(own, (a0, a1, a2), slice(0, QUARTER)).astype(bf16)
    next_sums[...] = ring_sums(sums[...], (a0, a1, a2))


def finish_kernel(where, own, a0, a1, a2, grad_weight, full):
    y = where[3]
    for block, distance in ((own, 0), (a0, 3), (a1, 1), (a2, 2)):
        at = pl.ds(pl.multiple_of(((y + distance) & 3) * QUARTER, UNIT), QUARTER)
        full[at] = block[...].astype(f32)
    grad_weight[...] = full[:SHARD]


def call(kernel, out_shape, args, scratch=(), flops=0, bytes_accessed=0, scalars=0, order=(), aliases={}, passed_out=0):
    specs = [pl.BlockSpec(memory_space=pltpu.SMEM)] * scalars
    specs += [pl.BlockSpec(memory_space=pltpu.VMEM)] * (len(args) - scalars)
    specs += [pl.BlockSpec(memory_space=pl.ANY)] * len(order)
    out_specs = jax.tree.map(lambda _: pl.BlockSpec(memory_space=pltpu.VMEM), out_shape)
    if passed_out:
        out_specs = out_specs[:-passed_out] + (pl.BlockSpec(memory_space=pl.ANY),) * passed_out
    return pl.pallas_call(
        kernel,
        out_shape=out_shape,
        in_specs=specs,
        out_specs=out_specs,
        scratch_shapes=list(scratch),
        input_output_aliases=aliases,
        compiler_params=pltpu.CompilerParams(vmem_limit_bytes=VMEM),
        cost_estimate=pl.CostEstimate(flops=flops, bytes_accessed=bytes_accessed, transcendentals=0),
    )(*args, *order)


AXES = {"z": ("tm", 16, 1), "y": ("tm", 16, 4), "x": ("fsdp", 8, 2)}


def ring(axis, blocks):
    name, size, stride = AXES[axis]
    got = []
    for block, distance in zip(blocks, STEPS):
        route = []
        for i in range(size):
            place = (i // stride) % 4
            route.append((i, i + ((place + distance) % 4 - place) * stride))
        got.append(lax.ppermute(block, name, route))
    return got


def swap_core(block):
    return lax.ppermute(block, "fsdp", [(i, i ^ 1) for i in range(8)])


def passed(block, distance):
    route = [(i - distance, i) for i in range(16) if 0 <= i - distance < 16]
    return lax.ppermute(block, "tm", route)


def per_device(clip, cotangent, weights):
    shape = clip.shape
    clip = clip.reshape(2, ROWS, C)
    cot = cotangent.reshape(2, ROWS, C)
    count = 32 * ROWS * (C // GROUPS)
    scale = 1.0 / math.sqrt(8 * 32 * ROWS)
    partial = functools.partial
    S = jax.ShapeDtypeStruct
    tm = lax.axis_index("tm")
    fsdp = lax.axis_index("fsdp")
    where = [tm == 0, fsdp & 1, fsdp >> 1, tm >> 2]
    where = jnp.stack([jnp.asarray(v, jnp.int32) for v in where])
    frame = S((ROWS, C), bf16)

    sums, last = call(first_kernel, (S((16, 8, C), f32), frame), (clip,))
    first, second = call(copy_kernel, (frame, frame), (cot,), order=(sums,))
    parts = lax.all_to_all(sums, "tm", 0, 0, tiled=True)
    stats, first, last = call(
        total_kernel,
        (S((2, C), f32), frame, frame),
        (parts,),
        order=(first, last),
        aliases={1: 1, 2: 2},
        passed_out=2,
    )
    near = call(widths_kernel, S((3, 2, PADDED, C), bf16), (cot,), order=(stats,))
    after = call(widths_kernel, S((3, 1, PADDED, C), bf16), (passed(first, -1)[None],))
    before = passed(last, 1)

    rows = 2 * SHARD_PAD + UNIT
    tap_flops = C * C * 2 * ROWS * 2
    pieces = (S((rows, C), f32), S((rows, C), bf16))
    act, keep_up, send_up = call(
        partial(near_kernel, count, scale),
        (S((2, ROWS, C), bf16), *pieces),
        (where, stats, clip, near),
        flops=9 * tap_flops,
        scalars=1,
    )
    mine = call(pack_kernel, S((4, SHARD, C), bf16), (where, weights, *ring("x", [weights] * 3)), scalars=1, order=(act,))
    other = swap_core(mine)
    keep_up, send_up = call(
        partial(upper_kernel, scale),
        pieces,
        (where, act, near, after, keep_up, send_up),
        flops=9 * tap_flops // 2,
        scalars=1,
        order=(mine,),
        aliases={4: 0, 5: 1},
    )
    got_up = swap_core(send_up)
    keep_low, send_low = call(
        partial(lower_kernel, count, scale),
        pieces,
        (where, stats, act, before, near, after),
        [pltpu.VMEM((ROWS, C), bf16)],
        flops=27 * tap_flops // 2,
        scalars=1,
        order=(send_up,),
    )
    got_low = swap_core(send_low)

    block = lambda rows: (S((rows, C), f32),) + (S((rows, C), bf16),) * 3
    held, *out = call(
        split_core_kernel, block(SHARD_PAD), (where, keep_up, got_up, keep_low, got_low), scalars=1
    )
    later = passed(second, -1)[None]
    grad0, sums0, full = call(
        partial(first_grad_kernel, count),
        (S((ROWS, C), f32), S((2, C), f32), S((8 * SHARD, C), bf16)),
        (where, stats, clip, near, after, mine, other),
        flops=27 * tap_flops // 2,
        scalars=1,
        order=(held,),
    )
    later = call(widths_kernel, S((3, 1, PADDED, C), bf16), (later,), order=(sums0,))
    grad1, sums1 = call(
        partial(second_grad_kernel, count),
        (S((ROWS, C), f32), S((2, C), f32)),
        (stats, clip, near, after, later, full),
        flops=27 * tap_flops // 2,
        order=(sums0,),
    )
    rows16 = [pltpu.VMEM((16, C), f32)]
    message = S((QUARTER + 16, C), bf16)
    held, sums, *out = call(
        split_x_kernel,
        (S((QUARTER, C), f32), S((2, C), f32), message, message, message),
        (where, held, *ring("x", out), sums0, sums1),
        rows16,
        scalars=1,
    )
    own, sums = call(split_y_kernel, (message, S((2, C), f32)), (held, sums, *ring("y", out)), rows16)
    own, sums = call(
        reduced_kernel, (S((QUARTER, C), bf16), S((2, C), f32)), (own, sums, *ring("z", [own] * 3))
    )
    grad_input = call(
        partial(final_kernel, count),
        S((2, ROWS, C), bf16),
        (stats, sums, clip, cot, grad0, grad1),
        bytes_accessed=8_000_000,
    )
    grad_weight = call(
        finish_kernel,
        S((SHARD, C), f32),
        (where, own, *ring("y", [own] * 3)),
        [pltpu.VMEM((SHARD_PAD, C), f32)],
        scalars=1,
    )
    return grad_input.reshape(shape), grad_weight


def solution(mesh):
    in_specs = (
        P("fsdp", "tm", None, None, None),
        P("fsdp", "tm", None, None, None),
        P("fsdp", None),
    )
    out_specs = (P("fsdp", "tm", None, None, None), P("fsdp", None))
    return jax.shard_map(
        per_device, mesh=mesh, in_specs=in_specs, out_specs=out_specs, check_vma=False
    )
```

```python
import functools
import math

import jax
import jax.numpy as jnp
from jax import lax
from jax.experimental import pallas as pl
from jax.experimental.pallas import tpu as pltpu
from jax.sharding import PartitionSpec as P

GROUPS = 32
C = 256
H = 16
W = 64
ROWS = H * W
PADDED = ROWS + 2 * W
HALF = C // 2
SHARD = 864
SHARD_PAD = 896
QUARTER = 224
UNIT = 32
VMEM = 20 * 1024 * 1024
epsilon = 1e-06
f32 = jnp.float32
bf16 = jnp.bfloat16


def group_total(rows):
    lane = lax.broadcasted_iota(jnp.int32, rows.shape, 1)
    for s in (1, 2, 4):
        up = pltpu.roll(rows, s, 1)
        down = pltpu.roll(rows, C - s, 1)
        rows = rows + jnp.where((lane & s) != 0, up, down)
    return rows


def center_inverse(stats, count):
    sums = group_total(stats) / count
    center = sums[0:1]
    spread = sums[1:2] - center * center
    return center, lax.rsqrt(spread + epsilon)


def sigmoid(v):
    return 0.5 * jnp.tanh(0.5 * v) + 0.5


def widths(target, cot, slot):
    zero = jnp.zeros((W, C), bf16)
    for kw in range(3):
        target[kw, slot, 0:W] = zero
        target[kw, slot, W + ROWS : PADDED] = zero
    column = lax.broadcasted_iota(jnp.int32, (W, C), 0)

    @pl.loop(0, H)
    def _(h):
        row = cot(pl.multiple_of(h * W, W))
        at = pl.ds(pl.multiple_of(h * W + W, W), W)
        wide = row.astype(f32)
        target[1, slot, at] = row
        target[0, slot, at] = jnp.where(column == W - 1, 0.0, pltpu.roll(wide, W - 1, 0)).astype(bf16)
        target[2, slot, at] = jnp.where(column == 0, 0.0, pltpu.roll(wide, 1, 0)).astype(bf16)


def first_kernel(clip, out, last):
    def step(i, carry):
        a, b = carry
        at = pl.ds(pl.multiple_of((i & 7) * 128, 128), 128)
        v = clip[i >> 3, at].astype(f32).reshape(16, 8, C)
        return a + v.sum(0), b + (v * v).sum(0)

    zero = jnp.zeros((8, C), f32)
    a, b = lax.fori_loop(0, 2 * ROWS // 128, step, (zero, zero))
    a, b = a.sum(0, keepdims=True), b.sum(0, keepdims=True)
    for i in range(16):
        out[i, 0:1] = a
        out[i, 1:2] = b
    last[...] = clip[1]


def copy_kernel(cot, order, first, second):
    first[...] = cot[0]
    second[...] = cot[1]


def widths_kernel(cot, *refs):
    wide = refs[-1]
    for t in range(cot.shape[0]):
        widths(wide, lambda r, t=t: cot[t, pl.ds(r, W)], t)


def total_kernel(parts, held0, held1, out, pass0, pass1):
    total = parts[0]
    for i in range(1, 16):
        total = total + parts[i]
    out[...] = total


def tap_rows(kh):
    return slice((2 - kh) * W, (2 - kh) * W + ROWS)


CONTRACT_ROWS = (((0,), (0,)), ((), ()))
CONTRACT_COLUMNS = (((1,), (1,)), ((), ()))


def tap_product(frames, views, channels):
    total = None
    for frame, view in zip(frames, views):
        part = lax.dot_general(frame[:, channels], view, CONTRACT_ROWS, preferred_element_type=f32)
        total = part if total is None else total + part
    return total


def store_tap(tap, total, first_unit, core, keep, send):
    spare = 2 * SHARD_PAD
    for u in range(total.shape[0] // UNIT):
        unit = tap * (C // UNIT) + first_unit + u
        shard = (unit * 1214) >> 15
        dest = ((shard >> 1) & 1) * SHARD_PAD + (unit - shard * (SHARD // UNIT)) * UNIT
        mine = (shard & 1) == core
        piece = total[u * UNIT : (u + 1) * UNIT]
        keep[pl.ds(pl.multiple_of(jnp.where(mine, dest, spare), UNIT), UNIT)] = piece
        send[pl.ds(pl.multiple_of(jnp.where(mine, spare, dest), UNIT), UNIT)] = piece.astype(bf16)


def clear_tails(keep, send):
    for place in range(2):
        tail = slice(place * SHARD_PAD + SHARD, (place + 1) * SHARD_PAD)
        keep[tail] = jnp.zeros((SHARD_PAD - SHARD, C), f32)
        send[tail] = jnp.zeros((SHARD_PAD - SHARD, C), bf16)
    keep[2 * SHARD_PAD :] = jnp.zeros((UNIT, C), f32)
    send[2 * SHARD_PAD :] = jnp.zeros((UNIT, C), bf16)


def middle_taps(low, high, channels, scale, core, act, near, after, keep, send):
    for tap in range(low, high):
        kh, kw = tap // 3 % 3, tap % 3
        rows = slice((2 - kh) * W, (2 - kh) * W + ROWS)
        total = tap_product((act[0], act[1]), (near[kw, 1, rows], after[kw, 0, rows]), channels)
        store_tap(tap, total * scale, channels.start // UNIT, core, keep, send)


def activate(center, inverse, frame, act, gain=None):
    @pl.loop(0, ROWS // 64)
    def _(i):
        at = pl.ds(pl.multiple_of(i * 64, 64), 64)
        v = (frame(at).astype(f32) - center) * inverse
        v = v * sigmoid(v)
        if gain is not None:
            v = v * gain
        act[at] = v.astype(bf16)


def near_kernel(count, scale, where, stats, clip, near, act, keep, send):
    center, inverse = center_inverse(stats[...], count)
    for t in range(2):
        activate(center, inverse, lambda at, t=t: clip[t, at], act.at[t])

    for kh in range(3):
        rows = tap_rows(kh)
        for kw in range(3):
            total = tap_product((act[0], act[1]), (near[kw, 0, rows], near[kw, 1, rows]), slice(None))
            store_tap(18 + kh * 3 + kw, total * scale, 0, where[1], keep, send)

    clear_tails(keep, send)


def upper_kernel(scale, where, act, near, after, keep_in, send_in, order, keep, send):
    middle_taps(14, 18, slice(0, C), scale, where[1], act, near, after, keep, send)
    middle_taps(13, 14, slice(HALF, C), scale, where[1], act, near, after, keep, send)


def lower_kernel(count, scale, where, stats, act, before, near, after, order, keep, send, act_before):
    core = where[1]
    center, inverse = center_inverse(stats[...], count)
    gain = jnp.where(where[0] == 1, 0.0, 1.0)
    activate(center, inverse, lambda at: before[at], act_before, gain)

    for kh in range(3):
        rows = tap_rows(kh)
        for kw in range(3):
            total = tap_product((act_before, act[0]), (near[kw, 1, rows], after[kw, 0, rows]), slice(None))
            store_tap(kh * 3 + kw, total * scale, 0, core, keep, send)

    middle_taps(9, 13, slice(0, C), scale, core, act, near, after, keep, send)
    middle_taps(13, 14, slice(0, HALF), scale, core, act, near, after, keep, send)
    clear_tails(keep, send)


def pack_kernel(where, own, left, right, far, order, packed):
    x = where[2]
    for block, distance in ((own, 0), (left, 3), (right, 1), (far, 2)):
        packed[(x + distance) % 4] = block[...]


def frame_grad(count, frame, stats, clip, views, weights, grad, sums):
    center, inverse = center_inverse(stats[...], count)
    rows_per = 256

    @pl.loop(0, ROWS // rows_per)
    def _(i):
        start = i * rows_per
        total = jnp.zeros((rows_per, C), f32)
        for tap in range(27):
            kt, kh, kw = tap // 9, tap // 3 % 3, tap % 3
            rows = pl.ds(pl.multiple_of((2 - kh) * W + start, W), rows_per)
            w = weights[tap * C : (tap + 1) * C]
            total += lax.dot_general(
                views[2 - kt](kw, rows), w, CONTRACT_COLUMNS, preferred_element_type=f32
            )
        grad[pl.ds(pl.multiple_of(start, rows_per), rows_per)] = total

    zero = jnp.zeros((8, C), f32)

    def finish(i, carry):
        a, b = carry
        at = pl.ds(pl.multiple_of(i * 64, 64), 64)
        v = (clip[frame, at].astype(f32) - center) * inverse
        s = sigmoid(v)
        g = grad[at] * (s * (1.0 + v * (1.0 - s)))
        grad[at] = g
        return a + g.reshape(8, 8, C).sum(0), b + (g * v).reshape(8, 8, C).sum(0)

    a, b = lax.fori_loop(0, ROWS // 64, finish, (zero, zero))
    sums[0:1] = a.sum(0, keepdims=True)
    sums[1:2] = b.sum(0, keepdims=True)


def first_grad_kernel(count, where, stats, clip, near, after, mine, other, order, grad, sums, full):
    core = where[1]
    for x in range(4):
        full[pl.ds(pl.multiple_of((2 * x + core) * SHARD, UNIT), SHARD)] = mine[x]
        full[pl.ds(pl.multiple_of((2 * x + 1 - core) * SHARD, UNIT), SHARD)] = other[x]
    views = (
        lambda kw, rows: near[kw, 0, rows],
        lambda kw, rows: near[kw, 1, rows],
        lambda kw, rows: after[kw, 0, rows],
    )
    frame_grad(count, 0, stats, clip, views, full, grad, sums)


def second_grad_kernel(count, stats, clip, near, after, later, full, order, grad, sums):
    views = (
        lambda kw, rows: near[kw, 1, rows],
        lambda kw, rows: after[kw, 0, rows],
        lambda kw, rows: later[kw, 0, rows],
    )
    frame_grad(count, 1, stats, clip, views, full, grad, sums)


def final_kernel(count, stats, sums, clip, cot, grad0, grad1, out):
    center, inverse = center_inverse(stats[...], count)
    means = group_total(sums[...]) / count
    total, cross = means[0:1], means[1:2]
    for frame, grad in enumerate((grad0, grad1)):

        @pl.loop(0, ROWS // 64)
        def _(i, frame=frame, grad=grad):
            at = pl.ds(pl.multiple_of(i * 64, 64), 64)
            v = (clip[frame, at].astype(f32) - center) * inverse
            g = cot[frame, at].astype(f32) + inverse * (grad[at] - total - v * cross)
            out[frame, at] = g.astype(bf16)


STEPS = (1, 3, 2)


def split_core_kernel(where, keep_up, got_up, keep_low, got_low, held, *out):
    x_own = where[2]

    def total(x, to):
        at = pl.ds(pl.multiple_of((x & 1) * SHARD_PAD, UNIT), SHARD_PAD)

        @pl.when(x < 2)
        def _():
            to[...] = (keep_low[at] + got_low[at].astype(f32)).astype(to.dtype)

        @pl.when(x >= 2)
        def _():
            to[...] = (keep_up[at] + got_up[at].astype(f32)).astype(to.dtype)

    total(x_own, held)
    for step, to in zip(STEPS, out):
        total((x_own + step) & 3, to)


def ring_add(own, arrived, at):
    return (own[at].astype(f32) + arrived[2][at].astype(f32)) + (arrived[0][at].astype(f32) + arrived[1][at].astype(f32))


def split_x_kernel(where, own, a0, a1, a2, sums0, sums1, held, sums, m0, m1, m2, rows):
    out = (m0, m1, m2)
    y = where[3]

    def total(quarter):
        at = pl.ds(pl.multiple_of((quarter & 3) * QUARTER, UNIT), QUARTER)
        return ring_add(own, (a0, a1, a2), at)

    held[...] = total(y)
    sums[...] = sums0[...] + sums1[...]
    for step, to in zip(STEPS, out):
        to[:QUARTER] = total(y + step).astype(bf16)
        write_sums(sums[...], rows, to)


def write_sums(sums, rows, out):
    rows[...] = jnp.zeros((16, C), f32)
    rest = sums
    for k in range(3):
        term = rest.astype(bf16).astype(f32)
        rest = rest - term
        rows[2 * k : 2 * k + 2] = term
    out[QUARTER:] = rows[...].astype(bf16)


def read_sums(block):
    wide = block[QUARTER:].astype(f32)
    return wide[0:2] + wide[2:4] + wide[4:6]


def ring_sums(own, arrived):
    return (own + read_sums(arrived[2])) + (read_sums(arrived[0]) + read_sums(arrived[1]))


def split_y_kernel(held, sums, a0, a1, a2, out, next_sums, rows):
    out[:QUARTER] = ring_add(held, (a0, a1, a2), slice(0, QUARTER)).astype(bf16)
    next_sums[...] = ring_sums(sums[...], (a0, a1, a2))
    write_sums(next_sums[...], rows, out)


def reduced_kernel(own, sums, a0, a1, a2, out, next_sums):
    out[...] = ring_add(own, (a0, a1, a2), slice(0, QUARTER)).astype(bf16)
    next_sums[...] = ring_sums(sums[...], (a0, a1, a2))


def finish_kernel(where, own, a0, a1, a2, grad_weight):
    y = where[3]
    whole = SHARD - 3 * QUARTER
    for block, distance in ((own, 0), (a0, 3), (a1, 1), (a2, 2)):
        quarter = (y + distance) & 3
        start = pl.multiple_of(quarter * QUARTER, UNIT)
        grad_weight[pl.ds(start, whole)] = block[:whole].astype(f32)

        @pl.when(quarter < 3)
        def _(block=block, start=start):
            grad_weight[pl.ds(start + whole, QUARTER - whole)] = block[whole:].astype(f32)


def call(kernel, out_shape, args, scratch=(), flops=0, bytes_accessed=0, scalars=0, order=(), aliases={}, passed_out=0):
    specs = [pl.BlockSpec(memory_space=pltpu.SMEM)] * scalars
    specs += [pl.BlockSpec(memory_space=pltpu.VMEM)] * (len(args) - scalars)
    specs += [pl.BlockSpec(memory_space=pl.ANY)] * len(order)
    out_specs = jax.tree.map(lambda _: pl.BlockSpec(memory_space=pltpu.VMEM), out_shape)
    if passed_out:
        out_specs = out_specs[:-passed_out] + (pl.BlockSpec(memory_space=pl.ANY),) * passed_out
    return pl.pallas_call(
        kernel,
        out_shape=out_shape,
        in_specs=specs,
        out_specs=out_specs,
        scratch_shapes=list(scratch),
        input_output_aliases=aliases,
        compiler_params=pltpu.CompilerParams(vmem_limit_bytes=VMEM),
        cost_estimate=pl.CostEstimate(flops=flops, bytes_accessed=bytes_accessed, transcendentals=0),
    )(*args, *order)


AXES = {"z": ("tm", 16, 1), "y": ("tm", 16, 4), "x": ("fsdp", 8, 2)}


def ring(axis, blocks):
    name, size, stride = AXES[axis]
    got = []
    for block, distance in zip(blocks, STEPS):
        route = []
        for i in range(size):
            place = (i // stride) % 4
            route.append((i, i + ((place + distance) % 4 - place) * stride))
        got.append(lax.ppermute(block, name, route))
    return got


def swap_core(block):
    return lax.ppermute(block, "fsdp", [(i, i ^ 1) for i in range(8)])


def passed(block, distance):
    route = [(i - distance, i) for i in range(16) if 0 <= i - distance < 16]
    return lax.ppermute(block, "tm", route)


def per_device(clip, cotangent, weights):
    shape = clip.shape
    clip = clip.reshape(2, ROWS, C)
    cot = cotangent.reshape(2, ROWS, C)
    count = 32 * ROWS * (C // GROUPS)
    scale = 1.0 / math.sqrt(8 * 32 * ROWS)
    partial = functools.partial
    S = jax.ShapeDtypeStruct
    tm = lax.axis_index("tm")
    fsdp = lax.axis_index("fsdp")
    where = [tm == 0, fsdp & 1, fsdp >> 1, tm >> 2]
    where = jnp.stack([jnp.asarray(v, jnp.int32) for v in where])
    frame = S((ROWS, C), bf16)

    sums, last = call(first_kernel, (S((16, 2, C), f32), frame), (clip,))
    first, second = call(copy_kernel, (frame, frame), (cot,), order=(sums,))
    parts = lax.all_to_all(sums, "tm", 0, 0, tiled=True)
    stats, first, last = call(
        total_kernel,
        (S((2, C), f32), frame, frame),
        (parts,),
        order=(first, last),
        aliases={1: 1, 2: 2},
        passed_out=2,
    )
    near = call(widths_kernel, S((3, 2, PADDED, C), bf16), (cot,), order=(stats,))
    after = call(widths_kernel, S((3, 1, PADDED, C), bf16), (passed(first, -1)[None],))
    before = passed(last, 1)

    rows = 2 * SHARD_PAD + UNIT
    tap_flops = C * C * 2 * ROWS * 2
    pieces = (S((rows, C), f32), S((rows, C), bf16))
    act, keep_up, send_up = call(
        partial(near_kernel, count, scale),
        (S((2, ROWS, C), bf16), *pieces),
        (where, stats, clip, near),
        flops=9 * tap_flops,
        scalars=1,
    )
    mine = call(pack_kernel, S((4, SHARD, C), bf16), (where, weights, *ring("x", [weights] * 3)), scalars=1, order=(act,))
    other = swap_core(mine)
    keep_up, send_up = call(
        partial(upper_kernel, scale),
        pieces,
        (where, act, near, after, keep_up, send_up),
        flops=9 * tap_flops // 2,
        scalars=1,
        order=(mine,),
        aliases={4: 0, 5: 1},
    )
    got_up = swap_core(send_up)
    keep_low, send_low = call(
        partial(lower_kernel, count, scale),
        pieces,
        (where, stats, act, before, near, after),
        [pltpu.VMEM((ROWS, C), bf16)],
        flops=27 * tap_flops // 2,
        scalars=1,
        order=(send_up,),
    )
    got_low = swap_core(send_low)

    block = lambda rows: (S((rows, C), f32),) + (S((rows, C), bf16),) * 3
    held, *out = call(
        split_core_kernel, block(SHARD_PAD), (where, keep_up, got_up, keep_low, got_low), scalars=1
    )
    later = passed(second, -1)[None]
    grad0, sums0, full = call(
        partial(first_grad_kernel, count),
        (S((ROWS, C), f32), S((2, C), f32), S((8 * SHARD, C), bf16)),
        (where, stats, clip, near, after, mine, other),
        flops=27 * tap_flops // 2,
        scalars=1,
        order=(held,),
    )
    later = call(widths_kernel, S((3, 1, PADDED, C), bf16), (later,), order=(sums0,))
    grad1, sums1 = call(
        partial(second_grad_kernel, count),
        (S((ROWS, C), f32), S((2, C), f32)),
        (stats, clip, near, after, later, full),
        flops=27 * tap_flops // 2,
        order=(sums0,),
    )
    rows16 = [pltpu.VMEM((16, C), f32)]
    message = S((QUARTER + 16, C), bf16)
    held, sums, *out = call(
        split_x_kernel,
        (S((QUARTER, C), f32), S((2, C), f32), message, message, message),
        (where, held, *ring("x", out), sums0, sums1),
        rows16,
        scalars=1,
    )
    own, sums = call(split_y_kernel, (message, S((2, C), f32)), (held, sums, *ring("y", out)), rows16)
    own, sums = call(
        reduced_kernel, (S((QUARTER, C), bf16), S((2, C), f32)), (own, sums, *ring("z", [own] * 3))
    )
    grad_input = call(
        partial(final_kernel, count),
        S((2, ROWS, C), bf16),
        (stats, sums, clip, cot, grad0, grad1),
        bytes_accessed=8_000_000,
    )
    grad_weight = call(
        finish_kernel,
        S((SHARD, C), f32),
        (where, own, *ring("y", [own] * 3)),
        scalars=1,
    )
    return grad_input.reshape(shape), grad_weight


def solution(mesh):
    in_specs = (
        P("fsdp", "tm", None, None, None),
        P("fsdp", "tm", None, None, None),
        P("fsdp", None),
    )
    out_specs = (P("fsdp", "tm", None, None, None), P("fsdp", None))
    return jax.shard_map(
        per_device, mesh=mesh, in_specs=in_specs, out_specs=out_specs, check_vma=False
    )
```

```python
import functools
import math

import jax
import jax.numpy as jnp
from jax import lax
from jax.experimental import pallas as pl
from jax.experimental.pallas import tpu as pltpu
from jax.sharding import PartitionSpec as P

GROUPS = 32
C = 256
H = 16
W = 64
ROWS = H * W
PADDED = ROWS + 2 * W
HALF = C // 2
SHARD = 864
SHARD_PAD = 896
QUARTER = 224
UNIT = 32
VMEM = 20 * 1024 * 1024
epsilon = 1e-06
f32 = jnp.float32
bf16 = jnp.bfloat16


def group_total(rows):
    lane = lax.broadcasted_iota(jnp.int32, rows.shape, 1)
    for s in (1, 2, 4):
        up = pltpu.roll(rows, s, 1)
        down = pltpu.roll(rows, C - s, 1)
        rows = rows + jnp.where((lane & s) != 0, up, down)
    return rows


def center_inverse(stats, count):
    sums = group_total(stats) / count
    center = sums[0:1]
    spread = sums[1:2] - center * center
    return center, lax.rsqrt(spread + epsilon)


def sigmoid(v):
    return 0.5 * jnp.tanh(0.5 * v) + 0.5


def widths(target, cot, slot):
    zero = jnp.zeros((W, C), bf16)
    for kw in range(3):
        target[kw, slot, 0:W] = zero
        target[kw, slot, W + ROWS : PADDED] = zero
    column = lax.broadcasted_iota(jnp.int32, (W, C), 0)

    @pl.loop(0, H)
    def _(h):
        row = cot(pl.multiple_of(h * W, W))
        at = pl.ds(pl.multiple_of(h * W + W, W), W)
        wide = row.astype(f32)
        target[1, slot, at] = row
        target[0, slot, at] = jnp.where(column == W - 1, 0.0, pltpu.roll(wide, W - 1, 0)).astype(bf16)
        target[2, slot, at] = jnp.where(column == 0, 0.0, pltpu.roll(wide, 1, 0)).astype(bf16)


def first_kernel(clip, out, last):
    def step(i, carry):
        a, b = carry
        at = pl.ds(pl.multiple_of((i & 7) * 128, 128), 128)
        v = clip[i >> 3, at].astype(f32).reshape(16, 8, C)
        return a + v.sum(0), b + (v * v).sum(0)

    zero = jnp.zeros((8, C), f32)
    a, b = lax.fori_loop(0, 2 * ROWS // 128, step, (zero, zero))
    a, b = a.sum(0, keepdims=True), b.sum(0, keepdims=True)
    for i in range(4):
        out[i, 0:1] = a
        out[i, 1:2] = b
    last[...] = clip[1]


def copy_kernel(cot, order, first, second):
    first[...] = cot[0]
    second[...] = cot[1]


def widths_kernel(cot, *refs):
    wide = refs[-1]
    for t in range(cot.shape[0]):
        widths(wide, lambda r, t=t: cot[t, pl.ds(r, W)], t)


def total_kernel(parts, held0, held1, out, pass0, pass1):
    out[...] = (parts[0] + parts[1]) + (parts[2] + parts[3])


def spread_total_kernel(parts, out):
    total = (parts[0] + parts[1]) + (parts[2] + parts[3])
    for i in range(4):
        out[i] = total


def tap_rows(kh):
    return slice((2 - kh) * W, (2 - kh) * W + ROWS)


CONTRACT_ROWS = (((0,), (0,)), ((), ()))
CONTRACT_COLUMNS = (((1,), (1,)), ((), ()))


def tap_product(frames, views, channels):
    total = None
    for frame, view in zip(frames, views):
        part = lax.dot_general(frame[:, channels], view, CONTRACT_ROWS, preferred_element_type=f32)
        total = part if total is None else total + part
    return total


def store_tap(tap, total, first_unit, core, keep, send):
    spare = 2 * SHARD_PAD
    for u in range(total.shape[0] // UNIT):
        unit = tap * (C // UNIT) + first_unit + u
        shard = (unit * 1214) >> 15
        dest = ((shard >> 1) & 1) * SHARD_PAD + (unit - shard * (SHARD // UNIT)) * UNIT
        mine = (shard & 1) == core
        piece = total[u * UNIT : (u + 1) * UNIT]
        keep[pl.ds(pl.multiple_of(jnp.where(mine, dest, spare), UNIT), UNIT)] = piece
        send[pl.ds(pl.multiple_of(jnp.where(mine, spare, dest), UNIT), UNIT)] = piece.astype(bf16)


def clear_tails(keep, send):
    for place in range(2):
        tail = slice(place * SHARD_PAD + SHARD, (place + 1) * SHARD_PAD)
        keep[tail] = jnp.zeros((SHARD_PAD - SHARD, C), f32)
        send[tail] = jnp.zeros((SHARD_PAD - SHARD, C), bf16)
    keep[2 * SHARD_PAD :] = jnp.zeros((UNIT, C), f32)
    send[2 * SHARD_PAD :] = jnp.zeros((UNIT, C), bf16)


def middle_taps(low, high, channels, scale, core, act, near, after, keep, send):
    for tap in range(low, high):
        kh, kw = tap // 3 % 3, tap % 3
        rows = slice((2 - kh) * W, (2 - kh) * W + ROWS)
        total = tap_product((act[0], act[1]), (near[kw, 1, rows], after[kw, 0, rows]), channels)
        store_tap(tap, total * scale, channels.start // UNIT, core, keep, send)


def activate(center, inverse, frame, act, gain=None):
    @pl.loop(0, ROWS // 64)
    def _(i):
        at = pl.ds(pl.multiple_of(i * 64, 64), 64)
        v = (frame(at).astype(f32) - center) * inverse
        v = v * sigmoid(v)
        if gain is not None:
            v = v * gain
        act[at] = v.astype(bf16)


def near_kernel(count, scale, where, stats, clip, near, act, keep, send):
    center, inverse = center_inverse(stats[...], count)
    for t in range(2):
        activate(center, inverse, lambda at, t=t: clip[t, at], act.at[t])

    for kh in range(3):
        rows = tap_rows(kh)
        for kw in range(3):
            total = tap_product((act[0], act[1]), (near[kw, 0, rows], near[kw, 1, rows]), slice(None))
            store_tap(18 + kh * 3 + kw, total * scale, 0, where[1], keep, send)

    clear_tails(keep, send)


def upper_kernel(scale, where, act, near, after, keep_in, send_in, order, keep, send):
    middle_taps(14, 18, slice(0, C), scale, where[1], act, near, after, keep, send)
    middle_taps(13, 14, slice(HALF, C), scale, where[1], act, near, after, keep, send)


def lower_kernel(count, scale, where, stats, act, before, near, after, order, keep, send, act_before):
    core = where[1]
    center, inverse = center_inverse(stats[...], count)
    gain = jnp.where(where[0] == 1, 0.0, 1.0)
    activate(center, inverse, lambda at: before[at], act_before, gain)

    for kh in range(3):
        rows = tap_rows(kh)
        for kw in range(3):
            total = tap_product((act_before, act[0]), (near[kw, 1, rows], after[kw, 0, rows]), slice(None))
            store_tap(kh * 3 + kw, total * scale, 0, core, keep, send)

    middle_taps(9, 13, slice(0, C), scale, core, act, near, after, keep, send)
    middle_taps(13, 14, slice(0, HALF), scale, core, act, near, after, keep, send)
    clear_tails(keep, send)


def pack_kernel(where, own, left, right, far, order, packed):
    x = where[2]
    for block, distance in ((own, 0), (left, 3), (right, 1), (far, 2)):
        packed[(x + distance) % 4] = block[...]


def frame_grad(count, frame, stats, clip, views, weights, grad, sums):
    center, inverse = center_inverse(stats[...], count)
    rows_per = 256

    @pl.loop(0, ROWS // rows_per)
    def _(i):
        start = i * rows_per
        total = jnp.zeros((rows_per, C), f32)
        for tap in range(27):
            kt, kh, kw = tap // 9, tap // 3 % 3, tap % 3
            rows = pl.ds(pl.multiple_of((2 - kh) * W + start, W), rows_per)
            w = weights[tap * C : (tap + 1) * C]
            total += lax.dot_general(
                views[2 - kt](kw, rows), w, CONTRACT_COLUMNS, preferred_element_type=f32
            )
        grad[pl.ds(pl.multiple_of(start, rows_per), rows_per)] = total

    zero = jnp.zeros((8, C), f32)

    def finish(i, carry):
        a, b = carry
        at = pl.ds(pl.multiple_of(i * 64, 64), 64)
        v = (clip[frame, at].astype(f32) - center) * inverse
        s = sigmoid(v)
        g = grad[at] * (s * (1.0 + v * (1.0 - s)))
        grad[at] = g
        return a + g.reshape(8, 8, C).sum(0), b + (g * v).reshape(8, 8, C).sum(0)

    a, b = lax.fori_loop(0, ROWS // 64, finish, (zero, zero))
    sums[0:1] = a.sum(0, keepdims=True)
    sums[1:2] = b.sum(0, keepdims=True)


def first_grad_kernel(count, where, stats, clip, near, after, mine, other, order, grad, sums, full):
    core = where[1]
    for x in range(4):
        full[pl.ds(pl.multiple_of((2 * x + core) * SHARD, UNIT), SHARD)] = mine[x]
        full[pl.ds(pl.multiple_of((2 * x + 1 - core) * SHARD, UNIT), SHARD)] = other[x]
    views = (
        lambda kw, rows: near[kw, 0, rows],
        lambda kw, rows: near[kw, 1, rows],
        lambda kw, rows: after[kw, 0, rows],
    )
    frame_grad(count, 0, stats, clip, views, full, grad, sums)


def second_grad_kernel(count, stats, clip, near, after, later, full, order, grad, sums):
    views = (
        lambda kw, rows: near[kw, 1, rows],
        lambda kw, rows: after[kw, 0, rows],
        lambda kw, rows: later[kw, 0, rows],
    )
    frame_grad(count, 1, stats, clip, views, full, grad, sums)


def final_kernel(count, stats, sums, clip, cot, grad0, grad1, out):
    center, inverse = center_inverse(stats[...], count)
    means = group_total(sums[...]) / count
    total, cross = means[0:1], means[1:2]
    for frame, grad in enumerate((grad0, grad1)):

        @pl.loop(0, ROWS // 64)
        def _(i, frame=frame, grad=grad):
            at = pl.ds(pl.multiple_of(i * 64, 64), 64)
            v = (clip[frame, at].astype(f32) - center) * inverse
            g = cot[frame, at].astype(f32) + inverse * (grad[at] - total - v * cross)
            out[frame, at] = g.astype(bf16)


STEPS = (1, 3, 2)


def split_core_kernel(where, keep_up, got_up, keep_low, got_low, held, *out):
    x_own = where[2]

    def total(x, to):
        at = pl.ds(pl.multiple_of((x & 1) * SHARD_PAD, UNIT), SHARD_PAD)

        @pl.when(x < 2)
        def _():
            to[...] = (keep_low[at] + got_low[at].astype(f32)).astype(to.dtype)

        @pl.when(x >= 2)
        def _():
            to[...] = (keep_up[at] + got_up[at].astype(f32)).astype(to.dtype)

    total(x_own, held)
    for step, to in zip(STEPS, out):
        total((x_own + step) & 3, to)


def ring_add(own, arrived, at):
    return (own[at].astype(f32) + arrived[2][at].astype(f32)) + (arrived[0][at].astype(f32) + arrived[1][at].astype(f32))


def split_x_kernel(where, own, a0, a1, a2, sums0, sums1, held, sums, m0, m1, m2, rows):
    out = (m0, m1, m2)
    y = where[3]

    def total(quarter):
        at = pl.ds(pl.multiple_of((quarter & 3) * QUARTER, UNIT), QUARTER)
        return ring_add(own, (a0, a1, a2), at)

    held[...] = total(y)
    sums[...] = sums0[...] + sums1[...]
    for step, to in zip(STEPS, out):
        to[:QUARTER] = total(y + step).astype(bf16)
        write_sums(sums[...], rows, to)


def write_sums(sums, rows, out):
    rows[...] = jnp.zeros((16, C), f32)
    rest = sums
    for k in range(3):
        term = rest.astype(bf16).astype(f32)
        rest = rest - term
        rows[2 * k : 2 * k + 2] = term
    out[QUARTER:] = rows[...].astype(bf16)


def read_sums(block):
    wide = block[QUARTER:].astype(f32)
    return wide[0:2] + wide[2:4] + wide[4:6]


def ring_sums(own, arrived):
    return (own + read_sums(arrived[2])) + (read_sums(arrived[0]) + read_sums(arrived[1]))


def split_y_kernel(held, sums, a0, a1, a2, out, next_sums, rows):
    out[:QUARTER] = ring_add(held, (a0, a1, a2), slice(0, QUARTER)).astype(bf16)
    next_sums[...] = ring_sums(sums[...], (a0, a1, a2))
    write_sums(next_sums[...], rows, out)


def reduced_kernel(own, sums, a0, a1, a2, out, next_sums):
    out[...] = ring_add(own, (a0, a1, a2), slice(0, QUARTER)).astype(bf16)
    next_sums[...] = ring_sums(sums[...], (a0, a1, a2))


def finish_kernel(where, own, a0, a1, a2, grad_weight):
    y = where[3]
    whole = SHARD - 3 * QUARTER
    for block, distance in ((own, 0), (a0, 3), (a1, 1), (a2, 2)):
        quarter = (y + distance) & 3
        start = pl.multiple_of(quarter * QUARTER, UNIT)
        grad_weight[pl.ds(start, whole)] = block[:whole].astype(f32)

        @pl.when(quarter < 3)
        def _(block=block, start=start):
            grad_weight[pl.ds(start + whole, QUARTER - whole)] = block[whole:].astype(f32)


def call(kernel, out_shape, args, scratch=(), flops=0, bytes_accessed=0, scalars=0, order=(), aliases={}, passed_out=0):
    specs = [pl.BlockSpec(memory_space=pltpu.SMEM)] * scalars
    specs += [pl.BlockSpec(memory_space=pltpu.VMEM)] * (len(args) - scalars)
    specs += [pl.BlockSpec(memory_space=pl.ANY)] * len(order)
    out_specs = jax.tree.map(lambda _: pl.BlockSpec(memory_space=pltpu.VMEM), out_shape)
    if passed_out:
        out_specs = out_specs[:-passed_out] + (pl.BlockSpec(memory_space=pl.ANY),) * passed_out
    return pl.pallas_call(
        kernel,
        out_shape=out_shape,
        in_specs=specs,
        out_specs=out_specs,
        scratch_shapes=list(scratch),
        input_output_aliases=aliases,
        compiler_params=pltpu.CompilerParams(vmem_limit_bytes=VMEM),
        cost_estimate=pl.CostEstimate(flops=flops, bytes_accessed=bytes_accessed, transcendentals=0),
    )(*args, *order)


AXES = {"z": ("tm", 16, 1), "y": ("tm", 16, 4), "x": ("fsdp", 8, 2)}


def ring(axis, blocks):
    name, size, stride = AXES[axis]
    got = []
    for block, distance in zip(blocks, STEPS):
        route = []
        for i in range(size):
            place = (i // stride) % 4
            route.append((i, i + ((place + distance) % 4 - place) * stride))
        got.append(lax.ppermute(block, name, route))
    return got


def swap_core(block):
    return lax.ppermute(block, "fsdp", [(i, i ^ 1) for i in range(8)])


def passed(block, distance):
    route = [(i - distance, i) for i in range(16) if 0 <= i - distance < 16]
    return lax.ppermute(block, "tm", route)


def per_device(clip, cotangent, weights):
    shape = clip.shape
    clip = clip.reshape(2, ROWS, C)
    cot = cotangent.reshape(2, ROWS, C)
    count = 32 * ROWS * (C // GROUPS)
    scale = 1.0 / math.sqrt(8 * 32 * ROWS)
    partial = functools.partial
    S = jax.ShapeDtypeStruct
    tm = lax.axis_index("tm")
    fsdp = lax.axis_index("fsdp")
    where = [tm == 0, fsdp & 1, fsdp >> 1, tm >> 2]
    where = jnp.stack([jnp.asarray(v, jnp.int32) for v in where])
    frame = S((ROWS, C), bf16)

    sums, last = call(first_kernel, (S((4, 2, C), f32), frame), (clip,))
    first, second = call(copy_kernel, (frame, frame), (cot,), order=(sums,))
    rows_of_z = [[4 * y + z for z in range(4)] for y in range(4)]
    rows_of_y = [[4 * y + z for y in range(4)] for z in range(4)]
    parts = lax.all_to_all(sums, "tm", 0, 0, axis_index_groups=rows_of_z, tiled=True)
    parts = call(spread_total_kernel, S((4, 2, C), f32), (parts,))
    parts = lax.all_to_all(parts, "tm", 0, 0, axis_index_groups=rows_of_y, tiled=True)
    stats, first, last = call(
        total_kernel,
        (S((2, C), f32), frame, frame),
        (parts,),
        order=(first, last),
        aliases={1: 1, 2: 2},
        passed_out=2,
    )
    near = call(widths_kernel, S((3, 2, PADDED, C), bf16), (cot,), order=(stats,))
    after = call(widths_kernel, S((3, 1, PADDED, C), bf16), (passed(first, -1)[None],))
    before = passed(last, 1)

    rows = 2 * SHARD_PAD + UNIT
    tap_flops = C * C * 2 * ROWS * 2
    pieces = (S((rows, C), f32), S((rows, C), bf16))
    act, keep_up, send_up = call(
        partial(near_kernel, count, scale),
        (S((2, ROWS, C), bf16), *pieces),
        (where, stats, clip, near),
        flops=9 * tap_flops,
        scalars=1,
    )
    mine = call(pack_kernel, S((4, SHARD, C), bf16), (where, weights, *ring("x", [weights] * 3)), scalars=1, order=(act,))
    other = swap_core(mine)
    keep_up, send_up = call(
        partial(upper_kernel, scale),
        pieces,
        (where, act, near, after, keep_up, send_up),
        flops=9 * tap_flops // 2,
        scalars=1,
        order=(mine,),
        aliases={4: 0, 5: 1},
    )
    got_up = swap_core(send_up)
    keep_low, send_low = call(
        partial(lower_kernel, count, scale),
        pieces,
        (where, stats, act, before, near, after),
        [pltpu.VMEM((ROWS, C), bf16)],
        flops=27 * tap_flops // 2,
        scalars=1,
        order=(send_up,),
    )
    got_low = swap_core(send_low)

    block = lambda rows: (S((rows, C), f32),) + (S((rows, C), bf16),) * 3
    held, *out = call(
        split_core_kernel, block(SHARD_PAD), (where, keep_up, got_up, keep_low, got_low), scalars=1
    )
    later = passed(second, -1)[None]
    grad0, sums0, full = call(
        partial(first_grad_kernel, count),
        (S((ROWS, C), f32), S((2, C), f32), S((8 * SHARD, C), bf16)),
        (where, stats, clip, near, after, mine, other),
        flops=27 * tap_flops // 2,
        scalars=1,
        order=(held,),
    )
    later = call(widths_kernel, S((3, 1, PADDED, C), bf16), (later,), order=(sums0,))
    grad1, sums1 = call(
        partial(second_grad_kernel, count),
        (S((ROWS, C), f32), S((2, C), f32)),
        (stats, clip, near, after, later, full),
        flops=27 * tap_flops // 2,
        order=(sums0,),
    )
    rows16 = [pltpu.VMEM((16, C), f32)]
    message = S((QUARTER + 16, C), bf16)
    held, sums, *out = call(
        split_x_kernel,
        (S((QUARTER, C), f32), S((2, C), f32), message, message, message),
        (where, held, *ring("x", out), sums0, sums1),
        rows16,
        scalars=1,
    )
    own, sums = call(split_y_kernel, (message, S((2, C), f32)), (held, sums, *ring("y", out)), rows16)
    own, sums = call(
        reduced_kernel, (S((QUARTER, C), bf16), S((2, C), f32)), (own, sums, *ring("z", [own] * 3))
    )
    grad_input = call(
        partial(final_kernel, count),
        S((2, ROWS, C), bf16),
        (stats, sums, clip, cot, grad0, grad1),
        bytes_accessed=8_000_000,
    )
    grad_weight = call(
        finish_kernel,
        S((SHARD, C), f32),
        (where, own, *ring("y", [own] * 3)),
        scalars=1,
    )
    return grad_input.reshape(shape), grad_weight


def solution(mesh):
    in_specs = (
        P("fsdp", "tm", None, None, None),
        P("fsdp", "tm", None, None, None),
        P("fsdp", None),
    )
    out_specs = (P("fsdp", "tm", None, None, None), P("fsdp", None))
    return jax.shard_map(
        per_device, mesh=mesh, in_specs=in_specs, out_specs=out_specs, check_vma=False
    )
```

```python
import functools
import math

import jax
import jax.numpy as jnp
from jax import lax
from jax.experimental import pallas as pl
from jax.experimental.pallas import tpu as pltpu
from jax.sharding import PartitionSpec as P

GROUPS = 32
C = 256
H = 16
W = 64
ROWS = H * W
PADDED = ROWS + 2 * W
HALF = C // 2
SHARD = 864
SHARD_PAD = 896
QUARTER = 224
UNIT = 32
VMEM = 20 * 1024 * 1024
epsilon = 1e-06
f32 = jnp.float32
bf16 = jnp.bfloat16


def group_total(rows):
    lane = lax.broadcasted_iota(jnp.int32, rows.shape, 1)
    for s in (1, 2, 4):
        up = pltpu.roll(rows, s, 1)
        down = pltpu.roll(rows, C - s, 1)
        rows = rows + jnp.where((lane & s) != 0, up, down)
    return rows


def center_inverse(stats, count):
    sums = group_total(stats) / count
    center = sums[0:1]
    spread = sums[1:2] - center * center
    return center, lax.rsqrt(spread + epsilon)


def sigmoid(v):
    return 0.5 * jnp.tanh(0.5 * v) + 0.5


def widths(target, cot, slot):
    zero = jnp.zeros((W, C), bf16)
    for kw in range(3):
        target[kw, slot, 0:W] = zero
        target[kw, slot, W + ROWS : PADDED] = zero
    column = lax.broadcasted_iota(jnp.int32, (W, C), 0)

    @pl.loop(0, H)
    def _(h):
        row = cot(pl.multiple_of(h * W, W))
        at = pl.ds(pl.multiple_of(h * W + W, W), W)
        wide = row.astype(f32)
        target[1, slot, at] = row
        target[0, slot, at] = jnp.where(column == W - 1, 0.0, pltpu.roll(wide, W - 1, 0)).astype(bf16)
        target[2, slot, at] = jnp.where(column == 0, 0.0, pltpu.roll(wide, 1, 0)).astype(bf16)


def first_kernel(clip, out, last):
    def step(i, carry):
        a, b = carry
        at = pl.ds(pl.multiple_of((i & 7) * 128, 128), 128)
        v = clip[i >> 3, at].astype(f32).reshape(16, 8, C)
        return a + v.sum(0), b + (v * v).sum(0)

    zero = jnp.zeros((8, C), f32)
    a, b = lax.fori_loop(0, 2 * ROWS // 128, step, (zero, zero))
    a, b = a.sum(0, keepdims=True), b.sum(0, keepdims=True)
    for i in range(16):
        out[i, 0:1] = a
        out[i, 1:2] = b
    last[...] = clip[1]


def copy_kernel(cot, order, first, second):
    first[...] = cot[0]
    second[...] = cot[1]


def widths_kernel(cot, *refs):
    wide = refs[-1]
    for t in range(cot.shape[0]):
        widths(wide, lambda r, t=t: cot[t, pl.ds(r, W)], t)


def total_kernel(parts, held, out, passed_on):
    total = parts[0]
    for i in range(1, 16):
        total = total + parts[i]
    out[...] = total


def tap_rows(kh):
    return slice((2 - kh) * W, (2 - kh) * W + ROWS)


CONTRACT_ROWS = (((0,), (0,)), ((), ()))
CONTRACT_COLUMNS = (((1,), (1,)), ((), ()))


def tap_product(frames, views, channels):
    total = None
    for frame, view in zip(frames, views):
        part = lax.dot_general(frame[:, channels], view, CONTRACT_ROWS, preferred_element_type=f32)
        total = part if total is None else total + part
    return total


def store_tap(tap, total, first_unit, core, keep, send):
    spare = 2 * SHARD_PAD
    for u in range(total.shape[0] // UNIT):
        unit = tap * (C // UNIT) + first_unit + u
        shard = (unit * 1214) >> 15
        dest = ((shard >> 1) & 1) * SHARD_PAD + (unit - shard * (SHARD // UNIT)) * UNIT
        mine = (shard & 1) == core
        piece = total[u * UNIT : (u + 1) * UNIT]
        keep[pl.ds(pl.multiple_of(jnp.where(mine, dest, spare), UNIT), UNIT)] = piece
        send[pl.ds(pl.multiple_of(jnp.where(mine, spare, dest), UNIT), UNIT)] = piece.astype(bf16)


def clear_tails(keep, send):
    for place in range(2):
        tail = slice(place * SHARD_PAD + SHARD, (place + 1) * SHARD_PAD)
        keep[tail] = jnp.zeros((SHARD_PAD - SHARD, C), f32)
        send[tail] = jnp.zeros((SHARD_PAD - SHARD, C), bf16)
    keep[2 * SHARD_PAD :] = jnp.zeros((UNIT, C), f32)
    send[2 * SHARD_PAD :] = jnp.zeros((UNIT, C), bf16)


def middle_taps(low, high, channels, scale, core, act, near, after, keep, send):
    for tap in range(low, high):
        kh, kw = tap // 3 % 3, tap % 3
        rows = slice((2 - kh) * W, (2 - kh) * W + ROWS)
        total = tap_product((act[0], act[1]), (near[kw, 1, rows], after[kw, 0, rows]), channels)
        store_tap(tap, total * scale, channels.start // UNIT, core, keep, send)


def activate(center, inverse, frame, act, gain=None):
    @pl.loop(0, ROWS // 64)
    def _(i):
        at = pl.ds(pl.multiple_of(i * 64, 64), 64)
        v = (frame(at).astype(f32) - center) * inverse
        v = v * sigmoid(v)
        if gain is not None:
            v = v * gain
        act[at] = v.astype(bf16)


def near_kernel(count, scale, where, stats, clip, near, act, keep, send):
    center, inverse = center_inverse(stats[...], count)
    for t in range(2):
        activate(center, inverse, lambda at, t=t: clip[t, at], act.at[t])

    for kh in range(3):
        rows = tap_rows(kh)
        for kw in range(3):
            total = tap_product((act[0], act[1]), (near[kw, 0, rows], near[kw, 1, rows]), slice(None))
            store_tap(18 + kh * 3 + kw, total * scale, 0, where[1], keep, send)

    clear_tails(keep, send)


def upper_kernel(scale, where, act, near, after, keep_in, send_in, order, keep, send):
    middle_taps(14, 18, slice(0, C), scale, where[1], act, near, after, keep, send)
    middle_taps(13, 14, slice(HALF, C), scale, where[1], act, near, after, keep, send)


def lower_kernel(count, scale, where, stats, act, before, near, after, order, keep, send, act_before):
    core = where[1]
    center, inverse = center_inverse(stats[...], count)
    gain = jnp.where(where[0] == 1, 0.0, 1.0)
    activate(center, inverse, lambda at: before[at], act_before, gain)

    for kh in range(3):
        rows = tap_rows(kh)
        for kw in range(3):
            total = tap_product((act_before, act[0]), (near[kw, 1, rows], after[kw, 0, rows]), slice(None))
            store_tap(kh * 3 + kw, total * scale, 0, core, keep, send)

    middle_taps(9, 13, slice(0, C), scale, core, act, near, after, keep, send)
    middle_taps(13, 14, slice(0, HALF), scale, core, act, near, after, keep, send)
    clear_tails(keep, send)


def pack_kernel(where, own, left, right, far, order, packed):
    x = where[2]
    for block, distance in ((own, 0), (left, 3), (right, 1), (far, 2)):
        packed[(x + distance) % 4] = block[...]


def frame_grad(count, frame, stats, clip, views, weights, grad, sums):
    center, inverse = center_inverse(stats[...], count)
    rows_per = 256

    @pl.loop(0, ROWS // rows_per)
    def _(i):
        start = i * rows_per
        total = jnp.zeros((rows_per, C), f32)
        for tap in range(27):
            kt, kh, kw = tap // 9, tap // 3 % 3, tap % 3
            rows = pl.ds(pl.multiple_of((2 - kh) * W + start, W), rows_per)
            w = weights[tap * C : (tap + 1) * C]
            total += lax.dot_general(
                views[2 - kt](kw, rows), w, CONTRACT_COLUMNS, preferred_element_type=f32
            )
        grad[pl.ds(pl.multiple_of(start, rows_per), rows_per)] = total

    zero = jnp.zeros((8, C), f32)

    def finish(i, carry):
        a, b = carry
        at = pl.ds(pl.multiple_of(i * 64, 64), 64)
        v = (clip[frame, at].astype(f32) - center) * inverse
        s = sigmoid(v)
        g = grad[at] * (s * (1.0 + v * (1.0 - s)))
        grad[at] = g
        return a + g.reshape(8, 8, C).sum(0), b + (g * v).reshape(8, 8, C).sum(0)

    a, b = lax.fori_loop(0, ROWS // 64, finish, (zero, zero))
    sums[0:1] = a.sum(0, keepdims=True)
    sums[1:2] = b.sum(0, keepdims=True)


def first_grad_kernel(count, where, stats, clip, near, after, mine, other, order, grad, sums, full):
    core = where[1]
    for x in range(4):
        full[pl.ds(pl.multiple_of((2 * x + core) * SHARD, UNIT), SHARD)] = mine[x]
        full[pl.ds(pl.multiple_of((2 * x + 1 - core) * SHARD, UNIT), SHARD)] = other[x]
    views = (
        lambda kw, rows: near[kw, 0, rows],
        lambda kw, rows: near[kw, 1, rows],
        lambda kw, rows: after[kw, 0, rows],
    )
    frame_grad(count, 0, stats, clip, views, full, grad, sums)


def second_grad_kernel(count, stats, clip, near, after, later, full, order, grad, sums):
    views = (
        lambda kw, rows: near[kw, 1, rows],
        lambda kw, rows: after[kw, 0, rows],
        lambda kw, rows: later[kw, 0, rows],
    )
    frame_grad(count, 1, stats, clip, views, full, grad, sums)


def final_kernel(count, stats, sums, clip, cot, grad0, grad1, out):
    center, inverse = center_inverse(stats[...], count)
    means = group_total(sums[...]) / count
    total, cross = means[0:1], means[1:2]
    for frame, grad in enumerate((grad0, grad1)):

        @pl.loop(0, ROWS // 64)
        def _(i, frame=frame, grad=grad):
            at = pl.ds(pl.multiple_of(i * 64, 64), 64)
            v = (clip[frame, at].astype(f32) - center) * inverse
            g = cot[frame, at].astype(f32) + inverse * (grad[at] - total - v * cross)
            out[frame, at] = g.astype(bf16)


STEPS = (1, 3, 2)


def split_core_kernel(where, keep_up, got_up, keep_low, got_low, held, *out):
    x_own = where[2]

    def total(x, to):
        at = pl.ds(pl.multiple_of((x & 1) * SHARD_PAD, UNIT), SHARD_PAD)

        @pl.when(x < 2)
        def _():
            to[...] = (keep_low[at] + got_low[at].astype(f32)).astype(to.dtype)

        @pl.when(x >= 2)
        def _():
            to[...] = (keep_up[at] + got_up[at].astype(f32)).astype(to.dtype)

    total(x_own, held)
    for step, to in zip(STEPS, out):
        total((x_own + step) & 3, to)


def ring_add(own, arrived, at):
    return (own[at].astype(f32) + arrived[2][at].astype(f32)) + (arrived[0][at].astype(f32) + arrived[1][at].astype(f32))


def split_x_kernel(where, own, a0, a1, a2, sums0, sums1, held, sums, m0, m1, m2, rows):
    out = (m0, m1, m2)
    y = where[3]

    def total(quarter):
        at = pl.ds(pl.multiple_of((quarter & 3) * QUARTER, UNIT), QUARTER)
        return ring_add(own, (a0, a1, a2), at)

    held[...] = total(y)
    sums[...] = sums0[...] + sums1[...]
    for step, to in zip(STEPS, out):
        to[:QUARTER] = total(y + step).astype(bf16)
        write_sums(sums[...], rows, to)


def write_sums(sums, rows, out):
    rows[...] = jnp.zeros((16, C), f32)
    rest = sums
    for k in range(3):
        term = rest.astype(bf16).astype(f32)
        rest = rest - term
        rows[2 * k : 2 * k + 2] = term
    out[QUARTER:] = rows[...].astype(bf16)


def read_sums(block):
    wide = block[QUARTER:].astype(f32)
    return wide[0:2] + wide[2:4] + wide[4:6]


def ring_sums(own, arrived):
    return (own + read_sums(arrived[2])) + (read_sums(arrived[0]) + read_sums(arrived[1]))


def split_y_kernel(held, sums, a0, a1, a2, out, next_sums, rows):
    out[:QUARTER] = ring_add(held, (a0, a1, a2), slice(0, QUARTER)).astype(bf16)
    next_sums[...] = ring_sums(sums[...], (a0, a1, a2))
    write_sums(next_sums[...], rows, out)


def reduced_kernel(own, sums, a0, a1, a2, out, next_sums):
    out[...] = ring_add(own, (a0, a1, a2), slice(0, QUARTER)).astype(bf16)
    next_sums[...] = ring_sums(sums[...], (a0, a1, a2))


def finish_kernel(where, own, a0, a1, a2, grad_weight):
    y = where[3]
    whole = SHARD - 3 * QUARTER
    for block, distance in ((own, 0), (a0, 3), (a1, 1), (a2, 2)):
        quarter = (y + distance) & 3
        start = pl.multiple_of(quarter * QUARTER, UNIT)
        grad_weight[pl.ds(start, whole)] = block[:whole].astype(f32)

        @pl.when(quarter < 3)
        def _(block=block, start=start):
            grad_weight[pl.ds(start + whole, QUARTER - whole)] = block[whole:].astype(f32)


def call(kernel, out_shape, args, scratch=(), flops=0, bytes_accessed=0, scalars=0, order=(), aliases={}, passed_out=0):
    specs = [pl.BlockSpec(memory_space=pltpu.SMEM)] * scalars
    specs += [pl.BlockSpec(memory_space=pltpu.VMEM)] * (len(args) - scalars)
    specs += [pl.BlockSpec(memory_space=pl.ANY)] * len(order)
    out_specs = jax.tree.map(lambda _: pl.BlockSpec(memory_space=pltpu.VMEM), out_shape)
    if passed_out:
        out_specs = out_specs[:-passed_out] + (pl.BlockSpec(memory_space=pl.ANY),) * passed_out
    return pl.pallas_call(
        kernel,
        out_shape=out_shape,
        in_specs=specs,
        out_specs=out_specs,
        scratch_shapes=list(scratch),
        input_output_aliases=aliases,
        compiler_params=pltpu.CompilerParams(vmem_limit_bytes=VMEM),
        cost_estimate=pl.CostEstimate(flops=flops, bytes_accessed=bytes_accessed, transcendentals=0),
    )(*args, *order)


AXES = {"z": ("tm", 16, 1), "y": ("tm", 16, 4), "x": ("fsdp", 8, 2)}


def ring(axis, blocks):
    name, size, stride = AXES[axis]
    got = []
    for block, distance in zip(blocks, STEPS):
        route = []
        for i in range(size):
            place = (i // stride) % 4
            route.append((i, i + ((place + distance) % 4 - place) * stride))
        got.append(lax.ppermute(block, name, route))
    return got


def swap_core(block):
    return lax.ppermute(block, "fsdp", [(i, i ^ 1) for i in range(8)])


def passed(block, distance):
    route = [(i - distance, i) for i in range(16) if 0 <= i - distance < 16]
    return lax.ppermute(block, "tm", route)


def per_device(clip, cotangent, weights):
    shape = clip.shape
    clip = clip.reshape(2, ROWS, C)
    cot = cotangent.reshape(2, ROWS, C)
    count = 32 * ROWS * (C // GROUPS)
    scale = 1.0 / math.sqrt(8 * 32 * ROWS)
    partial = functools.partial
    S = jax.ShapeDtypeStruct
    tm = lax.axis_index("tm")
    fsdp = lax.axis_index("fsdp")
    where = [tm == 0, fsdp & 1, fsdp >> 1, tm >> 2]
    where = jnp.stack([jnp.asarray(v, jnp.int32) for v in where])
    frame = S((ROWS, C), bf16)

    sums, last = call(first_kernel, (S((16, 2, C), f32), frame), (clip,))
    first, second = call(copy_kernel, (frame, frame), (cot,), order=(sums,))
    parts = lax.all_to_all(sums, "tm", 0, 0, tiled=True)
    stats, last = call(
        total_kernel, (S((2, C), f32), frame), (parts,), order=(last,), aliases={1: 1}, passed_out=1
    )
    near = call(widths_kernel, S((3, 2, PADDED, C), bf16), (cot,), order=(stats,))
    after = call(widths_kernel, S((3, 1, PADDED, C), bf16), (passed(first, -1)[None],))
    before = passed(last, 1)

    rows = 2 * SHARD_PAD + UNIT
    tap_flops = C * C * 2 * ROWS * 2
    pieces = (S((rows, C), f32), S((rows, C), bf16))
    act, keep_up, send_up = call(
        partial(near_kernel, count, scale),
        (S((2, ROWS, C), bf16), *pieces),
        (where, stats, clip, near),
        flops=9 * tap_flops,
        scalars=1,
    )
    mine = call(pack_kernel, S((4, SHARD, C), bf16), (where, weights, *ring("x", [weights] * 3)), scalars=1, order=(act,))
    other = swap_core(mine)
    keep_up, send_up = call(
        partial(upper_kernel, scale),
        pieces,
        (where, act, near, after, keep_up, send_up),
        flops=9 * tap_flops // 2,
        scalars=1,
        order=(mine,),
        aliases={4: 0, 5: 1},
    )
    got_up = swap_core(send_up)
    keep_low, send_low = call(
        partial(lower_kernel, count, scale),
        pieces,
        (where, stats, act, before, near, after),
        [pltpu.VMEM((ROWS, C), bf16)],
        flops=27 * tap_flops // 2,
        scalars=1,
        order=(send_up,),
    )
    got_low = swap_core(send_low)

    block = lambda rows: (S((rows, C), f32),) + (S((rows, C), bf16),) * 3
    held, *out = call(
        split_core_kernel, block(SHARD_PAD), (where, keep_up, got_up, keep_low, got_low), scalars=1
    )
    later = passed(second, -1)[None]
    grad0, sums0, full = call(
        partial(first_grad_kernel, count),
        (S((ROWS, C), f32), S((2, C), f32), S((8 * SHARD, C), bf16)),
        (where, stats, clip, near, after, mine, other),
        flops=27 * tap_flops // 2,
        scalars=1,
        order=(held,),
    )
    later = call(widths_kernel, S((3, 1, PADDED, C), bf16), (later,), order=(sums0,))
    grad1, sums1 = call(
        partial(second_grad_kernel, count),
        (S((ROWS, C), f32), S((2, C), f32)),
        (stats, clip, near, after, later, full),
        flops=27 * tap_flops // 2,
        order=(sums0,),
    )
    rows16 = [pltpu.VMEM((16, C), f32)]
    message = S((QUARTER + 16, C), bf16)
    held, sums, *out = call(
        split_x_kernel,
        (S((QUARTER, C), f32), S((2, C), f32), message, message, message),
        (where, held, *ring("x", out), sums0, sums1),
        rows16,
        scalars=1,
    )
    own, sums = call(split_y_kernel, (message, S((2, C), f32)), (held, sums, *ring("y", out)), rows16)
    own, sums = call(
        reduced_kernel, (S((QUARTER, C), bf16), S((2, C), f32)), (own, sums, *ring("z", [own] * 3))
    )
    grad_input = call(
        partial(final_kernel, count),
        S((2, ROWS, C), bf16),
        (stats, sums, clip, cot, grad0, grad1),
        bytes_accessed=8_000_000,
    )
    grad_weight = call(
        finish_kernel,
        S((SHARD, C), f32),
        (where, own, *ring("y", [own] * 3)),
        scalars=1,
    )
    return grad_input.reshape(shape), grad_weight


def solution(mesh):
    in_specs = (
        P("fsdp", "tm", None, None, None),
        P("fsdp", "tm", None, None, None),
        P("fsdp", None),
    )
    out_specs = (P("fsdp", "tm", None, None, None), P("fsdp", None))
    return jax.shard_map(
        per_device, mesh=mesh, in_specs=in_specs, out_specs=out_specs, check_vma=False
    )
```

```python
import functools
import math

import jax
import jax.numpy as jnp
from jax import lax
from jax.experimental import pallas as pl
from jax.experimental.pallas import tpu as pltpu
from jax.sharding import PartitionSpec as P

GROUPS = 32
C = 256
H = 16
W = 64
ROWS = H * W
PADDED = ROWS + 2 * W
HALF = C // 2
SHARD = 864
SHARD_PAD = 896
QUARTER = 224
UNIT = 32
VMEM = 20 * 1024 * 1024
epsilon = 1e-06
f32 = jnp.float32
bf16 = jnp.bfloat16


def group_total(rows):
    lane = lax.broadcasted_iota(jnp.int32, rows.shape, 1)
    for s in (1, 2, 4):
        up = pltpu.roll(rows, s, 1)
        down = pltpu.roll(rows, C - s, 1)
        rows = rows + jnp.where((lane & s) != 0, up, down)
    return rows


def center_inverse(stats, count):
    sums = group_total(stats) / count
    center = sums[0:1]
    spread = sums[1:2] - center * center
    return center, lax.rsqrt(spread + epsilon)


def sigmoid(v):
    return 0.5 * jnp.tanh(0.5 * v) + 0.5


def widths(target, cot, slot):
    zero = jnp.zeros((W, C), bf16)
    for kw in range(3):
        target[kw, slot, 0:W] = zero
        target[kw, slot, W + ROWS : PADDED] = zero
    column = lax.broadcasted_iota(jnp.int32, (W, C), 0)

    @pl.loop(0, H)
    def _(h):
        row = cot(pl.multiple_of(h * W, W))
        at = pl.ds(pl.multiple_of(h * W + W, W), W)
        wide = row.astype(f32)
        target[1, slot, at] = row
        target[0, slot, at] = jnp.where(column == W - 1, 0.0, pltpu.roll(wide, W - 1, 0)).astype(bf16)
        target[2, slot, at] = jnp.where(column == 0, 0.0, pltpu.roll(wide, 1, 0)).astype(bf16)


def first_kernel(clip, out, last):
    def step(i, carry):
        a, b = carry
        at = pl.ds(pl.multiple_of((i & 7) * 128, 128), 128)
        v = clip[i >> 3, at].astype(f32).reshape(16, 8, C)
        return a + v.sum(0), b + (v * v).sum(0)

    zero = jnp.zeros((8, C), f32)
    a, b = lax.fori_loop(0, 2 * ROWS // 128, step, (zero, zero))
    a, b = a.sum(0, keepdims=True), b.sum(0, keepdims=True)
    for i in range(16):
        out[i, 0:1] = a
        out[i, 1:2] = b
    last[...] = clip[1]


def copy_kernel(cot, order, first):
    first[...] = cot[0]


def second_frame_kernel(cot, order, second):
    second[...] = cot[1]


def widths_kernel(cot, *refs):
    wide = refs[-1]
    for t in range(cot.shape[0]):
        widths(wide, lambda r, t=t: cot[t, pl.ds(r, W)], t)


def total_kernel(parts, held, out, passed_on):
    total = parts[0]
    for i in range(1, 16):
        total = total + parts[i]
    out[...] = total


def tap_rows(kh):
    return slice((2 - kh) * W, (2 - kh) * W + ROWS)


CONTRACT_ROWS = (((0,), (0,)), ((), ()))
CONTRACT_COLUMNS = (((1,), (1,)), ((), ()))


def tap_product(frames, views, channels):
    total = None
    for frame, view in zip(frames, views):
        part = lax.dot_general(frame[:, channels], view, CONTRACT_ROWS, preferred_element_type=f32)
        total = part if total is None else total + part
    return total


def store_tap(tap, total, first_unit, core, keep, send):
    spare = 2 * SHARD_PAD
    for u in range(total.shape[0] // UNIT):
        unit = tap * (C // UNIT) + first_unit + u
        shard = (unit * 1214) >> 15
        dest = ((shard >> 1) & 1) * SHARD_PAD + (unit - shard * (SHARD // UNIT)) * UNIT
        mine = (shard & 1) == core
        piece = total[u * UNIT : (u + 1) * UNIT]
        keep[pl.ds(pl.multiple_of(jnp.where(mine, dest, spare), UNIT), UNIT)] = piece
        send[pl.ds(pl.multiple_of(jnp.where(mine, spare, dest), UNIT), UNIT)] = piece.astype(bf16)


def clear_tails(keep, send):
    for place in range(2):
        tail = slice(place * SHARD_PAD + SHARD, (place + 1) * SHARD_PAD)
        keep[tail] = jnp.zeros((SHARD_PAD - SHARD, C), f32)
        send[tail] = jnp.zeros((SHARD_PAD - SHARD, C), bf16)
    keep[2 * SHARD_PAD :] = jnp.zeros((UNIT, C), f32)
    send[2 * SHARD_PAD :] = jnp.zeros((UNIT, C), bf16)


def middle_taps(low, high, channels, scale, core, act, near, after, keep, send):
    for tap in range(low, high):
        kh, kw = tap // 3 % 3, tap % 3
        rows = slice((2 - kh) * W, (2 - kh) * W + ROWS)
        total = tap_product((act[0], act[1]), (near[kw, 1, rows], after[kw, 0, rows]), channels)
        store_tap(tap, total * scale, channels.start // UNIT, core, keep, send)


def activate(center, inverse, frame, act, gain=None):
    @pl.loop(0, ROWS // 64)
    def _(i):
        at = pl.ds(pl.multiple_of(i * 64, 64), 64)
        v = (frame(at).astype(f32) - center) * inverse
        v = v * sigmoid(v)
        if gain is not None:
            v = v * gain
        act[at] = v.astype(bf16)


def near_kernel(count, scale, where, stats, clip, near, act, keep, send):
    center, inverse = center_inverse(stats[...], count)
    for t in range(2):
        activate(center, inverse, lambda at, t=t: clip[t, at], act.at[t])

    for kh in range(3):
        rows = tap_rows(kh)
        for kw in range(3):
            total = tap_product((act[0], act[1]), (near[kw, 0, rows], near[kw, 1, rows]), slice(None))
            store_tap(18 + kh * 3 + kw, total * scale, 0, where[1], keep, send)

    clear_tails(keep, send)


def upper_kernel(scale, where, act, near, after, keep_in, send_in, order, keep, send):
    middle_taps(14, 18, slice(0, C), scale, where[1], act, near, after, keep, send)
    middle_taps(13, 14, slice(HALF, C), scale, where[1], act, near, after, keep, send)


def lower_kernel(count, scale, where, stats, act, before, near, after, order, keep, send, act_before):
    core = where[1]
    center, inverse = center_inverse(stats[...], count)
    gain = jnp.where(where[0] == 1, 0.0, 1.0)
    activate(center, inverse, lambda at: before[at], act_before, gain)

    for kh in range(3):
        rows = tap_rows(kh)
        for kw in range(3):
            total = tap_product((act_before, act[0]), (near[kw, 1, rows], after[kw, 0, rows]), slice(None))
            store_tap(kh * 3 + kw, total * scale, 0, core, keep, send)

    middle_taps(9, 13, slice(0, C), scale, core, act, near, after, keep, send)
    middle_taps(13, 14, slice(0, HALF), scale, core, act, near, after, keep, send)
    clear_tails(keep, send)


def pack_kernel(where, own, left, right, far, order, packed):
    x = where[2]
    for block, distance in ((own, 0), (left, 3), (right, 1), (far, 2)):
        packed[(x + distance) % 4] = block[...]


def frame_grad(count, frame, stats, clip, views, weights, grad, sums):
    center, inverse = center_inverse(stats[...], count)
    rows_per = 256

    @pl.loop(0, ROWS // rows_per)
    def _(i):
        start = i * rows_per
        total = jnp.zeros((rows_per, C), f32)
        for tap in range(27):
            kt, kh, kw = tap // 9, tap // 3 % 3, tap % 3
            rows = pl.ds(pl.multiple_of((2 - kh) * W + start, W), rows_per)
            w = weights[tap * C : (tap + 1) * C]
            total += lax.dot_general(
                views[2 - kt](kw, rows), w, CONTRACT_COLUMNS, preferred_element_type=f32
            )
        grad[pl.ds(pl.multiple_of(start, rows_per), rows_per)] = total

    zero = jnp.zeros((8, C), f32)

    def finish(i, carry):
        a, b = carry
        at = pl.ds(pl.multiple_of(i * 64, 64), 64)
        v = (clip[frame, at].astype(f32) - center) * inverse
        s = sigmoid(v)
        g = grad[at] * (s * (1.0 + v * (1.0 - s)))
        grad[at] = g
        return a + g.reshape(8, 8, C).sum(0), b + (g * v).reshape(8, 8, C).sum(0)

    a, b = lax.fori_loop(0, ROWS // 64, finish, (zero, zero))
    sums[0:1] = a.sum(0, keepdims=True)
    sums[1:2] = b.sum(0, keepdims=True)


def first_grad_kernel(count, where, stats, clip, near, after, mine, other, order, grad, sums, full):
    core = where[1]
    for x in range(4):
        full[pl.ds(pl.multiple_of((2 * x + core) * SHARD, UNIT), SHARD)] = mine[x]
        full[pl.ds(pl.multiple_of((2 * x + 1 - core) * SHARD, UNIT), SHARD)] = other[x]
    views = (
        lambda kw, rows: near[kw, 0, rows],
        lambda kw, rows: near[kw, 1, rows],
        lambda kw, rows: after[kw, 0, rows],
    )
    frame_grad(count, 0, stats, clip, views, full, grad, sums)


def second_grad_kernel(count, stats, clip, near, after, later, full, order, grad, sums):
    views = (
        lambda kw, rows: near[kw, 1, rows],
        lambda kw, rows: after[kw, 0, rows],
        lambda kw, rows: later[kw, 0, rows],
    )
    frame_grad(count, 1, stats, clip, views, full, grad, sums)


def final_kernel(count, stats, sums, clip, cot, grad0, grad1, out):
    center, inverse = center_inverse(stats[...], count)
    means = group_total(sums[...]) / count
    total, cross = means[0:1], means[1:2]
    for frame, grad in enumerate((grad0, grad1)):

        @pl.loop(0, ROWS // 64)
        def _(i, frame=frame, grad=grad):
            at = pl.ds(pl.multiple_of(i * 64, 64), 64)
            v = (clip[frame, at].astype(f32) - center) * inverse
            g = cot[frame, at].astype(f32) + inverse * (grad[at] - total - v * cross)
            out[frame, at] = g.astype(bf16)


STEPS = (1, 3, 2)


def split_core_kernel(where, keep_up, got_up, keep_low, got_low, held, *out):
    x_own = where[2]

    def total(x, to):
        at = pl.ds(pl.multiple_of((x & 1) * SHARD_PAD, UNIT), SHARD_PAD)

        @pl.when(x < 2)
        def _():
            to[...] = (keep_low[at] + got_low[at].astype(f32)).astype(to.dtype)

        @pl.when(x >= 2)
        def _():
            to[...] = (keep_up[at] + got_up[at].astype(f32)).astype(to.dtype)

    total(x_own, held)
    for step, to in zip(STEPS, out):
        total((x_own + step) & 3, to)


def ring_add(own, arrived, at):
    return (own[at].astype(f32) + arrived[2][at].astype(f32)) + (arrived[0][at].astype(f32) + arrived[1][at].astype(f32))


def split_x_kernel(where, own, a0, a1, a2, sums0, sums1, held, sums, m0, m1, m2, rows):
    out = (m0, m1, m2)
    y = where[3]

    def total(quarter):
        at = pl.ds(pl.multiple_of((quarter & 3) * QUARTER, UNIT), QUARTER)
        return ring_add(own, (a0, a1, a2), at)

    held[...] = total(y)
    sums[...] = sums0[...] + sums1[...]
    for step, to in zip(STEPS, out):
        to[:QUARTER] = total(y + step).astype(bf16)
        write_sums(sums[...], rows, to)


def write_sums(sums, rows, out):
    rows[...] = jnp.zeros((16, C), f32)
    rest = sums
    for k in range(3):
        term = rest.astype(bf16).astype(f32)
        rest = rest - term
        rows[2 * k : 2 * k + 2] = term
    out[QUARTER:] = rows[...].astype(bf16)


def read_sums(block):
    wide = block[QUARTER:].astype(f32)
    return wide[0:2] + wide[2:4] + wide[4:6]


def ring_sums(own, arrived):
    return (own + read_sums(arrived[2])) + (read_sums(arrived[0]) + read_sums(arrived[1]))


def split_y_kernel(held, sums, a0, a1, a2, out, next_sums, rows):
    out[:QUARTER] = ring_add(held, (a0, a1, a2), slice(0, QUARTER)).astype(bf16)
    next_sums[...] = ring_sums(sums[...], (a0, a1, a2))
    write_sums(next_sums[...], rows, out)


def reduced_kernel(own, sums, a0, a1, a2, out, next_sums):
    out[...] = ring_add(own, (a0, a1, a2), slice(0, QUARTER)).astype(bf16)
    next_sums[...] = ring_sums(sums[...], (a0, a1, a2))


def finish_kernel(where, own, a0, a1, a2, grad_weight):
    y = where[3]
    whole = SHARD - 3 * QUARTER
    for block, distance in ((own, 0), (a0, 3), (a1, 1), (a2, 2)):
        quarter = (y + distance) & 3
        start = pl.multiple_of(quarter * QUARTER, UNIT)
        grad_weight[pl.ds(start, whole)] = block[:whole].astype(f32)

        @pl.when(quarter < 3)
        def _(block=block, start=start):
            grad_weight[pl.ds(start + whole, QUARTER - whole)] = block[whole:].astype(f32)


def call(kernel, out_shape, args, scratch=(), flops=0, bytes_accessed=0, scalars=0, order=(), aliases={}, passed_out=0):
    specs = [pl.BlockSpec(memory_space=pltpu.SMEM)] * scalars
    specs += [pl.BlockSpec(memory_space=pltpu.VMEM)] * (len(args) - scalars)
    specs += [pl.BlockSpec(memory_space=pl.ANY)] * len(order)
    out_specs = jax.tree.map(lambda _: pl.BlockSpec(memory_space=pltpu.VMEM), out_shape)
    if passed_out:
        out_specs = out_specs[:-passed_out] + (pl.BlockSpec(memory_space=pl.ANY),) * passed_out
    return pl.pallas_call(
        kernel,
        out_shape=out_shape,
        in_specs=specs,
        out_specs=out_specs,
        scratch_shapes=list(scratch),
        input_output_aliases=aliases,
        compiler_params=pltpu.CompilerParams(vmem_limit_bytes=VMEM),
        cost_estimate=pl.CostEstimate(flops=flops, bytes_accessed=bytes_accessed, transcendentals=0),
    )(*args, *order)


AXES = {"z": ("tm", 16, 1), "y": ("tm", 16, 4), "x": ("fsdp", 8, 2)}


def ring(axis, blocks):
    name, size, stride = AXES[axis]
    got = []
    for block, distance in zip(blocks, STEPS):
        route = []
        for i in range(size):
            place = (i // stride) % 4
            route.append((i, i + ((place + distance) % 4 - place) * stride))
        got.append(lax.ppermute(block, name, route))
    return got


def swap_core(block):
    return lax.ppermute(block, "fsdp", [(i, i ^ 1) for i in range(8)])


def passed(block, distance):
    route = [(i - distance, i) for i in range(16) if 0 <= i - distance < 16]
    return lax.ppermute(block, "tm", route)


def per_device(clip, cotangent, weights):
    shape = clip.shape
    clip = clip.reshape(2, ROWS, C)
    cot = cotangent.reshape(2, ROWS, C)
    count = 32 * ROWS * (C // GROUPS)
    scale = 1.0 / math.sqrt(8 * 32 * ROWS)
    partial = functools.partial
    S = jax.ShapeDtypeStruct
    tm = lax.axis_index("tm")
    fsdp = lax.axis_index("fsdp")
    where = [tm == 0, fsdp & 1, fsdp >> 1, tm >> 2]
    where = jnp.stack([jnp.asarray(v, jnp.int32) for v in where])
    frame = S((ROWS, C), bf16)

    sums, last = call(first_kernel, (S((16, 2, C), f32), frame), (clip,))
    first = call(copy_kernel, frame, (cot,), order=(sums,))
    parts = lax.all_to_all(sums, "tm", 0, 0, tiled=True)
    stats, last = call(
        total_kernel, (S((2, C), f32), frame), (parts,), order=(last,), aliases={1: 1}, passed_out=1
    )
    near = call(widths_kernel, S((3, 2, PADDED, C), bf16), (cot,), order=(stats,))
    after = call(widths_kernel, S((3, 1, PADDED, C), bf16), (passed(first, -1)[None],))
    before = passed(last, 1)

    rows = 2 * SHARD_PAD + UNIT
    tap_flops = C * C * 2 * ROWS * 2
    pieces = (S((rows, C), f32), S((rows, C), bf16))
    act, keep_up, send_up = call(
        partial(near_kernel, count, scale),
        (S((2, ROWS, C), bf16), *pieces),
        (where, stats, clip, near),
        flops=9 * tap_flops,
        scalars=1,
    )
    mine = call(pack_kernel, S((4, SHARD, C), bf16), (where, weights, *ring("x", [weights] * 3)), scalars=1, order=(act,))
    other = swap_core(mine)
    keep_up, send_up = call(
        partial(upper_kernel, scale),
        pieces,
        (where, act, near, after, keep_up, send_up),
        flops=9 * tap_flops // 2,
        scalars=1,
        order=(mine,),
        aliases={4: 0, 5: 1},
    )
    got_up = swap_core(send_up)
    keep_low, send_low = call(
        partial(lower_kernel, count, scale),
        pieces,
        (where, stats, act, before, near, after),
        [pltpu.VMEM((ROWS, C), bf16)],
        flops=27 * tap_flops // 2,
        scalars=1,
        order=(send_up,),
    )
    got_low = swap_core(send_low)

    block = lambda rows: (S((rows, C), f32),) + (S((rows, C), bf16),) * 3
    held, *out = call(
        split_core_kernel, block(SHARD_PAD), (where, keep_up, got_up, keep_low, got_low), scalars=1
    )
    second = call(second_frame_kernel, frame, (cot,), order=(keep_low,))
    later = passed(second, -1)[None]
    grad0, sums0, full = call(
        partial(first_grad_kernel, count),
        (S((ROWS, C), f32), S((2, C), f32), S((8 * SHARD, C), bf16)),
        (where, stats, clip, near, after, mine, other),
        flops=27 * tap_flops // 2,
        scalars=1,
        order=(held,),
    )
    later = call(widths_kernel, S((3, 1, PADDED, C), bf16), (later,), order=(sums0,))
    grad1, sums1 = call(
        partial(second_grad_kernel, count),
        (S((ROWS, C), f32), S((2, C), f32)),
        (stats, clip, near, after, later, full),
        flops=27 * tap_flops // 2,
        order=(sums0,),
    )
    rows16 = [pltpu.VMEM((16, C), f32)]
    message = S((QUARTER + 16, C), bf16)
    held, sums, *out = call(
        split_x_kernel,
        (S((QUARTER, C), f32), S((2, C), f32), message, message, message),
        (where, held, *ring("x", out), sums0, sums1),
        rows16,
        scalars=1,
    )
    own, sums = call(split_y_kernel, (message, S((2, C), f32)), (held, sums, *ring("y", out)), rows16)
    own, sums = call(
        reduced_kernel, (S((QUARTER, C), bf16), S((2, C), f32)), (own, sums, *ring("z", [own] * 3))
    )
    grad_input = call(
        partial(final_kernel, count),
        S((2, ROWS, C), bf16),
        (stats, sums, clip, cot, grad0, grad1),
        bytes_accessed=8_000_000,
    )
    grad_weight = call(
        finish_kernel,
        S((SHARD, C), f32),
        (where, own, *ring("y", [own] * 3)),
        scalars=1,
    )
    return grad_input.reshape(shape), grad_weight


def solution(mesh):
    in_specs = (
        P("fsdp", "tm", None, None, None),
        P("fsdp", "tm", None, None, None),
        P("fsdp", None),
    )
    out_specs = (P("fsdp", "tm", None, None, None), P("fsdp", None))
    return jax.shard_map(
        per_device, mesh=mesh, in_specs=in_specs, out_specs=out_specs, check_vma=False
    )
```

```python
import functools
import math

import jax
import jax.numpy as jnp
from jax import lax
from jax.experimental import pallas as pl
from jax.experimental.pallas import tpu as pltpu
from jax.sharding import PartitionSpec as P

GROUPS = 32
C = 256
H = 16
W = 64
ROWS = H * W
PADDED = ROWS + 2 * W
HALF = C // 2
SHARD = 864
SHARD_PAD = 896
QUARTER = 224
UNIT = 32
VMEM = 20 * 1024 * 1024
epsilon = 1e-06
f32 = jnp.float32
bf16 = jnp.bfloat16


def group_total(rows):
    lane = lax.broadcasted_iota(jnp.int32, rows.shape, 1)
    for s in (1, 2, 4):
        up = pltpu.roll(rows, s, 1)
        down = pltpu.roll(rows, C - s, 1)
        rows = rows + jnp.where((lane & s) != 0, up, down)
    return rows


def center_inverse(stats, count):
    sums = group_total(stats) / count
    center = sums[0:1]
    spread = sums[1:2] - center * center
    return center, lax.rsqrt(spread + epsilon)


def sigmoid(v):
    return 0.5 * jnp.tanh(0.5 * v) + 0.5


def widths(target, cot, slot):
    zero = jnp.zeros((W, C), bf16)
    for kw in range(3):
        target[kw, slot, 0:W] = zero
        target[kw, slot, W + ROWS : PADDED] = zero
    column = lax.broadcasted_iota(jnp.int32, (W, C), 0)

    @pl.loop(0, H)
    def _(h):
        row = cot(pl.multiple_of(h * W, W))
        at = pl.ds(pl.multiple_of(h * W + W, W), W)
        wide = row.astype(f32)
        target[1, slot, at] = row
        target[0, slot, at] = jnp.where(column == W - 1, 0.0, pltpu.roll(wide, W - 1, 0)).astype(bf16)
        target[2, slot, at] = jnp.where(column == 0, 0.0, pltpu.roll(wide, 1, 0)).astype(bf16)


def first_kernel(clip, out, last):
    def step(i, carry):
        a, b = carry
        at = pl.ds(pl.multiple_of((i & 7) * 128, 128), 128)
        v = clip[i >> 3, at].astype(f32).reshape(16, 8, C)
        return a + v.sum(0), b + (v * v).sum(0)

    zero = jnp.zeros((8, C), f32)
    a, b = lax.fori_loop(0, 2 * ROWS // 128, step, (zero, zero))
    a, b = a.sum(0, keepdims=True), b.sum(0, keepdims=True)
    for i in range(16):
        out[i, 0:1] = a
        out[i, 1:2] = b
    last[...] = clip[1]


def copy_kernel(cot, order, first):
    first[...] = cot[0]


def second_frame_kernel(cot, order, second):
    second[...] = cot[1]


def widths_kernel(cot, *refs):
    wide = refs[-1]
    for t in range(cot.shape[0]):
        widths(wide, lambda r, t=t: cot[t, pl.ds(r, W)], t)


def total_kernel(parts, held, out, passed_on):
    total = parts[0]
    for i in range(1, 16):
        total = total + parts[i]
    out[...] = total


def tap_rows(kh):
    return slice((2 - kh) * W, (2 - kh) * W + ROWS)


CONTRACT_ROWS = (((0,), (0,)), ((), ()))
CONTRACT_COLUMNS = (((1,), (1,)), ((), ()))


def tap_product(frames, views, channels):
    total = None
    for frame, view in zip(frames, views):
        part = lax.dot_general(frame[:, channels], view, CONTRACT_ROWS, preferred_element_type=f32)
        total = part if total is None else total + part
    return total


def store_tap(tap, total, first_unit, core, keep, send):
    spare = 2 * SHARD_PAD
    for u in range(total.shape[0] // UNIT):
        unit = tap * (C // UNIT) + first_unit + u
        shard = (unit * 1214) >> 15
        dest = ((shard >> 1) & 1) * SHARD_PAD + (unit - shard * (SHARD // UNIT)) * UNIT
        mine = (shard & 1) == core
        piece = total[u * UNIT : (u + 1) * UNIT]
        keep[pl.ds(pl.multiple_of(jnp.where(mine, dest, spare), UNIT), UNIT)] = piece
        send[pl.ds(pl.multiple_of(jnp.where(mine, spare, dest), UNIT), UNIT)] = piece.astype(bf16)


def clear_tails(keep, send):
    for place in range(2):
        tail = slice(place * SHARD_PAD + SHARD, (place + 1) * SHARD_PAD)
        keep[tail] = jnp.zeros((SHARD_PAD - SHARD, C), f32)
        send[tail] = jnp.zeros((SHARD_PAD - SHARD, C), bf16)
    keep[2 * SHARD_PAD :] = jnp.zeros((UNIT, C), f32)
    send[2 * SHARD_PAD :] = jnp.zeros((UNIT, C), bf16)


def middle_taps(low, high, channels, scale, core, act, near, after, keep, send):
    for tap in range(low, high):
        kh, kw = tap // 3 % 3, tap % 3
        rows = slice((2 - kh) * W, (2 - kh) * W + ROWS)
        total = tap_product((act[0], act[1]), (near[kw, 1, rows], after[kw, 0, rows]), channels)
        store_tap(tap, total * scale, channels.start // UNIT, core, keep, send)


def activate(center, inverse, frame, act, gain=None):
    @pl.loop(0, ROWS // 64)
    def _(i):
        at = pl.ds(pl.multiple_of(i * 64, 64), 64)
        v = (frame(at).astype(f32) - center) * inverse
        v = v * sigmoid(v)
        if gain is not None:
            v = v * gain
        act[at] = v.astype(bf16)


def near_kernel(count, scale, where, stats, clip, near, act, keep, send):
    center, inverse = center_inverse(stats[...], count)
    for t in range(2):
        activate(center, inverse, lambda at, t=t: clip[t, at], act.at[t])

    for kh in range(3):
        rows = tap_rows(kh)
        for kw in range(3):
            total = tap_product((act[0], act[1]), (near[kw, 0, rows], near[kw, 1, rows]), slice(None))
            store_tap(18 + kh * 3 + kw, total * scale, 0, where[1], keep, send)

    clear_tails(keep, send)


def upper_kernel(scale, where, act, near, after, keep_in, send_in, order, keep, send):
    middle_taps(14, 18, slice(0, C), scale, where[1], act, near, after, keep, send)
    middle_taps(13, 14, slice(HALF, C), scale, where[1], act, near, after, keep, send)


def lower_kernel(count, scale, where, stats, act, before, near, after, order, keep, send, act_before):
    core = where[1]
    center, inverse = center_inverse(stats[...], count)
    gain = jnp.where(where[0] == 1, 0.0, 1.0)
    activate(center, inverse, lambda at: before[at], act_before, gain)

    for kh in range(3):
        rows = tap_rows(kh)
        for kw in range(3):
            total = tap_product((act_before, act[0]), (near[kw, 1, rows], after[kw, 0, rows]), slice(None))
            store_tap(kh * 3 + kw, total * scale, 0, core, keep, send)

    middle_taps(9, 13, slice(0, C), scale, core, act, near, after, keep, send)
    middle_taps(13, 14, slice(0, HALF), scale, core, act, near, after, keep, send)
    clear_tails(keep, send)


def pack_kernel(where, own, left, right, far, order, packed):
    x = where[2]
    for block, distance in ((own, 0), (left, 3), (right, 1), (far, 2)):
        packed[(x + distance) % 4] = block[...]


def frame_grad(count, frame, stats, clip, views, weights, grad, sums):
    center, inverse = center_inverse(stats[...], count)
    rows_per = 256

    @pl.loop(0, ROWS // rows_per)
    def _(i):
        start = i * rows_per
        total = jnp.zeros((rows_per, C), f32)
        for tap in range(27):
            kt, kh, kw = tap // 9, tap // 3 % 3, tap % 3
            rows = pl.ds(pl.multiple_of((2 - kh) * W + start, W), rows_per)
            w = weights[tap * C : (tap + 1) * C]
            total += lax.dot_general(
                views[2 - kt](kw, rows), w, CONTRACT_COLUMNS, preferred_element_type=f32
            )
        grad[pl.ds(pl.multiple_of(start, rows_per), rows_per)] = total

    zero = jnp.zeros((8, C), f32)

    def finish(i, carry):
        a, b = carry
        at = pl.ds(pl.multiple_of(i * 64, 64), 64)
        v = (clip[frame, at].astype(f32) - center) * inverse
        s = sigmoid(v)
        g = grad[at] * (s * (1.0 + v * (1.0 - s)))
        grad[at] = g
        return a + g.reshape(8, 8, C).sum(0), b + (g * v).reshape(8, 8, C).sum(0)

    a, b = lax.fori_loop(0, ROWS // 64, finish, (zero, zero))
    sums[0:1] = a.sum(0, keepdims=True)
    sums[1:2] = b.sum(0, keepdims=True)


def first_grad_kernel(count, where, stats, clip, near, after, mine, other, order, grad, sums, full):
    core = where[1]
    for x in range(4):
        full[pl.ds(pl.multiple_of((2 * x + core) * SHARD, UNIT), SHARD)] = mine[x]
        full[pl.ds(pl.multiple_of((2 * x + 1 - core) * SHARD, UNIT), SHARD)] = other[x]
    views = (
        lambda kw, rows: near[kw, 0, rows],
        lambda kw, rows: near[kw, 1, rows],
        lambda kw, rows: after[kw, 0, rows],
    )
    frame_grad(count, 0, stats, clip, views, full, grad, sums)


def second_grad_kernel(count, stats, clip, near, after, later, full, order, grad, sums):
    views = (
        lambda kw, rows: near[kw, 1, rows],
        lambda kw, rows: after[kw, 0, rows],
        lambda kw, rows: later[kw, 0, rows],
    )
    frame_grad(count, 1, stats, clip, views, full, grad, sums)


def final_kernel(count, stats, sums, clip, cot, grad0, grad1, out):
    center, inverse = center_inverse(stats[...], count)
    means = group_total(sums[...]) / count
    total, cross = means[0:1], means[1:2]
    for frame, grad in enumerate((grad0, grad1)):

        @pl.loop(0, ROWS // 64)
        def _(i, frame=frame, grad=grad):
            at = pl.ds(pl.multiple_of(i * 64, 64), 64)
            v = (clip[frame, at].astype(f32) - center) * inverse
            g = cot[frame, at].astype(f32) + inverse * (grad[at] - total - v * cross)
            out[frame, at] = g.astype(bf16)


STEPS = (1, 3, 2)


def split_core_kernel(where, keep_up, got_up, keep_low, got_low, held, *out):
    x_own = where[2]

    def total(x, to):
        at = pl.ds(pl.multiple_of((x & 1) * SHARD_PAD, UNIT), SHARD_PAD)

        @pl.when(x < 2)
        def _():
            to[...] = (keep_low[at] + got_low[at].astype(f32)).astype(to.dtype)

        @pl.when(x >= 2)
        def _():
            to[...] = (keep_up[at] + got_up[at].astype(f32)).astype(to.dtype)

    total(x_own, held)
    for step, to in zip(STEPS, out):
        total((x_own + step) & 3, to)


def ring_add(own, arrived, at):
    return (own[at].astype(f32) + arrived[2][at].astype(f32)) + (arrived[0][at].astype(f32) + arrived[1][at].astype(f32))


def split_x_kernel(where, own, a0, a1, a2, sums0, sums1, held, sums, m0, m1, m2, rows):
    out = (m0, m1, m2)
    y = where[3]

    def total(quarter):
        at = pl.ds(pl.multiple_of((quarter & 3) * QUARTER, UNIT), QUARTER)
        return ring_add(own, (a0, a1, a2), at)

    held[...] = total(y)
    sums[...] = sums0[...] + sums1[...]
    for step, to in zip(STEPS, out):
        to[:QUARTER] = total(y + step).astype(bf16)
        write_sums(sums[...], rows, to)


def write_sums(sums, rows, out):
    rows[...] = jnp.zeros((16, C), f32)
    rest = sums
    for k in range(3):
        term = rest.astype(bf16).astype(f32)
        rest = rest - term
        rows[2 * k : 2 * k + 2] = term
    out[QUARTER:] = rows[...].astype(bf16)


def read_sums(block):
    wide = block[QUARTER:].astype(f32)
    return wide[0:2] + wide[2:4] + wide[4:6]


def ring_sums(own, arrived):
    return (own + read_sums(arrived[2])) + (read_sums(arrived[0]) + read_sums(arrived[1]))


def split_y_kernel(held, sums, a0, a1, a2, out, next_sums, rows):
    out[:QUARTER] = ring_add(held, (a0, a1, a2), slice(0, QUARTER)).astype(bf16)
    next_sums[...] = ring_sums(sums[...], (a0, a1, a2))
    write_sums(next_sums[...], rows, out)


def reduced_kernel(own, sums, a0, a1, a2, out, next_sums):
    out[...] = ring_add(own, (a0, a1, a2), slice(0, QUARTER)).astype(bf16)
    next_sums[...] = ring_sums(sums[...], (a0, a1, a2))


def finish_kernel(where, own, a0, a1, a2, grad_weight, wide, sems):
    y = where[3]
    whole = SHARD - 3 * QUARTER
    for k, (block, distance) in enumerate(((own, 0), (a0, 3), (a1, 1), (a2, 2))):
        quarter = (y + distance) & 3
        wide[k] = block[...].astype(f32)
        start = pl.multiple_of(quarter * QUARTER, UNIT)
        pltpu.make_async_copy(wide.at[k, :whole], grad_weight.at[pl.ds(start, whole)], sems.at[0, k]).start()

        @pl.when(quarter < 3)
        def _(k=k, start=start):
            pltpu.make_async_copy(
                wide.at[k, whole:], grad_weight.at[pl.ds(start + whole, QUARTER - whole)], sems.at[1, k]
            ).start()

    for k, distance in enumerate((0, 3, 1, 2)):
        quarter = (y + distance) & 3
        start = pl.multiple_of(quarter * QUARTER, UNIT)
        pltpu.make_async_copy(wide.at[k, :whole], grad_weight.at[pl.ds(start, whole)], sems.at[0, k]).wait()

        @pl.when(quarter < 3)
        def _(k=k, start=start):
            pltpu.make_async_copy(
                wide.at[k, whole:], grad_weight.at[pl.ds(start + whole, QUARTER - whole)], sems.at[1, k]
            ).wait()


def call(kernel, out_shape, args, scratch=(), flops=0, bytes_accessed=0, scalars=0, order=(), aliases={}, passed_out=0):
    specs = [pl.BlockSpec(memory_space=pltpu.SMEM)] * scalars
    specs += [pl.BlockSpec(memory_space=pltpu.VMEM)] * (len(args) - scalars)
    specs += [pl.BlockSpec(memory_space=pl.ANY)] * len(order)
    out_specs = jax.tree.map(lambda _: pl.BlockSpec(memory_space=pltpu.VMEM), out_shape)
    if passed_out:
        out_specs = out_specs[:-passed_out] + (pl.BlockSpec(memory_space=pl.ANY),) * passed_out
    return pl.pallas_call(
        kernel,
        out_shape=out_shape,
        in_specs=specs,
        out_specs=out_specs,
        scratch_shapes=list(scratch),
        input_output_aliases=aliases,
        compiler_params=pltpu.CompilerParams(vmem_limit_bytes=VMEM),
        cost_estimate=pl.CostEstimate(flops=flops, bytes_accessed=bytes_accessed, transcendentals=0),
    )(*args, *order)


AXES = {"z": ("tm", 16, 1), "y": ("tm", 16, 4), "x": ("fsdp", 8, 2)}


def ring(axis, blocks):
    name, size, stride = AXES[axis]
    got = []
    for block, distance in zip(blocks, STEPS):
        route = []
        for i in range(size):
            place = (i // stride) % 4
            route.append((i, i + ((place + distance) % 4 - place) * stride))
        got.append(lax.ppermute(block, name, route))
    return got


def swap_core(block):
    return lax.ppermute(block, "fsdp", [(i, i ^ 1) for i in range(8)])


def passed(block, distance):
    route = [(i - distance, i) for i in range(16) if 0 <= i - distance < 16]
    return lax.ppermute(block, "tm", route)


def per_device(clip, cotangent, weights):
    shape = clip.shape
    clip = clip.reshape(2, ROWS, C)
    cot = cotangent.reshape(2, ROWS, C)
    count = 32 * ROWS * (C // GROUPS)
    scale = 1.0 / math.sqrt(8 * 32 * ROWS)
    partial = functools.partial
    S = jax.ShapeDtypeStruct
    tm = lax.axis_index("tm")
    fsdp = lax.axis_index("fsdp")
    where = [tm == 0, fsdp & 1, fsdp >> 1, tm >> 2]
    where = jnp.stack([jnp.asarray(v, jnp.int32) for v in where])
    frame = S((ROWS, C), bf16)

    sums, last = call(first_kernel, (S((16, 2, C), f32), frame), (clip,))
    first = call(copy_kernel, frame, (cot,), order=(sums,))
    parts = lax.all_to_all(sums, "tm", 0, 0, tiled=True)
    stats, last = call(
        total_kernel, (S((2, C), f32), frame), (parts,), order=(last,), aliases={1: 1}, passed_out=1
    )
    near = call(widths_kernel, S((3, 2, PADDED, C), bf16), (cot,), order=(stats,))
    after = call(widths_kernel, S((3, 1, PADDED, C), bf16), (passed(first, -1)[None],))
    before = passed(last, 1)

    rows = 2 * SHARD_PAD + UNIT
    tap_flops = C * C * 2 * ROWS * 2
    pieces = (S((rows, C), f32), S((rows, C), bf16))
    act, keep_up, send_up = call(
        partial(near_kernel, count, scale),
        (S((2, ROWS, C), bf16), *pieces),
        (where, stats, clip, near),
        flops=9 * tap_flops,
        scalars=1,
    )
    mine = call(pack_kernel, S((4, SHARD, C), bf16), (where, weights, *ring("x", [weights] * 3)), scalars=1, order=(act,))
    other = swap_core(mine)
    keep_up, send_up = call(
        partial(upper_kernel, scale),
        pieces,
        (where, act, near, after, keep_up, send_up),
        flops=9 * tap_flops // 2,
        scalars=1,
        order=(mine,),
        aliases={4: 0, 5: 1},
    )
    got_up = swap_core(send_up)
    keep_low, send_low = call(
        partial(lower_kernel, count, scale),
        pieces,
        (where, stats, act, before, near, after),
        [pltpu.VMEM((ROWS, C), bf16)],
        flops=27 * tap_flops // 2,
        scalars=1,
        order=(send_up,),
    )
    got_low = swap_core(send_low)

    block = lambda rows: (S((rows, C), f32),) + (S((rows, C), bf16),) * 3
    held, *out = call(
        split_core_kernel, block(SHARD_PAD), (where, keep_up, got_up, keep_low, got_low), scalars=1
    )
    second = call(second_frame_kernel, frame, (cot,), order=(keep_low,))
    later = passed(second, -1)[None]
    grad0, sums0, full = call(
        partial(first_grad_kernel, count),
        (S((ROWS, C), f32), S((2, C), f32), S((8 * SHARD, C), bf16)),
        (where, stats, clip, near, after, mine, other),
        flops=27 * tap_flops // 2,
        scalars=1,
        order=(held,),
    )
    later = call(widths_kernel, S((3, 1, PADDED, C), bf16), (later,), order=(sums0,))
    grad1, sums1 = call(
        partial(second_grad_kernel, count),
        (S((ROWS, C), f32), S((2, C), f32)),
        (stats, clip, near, after, later, full),
        flops=27 * tap_flops // 2,
        order=(sums0,),
    )
    rows16 = [pltpu.VMEM((16, C), f32)]
    message = S((QUARTER + 16, C), bf16)
    held, sums, *out = call(
        split_x_kernel,
        (S((QUARTER, C), f32), S((2, C), f32), message, message, message),
        (where, held, *ring("x", out), sums0, sums1),
        rows16,
        scalars=1,
    )
    own, sums = call(split_y_kernel, (message, S((2, C), f32)), (held, sums, *ring("y", out)), rows16)
    own, sums = call(
        reduced_kernel, (S((QUARTER, C), bf16), S((2, C), f32)), (own, sums, *ring("z", [own] * 3))
    )
    grad_input = call(
        partial(final_kernel, count),
        S((2, ROWS, C), bf16),
        (stats, sums, clip, cot, grad0, grad1),
        bytes_accessed=8_000_000,
    )
    grad_weight = pl.pallas_call(
        finish_kernel,
        out_shape=S((SHARD, C), f32),
        in_specs=[pl.BlockSpec(memory_space=pltpu.SMEM)] + [pl.BlockSpec(memory_space=pltpu.VMEM)] * 4,
        out_specs=pl.BlockSpec(memory_space=pl.ANY),
        scratch_shapes=[pltpu.VMEM((4, QUARTER, C), f32), pltpu.SemaphoreType.DMA((2, 4))],
        compiler_params=pltpu.CompilerParams(vmem_limit_bytes=VMEM),
    )(where, own, *ring("y", [own] * 3))
    return grad_input.reshape(shape), grad_weight


def solution(mesh):
    in_specs = (
        P("fsdp", "tm", None, None, None),
        P("fsdp", "tm", None, None, None),
        P("fsdp", None),
    )
    out_specs = (P("fsdp", "tm", None, None, None), P("fsdp", None))
    return jax.shard_map(
        per_device, mesh=mesh, in_specs=in_specs, out_specs=out_specs, check_vma=False
    )
```

```python
import functools
import math

import jax
import jax.numpy as jnp
from jax import lax
from jax.experimental import pallas as pl
from jax.experimental.pallas import tpu as pltpu
from jax.sharding import PartitionSpec as P

GROUPS = 32
C = 256
H = 16
W = 64
ROWS = H * W
PADDED = ROWS + 2 * W
HALF = C // 2
SHARD = 864
SHARD_PAD = 896
QUARTER = 224
UNIT = 32
VMEM = 20 * 1024 * 1024
epsilon = 1e-06
f32 = jnp.float32
bf16 = jnp.bfloat16


def group_total(rows):
    lane = lax.broadcasted_iota(jnp.int32, rows.shape, 1)
    for s in (1, 2, 4):
        up = pltpu.roll(rows, s, 1)
        down = pltpu.roll(rows, C - s, 1)
        rows = rows + jnp.where((lane & s) != 0, up, down)
    return rows


def center_inverse(stats, count):
    sums = group_total(stats) / count
    center = sums[0:1]
    spread = sums[1:2] - center * center
    return center, lax.rsqrt(spread + epsilon)


def sigmoid(v):
    return 0.5 * jnp.tanh(0.5 * v) + 0.5


def widths(target, cot, slot):
    zero = jnp.zeros((W, C), bf16)
    for kw in range(3):
        target[kw, slot, 0:W] = zero
        target[kw, slot, W + ROWS : PADDED] = zero
    column = lax.broadcasted_iota(jnp.int32, (W, C), 0)

    @pl.loop(0, H)
    def _(h):
        row = cot(pl.multiple_of(h * W, W))
        at = pl.ds(pl.multiple_of(h * W + W, W), W)
        wide = row.astype(f32)
        target[1, slot, at] = row
        target[0, slot, at] = jnp.where(column == W - 1, 0.0, pltpu.roll(wide, W - 1, 0)).astype(bf16)
        target[2, slot, at] = jnp.where(column == 0, 0.0, pltpu.roll(wide, 1, 0)).astype(bf16)


def first_kernel(clip, out, last):
    def step(i, carry):
        a, b = carry
        at = pl.ds(pl.multiple_of((i & 7) * 128, 128), 128)
        v = clip[i >> 3, at].astype(f32).reshape(16, 8, C)
        return a + v.sum(0), b + (v * v).sum(0)

    zero = jnp.zeros((8, C), f32)
    a, b = lax.fori_loop(0, 2 * ROWS // 128, step, (zero, zero))
    a, b = a.sum(0, keepdims=True), b.sum(0, keepdims=True)
    for i in range(16):
        out[i, 0:1] = a
        out[i, 1:2] = b
    last[...] = clip[1]


def copy_kernel(cot, order, first):
    first[...] = cot[0]


def second_frame_kernel(cot, order, second):
    second[...] = cot[1]


def widths_kernel(cot, *refs):
    wide = refs[-1]
    for t in range(cot.shape[0]):
        widths(wide, lambda r, t=t: cot[t, pl.ds(r, W)], t)


def total_kernel(parts, held, out, passed_on):
    total = parts[0]
    for i in range(1, 16):
        total = total + parts[i]
    out[...] = total


def tap_rows(kh):
    return slice((2 - kh) * W, (2 - kh) * W + ROWS)


CONTRACT_ROWS = (((0,), (0,)), ((), ()))
CONTRACT_COLUMNS = (((1,), (1,)), ((), ()))


def tap_product(frames, views, channels):
    total = None
    for frame, view in zip(frames, views):
        part = lax.dot_general(frame[:, channels], view, CONTRACT_ROWS, preferred_element_type=f32)
        total = part if total is None else total + part
    return total


def store_tap(tap, total, first_unit, core, keep, send):
    spare = 2 * SHARD_PAD
    for u in range(total.shape[0] // UNIT):
        unit = tap * (C // UNIT) + first_unit + u
        shard = (unit * 1214) >> 15
        dest = ((shard >> 1) & 1) * SHARD_PAD + (unit - shard * (SHARD // UNIT)) * UNIT
        mine = (shard & 1) == core
        piece = total[u * UNIT : (u + 1) * UNIT]
        keep[pl.ds(pl.multiple_of(jnp.where(mine, dest, spare), UNIT), UNIT)] = piece
        send[pl.ds(pl.multiple_of(jnp.where(mine, spare, dest), UNIT), UNIT)] = piece.astype(bf16)


def clear_tails(keep, send):
    for place in range(2):
        tail = slice(place * SHARD_PAD + SHARD, (place + 1) * SHARD_PAD)
        keep[tail] = jnp.zeros((SHARD_PAD - SHARD, C), f32)
        send[tail] = jnp.zeros((SHARD_PAD - SHARD, C), bf16)
    keep[2 * SHARD_PAD :] = jnp.zeros((UNIT, C), f32)
    send[2 * SHARD_PAD :] = jnp.zeros((UNIT, C), bf16)


def middle_taps(low, high, channels, scale, core, act, near, after, keep, send):
    for tap in range(low, high):
        kh, kw = tap // 3 % 3, tap % 3
        rows = slice((2 - kh) * W, (2 - kh) * W + ROWS)
        total = tap_product((act[0], act[1]), (near[kw, 1, rows], after[kw, 0, rows]), channels)
        store_tap(tap, total * scale, channels.start // UNIT, core, keep, send)


def activate(center, inverse, frame, act, gain=None):
    @pl.loop(0, ROWS // 64)
    def _(i):
        at = pl.ds(pl.multiple_of(i * 64, 64), 64)
        v = (frame(at).astype(f32) - center) * inverse
        v = v * sigmoid(v)
        if gain is not None:
            v = v * gain
        act[at] = v.astype(bf16)


def near_kernel(count, scale, where, stats, clip, near, act, keep, send):
    center, inverse = center_inverse(stats[...], count)
    for t in range(2):
        activate(center, inverse, lambda at, t=t: clip[t, at], act.at[t])

    for kh in range(3):
        rows = tap_rows(kh)
        for kw in range(3):
            total = tap_product((act[0], act[1]), (near[kw, 0, rows], near[kw, 1, rows]), slice(None))
            store_tap(18 + kh * 3 + kw, total * scale, 0, where[1], keep, send)

    clear_tails(keep, send)


def upper_kernel(scale, where, act, near, after, keep_in, send_in, order, keep, send):
    middle_taps(14, 18, slice(0, C), scale, where[1], act, near, after, keep, send)
    middle_taps(13, 14, slice(HALF, C), scale, where[1], act, near, after, keep, send)


def lower_kernel(count, scale, where, stats, act, before, near, after, order, keep, send, act_before):
    core = where[1]
    center, inverse = center_inverse(stats[...], count)
    gain = jnp.where(where[0] == 1, 0.0, 1.0)
    activate(center, inverse, lambda at: before[at], act_before, gain)

    for kh in range(3):
        rows = tap_rows(kh)
        for kw in range(3):
            total = tap_product((act_before, act[0]), (near[kw, 1, rows], after[kw, 0, rows]), slice(None))
            store_tap(kh * 3 + kw, total * scale, 0, core, keep, send)

    middle_taps(9, 13, slice(0, C), scale, core, act, near, after, keep, send)
    middle_taps(13, 14, slice(0, HALF), scale, core, act, near, after, keep, send)
    clear_tails(keep, send)


def pack_kernel(where, own, left, right, far, order, packed):
    x = where[2]
    for block, distance in ((own, 0), (left, 3), (right, 1), (far, 2)):
        packed[(x + distance) % 4] = block[...]


def frame_grad(count, frame, stats, clip, views, weights, grad, sums):
    center, inverse = center_inverse(stats[...], count)
    rows_per = 256

    @pl.loop(0, ROWS // rows_per)
    def _(i):
        start = i * rows_per
        total = jnp.zeros((rows_per, C), f32)
        for tap in range(27):
            kt, kh, kw = tap // 9, tap // 3 % 3, tap % 3
            rows = pl.ds(pl.multiple_of((2 - kh) * W + start, W), rows_per)
            w = weights[tap * C : (tap + 1) * C]
            total += lax.dot_general(
                views[2 - kt](kw, rows), w, CONTRACT_COLUMNS, preferred_element_type=f32
            )
        grad[pl.ds(pl.multiple_of(start, rows_per), rows_per)] = total

    zero = jnp.zeros((8, C), f32)

    def finish(i, carry):
        a, b = carry
        at = pl.ds(pl.multiple_of(i * 64, 64), 64)
        v = (clip[frame, at].astype(f32) - center) * inverse
        s = sigmoid(v)
        g = grad[at] * (s * (1.0 + v * (1.0 - s)))
        grad[at] = g
        return a + g.reshape(8, 8, C).sum(0), b + (g * v).reshape(8, 8, C).sum(0)

    a, b = lax.fori_loop(0, ROWS // 64, finish, (zero, zero))
    sums[0:1] = a.sum(0, keepdims=True)
    sums[1:2] = b.sum(0, keepdims=True)


def first_grad_kernel(count, where, stats, clip, near, after, mine, other, order, grad, sums, full):
    core = where[1]
    for x in range(4):
        full[pl.ds(pl.multiple_of((2 * x + core) * SHARD, UNIT), SHARD)] = mine[x]
        full[pl.ds(pl.multiple_of((2 * x + 1 - core) * SHARD, UNIT), SHARD)] = other[x]
    views = (
        lambda kw, rows: near[kw, 0, rows],
        lambda kw, rows: near[kw, 1, rows],
        lambda kw, rows: after[kw, 0, rows],
    )
    frame_grad(count, 0, stats, clip, views, full, grad, sums)


def second_grad_kernel(count, stats, clip, near, after, later, full, order, grad, sums):
    views = (
        lambda kw, rows: near[kw, 1, rows],
        lambda kw, rows: after[kw, 0, rows],
        lambda kw, rows: later[kw, 0, rows],
    )
    frame_grad(count, 1, stats, clip, views, full, grad, sums)


def final_kernel(count, stats, sums, clip, cot, grad0, grad1, out):
    center, inverse = center_inverse(stats[...], count)
    means = group_total(sums[...]) / count
    total, cross = means[0:1], means[1:2]
    for frame, grad in enumerate((grad0, grad1)):

        @pl.loop(0, ROWS // 64)
        def _(i, frame=frame, grad=grad):
            at = pl.ds(pl.multiple_of(i * 64, 64), 64)
            v = (clip[frame, at].astype(f32) - center) * inverse
            g = cot[frame, at].astype(f32) + inverse * (grad[at] - total - v * cross)
            out[frame, at] = g.astype(bf16)


STEPS = (1, 3, 2)


def split_core_kernel(where, keep_up, got_up, keep_low, got_low, held, *out):
    x_own = where[2]

    def total(x, to):
        at = pl.ds(pl.multiple_of((x & 1) * SHARD_PAD, UNIT), SHARD_PAD)

        @pl.when(x < 2)
        def _():
            to[...] = (keep_low[at] + got_low[at].astype(f32)).astype(to.dtype)

        @pl.when(x >= 2)
        def _():
            to[...] = (keep_up[at] + got_up[at].astype(f32)).astype(to.dtype)

    total(x_own, held)
    for step, to in zip(STEPS, out):
        total((x_own + step) & 3, to)


def ring_add(own, arrived, at):
    return (own[at].astype(f32) + arrived[2][at].astype(f32)) + (arrived[0][at].astype(f32) + arrived[1][at].astype(f32))


def split_x_kernel(where, own, a0, a1, a2, sums0, sums1, held, sums, m0, m1, m2, rows):
    out = (m0, m1, m2)
    y = where[3]

    def total(quarter):
        at = pl.ds(pl.multiple_of((quarter & 3) * QUARTER, UNIT), QUARTER)
        return ring_add(own, (a0, a1, a2), at)

    held[...] = total(y)
    sums[...] = sums0[...] + sums1[...]
    for step, to in zip(STEPS, out):
        to[:QUARTER] = total(y + step).astype(bf16)
        write_sums(sums[...], rows, to)


def write_sums(sums, rows, out):
    rows[...] = jnp.zeros((16, C), f32)
    rest = sums
    for k in range(3):
        term = rest.astype(bf16).astype(f32)
        rest = rest - term
        rows[2 * k : 2 * k + 2] = term
    out[QUARTER:] = rows[...].astype(bf16)


def read_sums(block):
    wide = block[QUARTER:].astype(f32)
    return wide[0:2] + wide[2:4] + wide[4:6]


def ring_sums(own, arrived):
    return (own + read_sums(arrived[2])) + (read_sums(arrived[0]) + read_sums(arrived[1]))


def split_y_kernel(held, sums, a0, a1, a2, out, next_sums, rows):
    out[:QUARTER] = ring_add(held, (a0, a1, a2), slice(0, QUARTER)).astype(bf16)
    next_sums[...] = ring_sums(sums[...], (a0, a1, a2))
    write_sums(next_sums[...], rows, out)


def reduced_kernel(own, sums, a0, a1, a2, out, next_sums):
    out[...] = ring_add(own, (a0, a1, a2), slice(0, QUARTER)).astype(bf16)
    next_sums[...] = ring_sums(sums[...], (a0, a1, a2))


def finish_kernel(where, own, a0, a1, a2, grad_weight):
    y = where[3]
    whole = SHARD - 3 * QUARTER
    for block, distance in ((own, 0), (a0, 3), (a1, 1), (a2, 2)):
        quarter = (y + distance) & 3
        start = pl.multiple_of(quarter * QUARTER, UNIT)
        grad_weight[pl.ds(start, whole)] = block[:whole].astype(f32)

        @pl.when(quarter < 3)
        def _(block=block, start=start):
            grad_weight[pl.ds(start + whole, QUARTER - whole)] = block[whole:].astype(f32)


def call(kernel, out_shape, args, scratch=(), flops=0, bytes_accessed=0, scalars=0, order=(), aliases={}, passed_out=0):
    specs = [pl.BlockSpec(memory_space=pltpu.SMEM)] * scalars
    specs += [pl.BlockSpec(memory_space=pltpu.VMEM)] * (len(args) - scalars)
    specs += [pl.BlockSpec(memory_space=pl.ANY)] * len(order)
    out_specs = jax.tree.map(lambda _: pl.BlockSpec(memory_space=pltpu.VMEM), out_shape)
    if passed_out:
        out_specs = out_specs[:-passed_out] + (pl.BlockSpec(memory_space=pl.ANY),) * passed_out
    return pl.pallas_call(
        kernel,
        out_shape=out_shape,
        in_specs=specs,
        out_specs=out_specs,
        scratch_shapes=list(scratch),
        input_output_aliases=aliases,
        compiler_params=pltpu.CompilerParams(vmem_limit_bytes=VMEM),
        cost_estimate=pl.CostEstimate(flops=flops, bytes_accessed=bytes_accessed, transcendentals=0),
    )(*args, *order)


AXES = {"z": ("tm", 16, 1), "y": ("tm", 16, 4), "x": ("fsdp", 8, 2)}


def ring(axis, blocks):
    name, size, stride = AXES[axis]
    got = []
    for block, distance in zip(blocks, STEPS):
        route = []
        for i in range(size):
            place = (i // stride) % 4
            route.append((i, i + ((place + distance) % 4 - place) * stride))
        got.append(lax.ppermute(block, name, route))
    return got


def swap_core(block):
    return lax.ppermute(block, "fsdp", [(i, i ^ 1) for i in range(8)])


def passed(block, distance):
    route = [(i - distance, i) for i in range(16) if 0 <= i - distance < 16]
    return lax.ppermute(block, "tm", route)


def per_device(clip, cotangent, weights):
    shape = clip.shape
    clip = clip.reshape(2, ROWS, C)
    cot = cotangent.reshape(2, ROWS, C)
    count = 32 * ROWS * (C // GROUPS)
    scale = 1.0 / math.sqrt(8 * 32 * ROWS)
    partial = functools.partial
    S = jax.ShapeDtypeStruct
    tm = lax.axis_index("tm")
    fsdp = lax.axis_index("fsdp")
    where = [tm == 0, fsdp & 1, fsdp >> 1, tm >> 2]
    where = jnp.stack([jnp.asarray(v, jnp.int32) for v in where])
    frame = S((ROWS, C), bf16)

    sums, last = call(first_kernel, (S((16, 2, C), f32), frame), (clip,))
    first = call(copy_kernel, frame, (cot,), order=(sums,))
    parts = lax.all_to_all(sums, "tm", 0, 0, tiled=True)
    stats, last = call(
        total_kernel, (S((2, C), f32), frame), (parts,), order=(last,), aliases={1: 1}, passed_out=1
    )
    near = call(widths_kernel, S((3, 2, PADDED, C), bf16), (cot,), order=(stats,))
    after = call(widths_kernel, S((3, 1, PADDED, C), bf16), (passed(first, -1)[None],))
    before = passed(last, 1)

    rows = 2 * SHARD_PAD + UNIT
    tap_flops = C * C * 2 * ROWS * 2
    pieces = (S((rows, C), f32), S((rows, C), bf16))
    act, keep_up, send_up = call(
        partial(near_kernel, count, scale),
        (S((2, ROWS, C), bf16), *pieces),
        (where, stats, clip, near),
        flops=9 * tap_flops,
        scalars=1,
    )
    mine = call(pack_kernel, S((4, SHARD, C), bf16), (where, weights, *ring("x", [weights] * 3)), scalars=1, order=(act,))
    other = swap_core(mine)
    keep_up, send_up = call(
        partial(upper_kernel, scale),
        pieces,
        (where, act, near, after, keep_up, send_up),
        flops=9 * tap_flops // 2,
        scalars=1,
        order=(act,),
        aliases={4: 0, 5: 1},
    )
    got_up = swap_core(send_up)
    keep_low, send_low = call(
        partial(lower_kernel, count, scale),
        pieces,
        (where, stats, act, before, near, after),
        [pltpu.VMEM((ROWS, C), bf16)],
        flops=27 * tap_flops // 2,
        scalars=1,
        order=(send_up,),
    )
    got_low = swap_core(send_low)

    block = lambda rows: (S((rows, C), f32),) + (S((rows, C), bf16),) * 3
    held, *out = call(
        split_core_kernel, block(SHARD_PAD), (where, keep_up, got_up, keep_low, got_low), scalars=1
    )
    second = call(second_frame_kernel, frame, (cot,), order=(keep_low,))
    later = passed(second, -1)[None]
    grad0, sums0, full = call(
        partial(first_grad_kernel, count),
        (S((ROWS, C), f32), S((2, C), f32), S((8 * SHARD, C), bf16)),
        (where, stats, clip, near, after, mine, other),
        flops=27 * tap_flops // 2,
        scalars=1,
        order=(held,),
    )
    later = call(widths_kernel, S((3, 1, PADDED, C), bf16), (later,), order=(sums0,))
    grad1, sums1 = call(
        partial(second_grad_kernel, count),
        (S((ROWS, C), f32), S((2, C), f32)),
        (stats, clip, near, after, later, full),
        flops=27 * tap_flops // 2,
        order=(sums0,),
    )
    rows16 = [pltpu.VMEM((16, C), f32)]
    message = S((QUARTER + 16, C), bf16)
    held, sums, *out = call(
        split_x_kernel,
        (S((QUARTER, C), f32), S((2, C), f32), message, message, message),
        (where, held, *ring("x", out), sums0, sums1),
        rows16,
        scalars=1,
    )
    own, sums = call(split_y_kernel, (message, S((2, C), f32)), (held, sums, *ring("y", out)), rows16)
    own, sums = call(
        reduced_kernel, (S((QUARTER, C), bf16), S((2, C), f32)), (own, sums, *ring("z", [own] * 3))
    )
    grad_input = call(
        partial(final_kernel, count),
        S((2, ROWS, C), bf16),
        (stats, sums, clip, cot, grad0, grad1),
        bytes_accessed=8_000_000,
    )
    grad_weight = call(
        finish_kernel,
        S((SHARD, C), f32),
        (where, own, *ring("y", [own] * 3)),
        scalars=1,
    )
    return grad_input.reshape(shape), grad_weight


def solution(mesh):
    in_specs = (
        P("fsdp", "tm", None, None, None),
        P("fsdp", "tm", None, None, None),
        P("fsdp", None),
    )
    out_specs = (P("fsdp", "tm", None, None, None), P("fsdp", None))
    return jax.shard_map(
        per_device, mesh=mesh, in_specs=in_specs, out_specs=out_specs, check_vma=False
    )
```
